128 devices in a mesh: img: 16 (over z, y), space: 8 (over x, core).
Axes of the slice: x: 4, y: 4, z: 4, core: 2. Of those that a mesh axis runs over, the one named last changes fastest.
Arguments:
- path: float32 [16, 8, 1024, 1024], P('img', None, 'space'), may hold values from -3 to 3
- tilt: float32 [8, 1024, 1024], P(None, 'space'), may hold values from -4 to 4
Outputs:
- new_path: float32 [16, 8, 1024, 1024], P('img', None, 'space')
The draws below stay inside these ranges and needn't reach their ends.
All inputs are finite; a program needn't handle non-finite values.
Results may differ from the reference program's by a relative error of at most 0.0003.
Values sent between devices are 32-bit elements; how exact they have to be, the bound alone decides.
No kernel may reach another device: no remote copies, remote signals or barrier semaphores. Data moves between devices by JAX's collectives and lax.ppermute only.
A program may use at most 128 MiB of HBM per device.

```python
import math
import jax
import jax.numpy as jnp
from jax import lax

PLANES = 8
COLS = 1024
STEPS = 2
IMAGES = 16
ROWS = 1024


def draw_path(key, part):
    keys = jax.random.split(key, 6)
    shape = (PLANES, ROWS, COLS)
    rows = jnp.arange(ROWS, dtype=jnp.float32) / ROWS
    trend = (1.0 + 2.0 * rows)[None, :, None]
    start = 0.35 * jnp.clip(jax.random.normal(keys[0], shape, jnp.float32), -2.0, 2.0)
    change = 0.15 * jnp.clip(jax.random.normal(keys[1], shape, jnp.float32), -2.0, 2.0) * trend
    row_scale = jnp.exp(jax.random.uniform(keys[2], (1, ROWS, 1), jnp.float32, 0.0, math.log(2.0)))
    col_scale = jnp.exp(jax.random.uniform(keys[3], (1, 1, COLS), jnp.float32, 0.0, math.log(2.0)))
    image_scale = jnp.exp(jax.random.uniform(keys[4], (IMAGES, 1, 1, 1), jnp.float32, math.log(0.002), math.log(0.02)))
    noise = jnp.clip(jax.random.normal(keys[5], (IMAGES,) + shape, jnp.float32), -4.0, 4.0)
    frac = (jnp.arange(IMAGES, dtype=jnp.float32) / (IMAGES - 1))[:, None, None, None]
    return start[None] + frac * change[None] + image_scale * (trend * row_scale * col_scale)[None] * noise


def shard_levels(stream_key, dims, shards, least, top_value):
    def one(axis_at, parts):
        draws = jax.random.uniform(jax.random.fold_in(jax.random.fold_in(stream_key, 6), axis_at), (parts,), jnp.float32, least / len(shards), top_value / len(shards))
        return jnp.repeat(jnp.exp(draws), dims[axis_at] // parts).reshape((-1,) + (1,) * (len(dims) - axis_at - 1))

    factor_of = one(*shards[0])
    for cut in shards[1:]:
        factor_of = factor_of * one(*cut)
    return factor_of


def normal_values(stream_key, extent, scale, bound, pieces=(), held_as=jnp.bfloat16):
    loudness = shard_levels(stream_key, extent, pieces, -0.22, 0.18) if pieces else 1.0
    array = jax.random.normal(stream_key, extent, jnp.float32) * scale * loudness
    return jnp.minimum(jnp.maximum(array, -bound), bound).astype(held_as)


def setup_inputs(seed: int = 0) -> dict:
    streams_of = jax.random.split(jax.random.key(seed), 3)
    path = draw_path(jax.random.fold_in(streams_of[2], 71), 0)
    tilt = normal_values(streams_of[1], (PLANES, ROWS, COLS), 1.0, 4.0, ((1, 8),), jnp.float32)
    return {"path": path, "tilt": tilt}


KAPPA = 1.0
DT = 0.006
EPS = 1e-06

def laplace(ext):
    core = ext[..., 1:-1, :]
    total = ext[..., 2:, :] + ext[..., :-2, :]
    total = total + jnp.roll(core, 1, axis=-1) + jnp.roll(core, -1, axis=-1)
    total = total + jnp.roll(core, 1, axis=-3) + jnp.roll(core, -1, axis=-3)
    return total - 6.0 * core

def wrap_rows(field, width):
    return jnp.concatenate([field[..., -width:, :], field, field[..., :width, :]], axis=-2)

def spacing(dist):
    count = dist.shape[0]
    arc = jnp.cumsum(dist)
    target = jnp.arange(count).astype(dist.dtype) * (arc[count - 1] / (count - 1))
    slots = jnp.arange(count, dtype=jnp.int32)
    inside = (slots[None, :] >= 1) & (slots[None, :] <= count - 2) & (arc[None, :] <= target[:, None])
    lower = lax.optimization_barrier(jnp.sum(inside.astype(jnp.int32), axis=1))
    pick_low = (slots[None, :] == lower[:, None]).astype(dist.dtype)
    pick_high = (slots[None, :] == lower[:, None] + 1).astype(dist.dtype)
    start = lax.optimization_barrier(jnp.sum(pick_low * arc[None, :], axis=1))
    length = lax.optimization_barrier(jnp.sum(pick_high * dist[None, :], axis=1))
    share = (target - start) / length
    return pick_low * (1.0 - share)[:, None] + pick_high * share[:, None]

def reference(path, tilt):
    count = path.shape[0]
    tilt_ext = wrap_rows(tilt, 1)
    phi = path
    for step in range(STEPS):
        current = phi

        def update(index):
            image = current[index]
            before = current[jnp.maximum(index - 1, 0)]
            after = current[jnp.minimum(index + 1, count - 1)]
            ext = wrap_rows(image, 2)
            inner = ext[..., 1:-1, :]
            potential = inner * inner * inner - inner - KAPPA * laplace(ext) - tilt_ext
            force = laplace(potential)
            diff = after - before
            coef = jnp.sum(force * diff) / (jnp.sum(diff * diff) + EPS)
            interior = (index > 0) & (index < count - 1)
            direction = jnp.where(interior, force - coef * diff, force)
            return image + DT * direction
        phi = lax.map(update, jnp.arange(count, dtype=jnp.int32))
    final = phi

    def segment(index):
        gap = final[index] - final[index - 1]
        return jnp.sum(gap * gap)
    squares = lax.map(segment, jnp.arange(1, count, dtype=jnp.int32))
    dist = jnp.concatenate([jnp.zeros((1,), squares.dtype), jnp.sqrt(squares + EPS)])
    weights = spacing(dist)
    flat = final.reshape(count, -1)
    moved = jnp.dot(weights, flat, precision=lax.Precision.HIGHEST, preferred_element_type=jnp.float32)
    return moved.reshape(final.shape)
```

```python
import functools

import jax
import jax.numpy as jnp
from jax import lax
from jax.experimental import pallas as pl
from jax.experimental.pallas import tpu as pltpu
from jax.sharding import PartitionSpec as P

DT = 0.006
EPS = 1e-06
RIM = 4
LANES = 128
GROUP = 16
VMEM_LIMIT = 48 * 1024 * 1024

vmem = pl.BlockSpec(memory_space=pltpu.VMEM)
smem = pl.BlockSpec(memory_space=pltpu.SMEM)


def lane_of(shape):
    return lax.broadcasted_iota(jnp.int32, shape, len(shape) - 1)


def strip_of(before, own, after, planes):
    shape = own(0).shape
    lane = lane_of(shape)
    strip = jnp.zeros(shape, jnp.float32)
    for p in range(planes):
        mid = own(p)
        left = pltpu.roll(jnp.where(lane >= LANES - RIM, before(p), mid), (GROUP * p + RIM) % LANES, 1)
        right = pltpu.roll(jnp.where(lane >= LANES - RIM, mid, after(p)), (GROUP * p + 3 * RIM) % LANES, 1)
        place = lane - GROUP * p
        strip = jnp.where((place >= 0) & (place < 2 * RIM), left, strip)
        strip = jnp.where((place >= 2 * RIM) & (place < 4 * RIM), right, strip)
    return strip


def pack_kernel(own_ref, low_ref, high_ref, out_ref):
    planes, rows, cols = own_ref.shape
    half = rows // 2
    blocks = cols // LANES
    for c in range(blocks):
        cut = slice(c * LANES, (c + 1) * LANES)
        for p in range(planes):
            out_ref[c, p, :RIM] = low_ref[p, -RIM:, cut]
            out_ref[c, p, RIM:] = own_ref[p, : half + RIM, cut]
            out_ref[blocks + c, p, : half + RIM] = own_ref[p, half - RIM :, cut]
            out_ref[blocks + c, p, half + RIM :] = high_ref[p, :RIM, cut]

    def strips(k, carry):
        row = (k // blocks) * blocks
        c = k % blocks
        before = row + (c + blocks - 1) % blocks
        after = row + (c + 1) % blocks
        out_ref[k, planes] = strip_of(
            lambda p: out_ref[before, p], lambda p: out_ref[k, p], lambda p: out_ref[after, p], planes
        )
        return carry

    lax.fori_loop(0, 2 * blocks, strips, 0)


def pack(own, low, high):
    planes, rows, cols = own.shape
    return pl.pallas_call(
        pack_kernel,
        out_shape=jax.ShapeDtypeStruct((2 * cols // LANES, planes + 1, rows // 2 + 2 * RIM, LANES), jnp.float32),
        in_specs=[vmem] * 3,
        out_specs=vmem,
        compiler_params=pltpu.CompilerParams(vmem_limit_bytes=VMEM_LIMIT),
        name="pack",
    )(own, low, high)


def pack_one_kernel(place_ref, own_ref, low_ref, high_ref, out_ref, near):
    planes, rows, cols = own_ref.shape
    half = rows // 2
    blocks = cols // LANES
    place = place_ref[0]
    c = place % blocks
    for at, shift in enumerate((blocks - 1, 0, 1)):
        cut = pl.ds(pl.multiple_of(((c + shift) % blocks) * LANES, LANES), LANES)

        @pl.when(place < blocks)
        def _():
            for p in range(planes):
                near[at, p, :RIM] = low_ref[p, -RIM:, cut]
                near[at, p, RIM:] = own_ref[p, : half + RIM, cut]

        @pl.when(place >= blocks)
        def _():
            for p in range(planes):
                near[at, p, : half + RIM] = own_ref[p, half - RIM :, cut]
                near[at, p, half + RIM :] = high_ref[p, :RIM, cut]

    for p in range(planes):
        out_ref[p] = near[1, p]
    out_ref[planes] = strip_of(lambda p: near[0, p], lambda p: near[1, p], lambda p: near[2, p], planes)


def pack_one(place, own, low, high):
    planes, rows, cols = own.shape
    block = (rows // 2 + 2 * RIM, LANES)
    return pl.pallas_call(
        pack_one_kernel,
        out_shape=jax.ShapeDtypeStruct((planes + 1, *block), jnp.float32),
        in_specs=[smem] + [vmem] * 3,
        out_specs=vmem,
        scratch_shapes=[pltpu.VMEM((3, planes, *block), jnp.float32)],
        compiler_params=pltpu.CompilerParams(vmem_limit_bytes=VMEM_LIMIT),
        name="pack_one",
    )(place, own, low, high)


def rows_sum(x):
    rows = x.shape[0]
    return pltpu.roll(x, 1, 0) + pltpu.roll(x, rows - 1, 0)


def laplace_strip(s):
    total = pltpu.roll(s, GROUP, 1) + pltpu.roll(s, LANES - GROUP, 1)
    total = total + pltpu.roll(s, 1, 1) + pltpu.roll(s, LANES - 1, 1)
    return total + rows_sum(s) - 6.0 * s


def laplace_plane(x, below, above, strip, p):
    lane = lane_of(x.shape)
    left = jnp.where(lane == 0, pltpu.roll(strip, (LANES - GROUP * p - (RIM - 1)) % LANES, 1), pltpu.roll(x, 1, 1))
    right = jnp.where(
        lane == LANES - 1, pltpu.roll(strip, (LANES - 1 - GROUP * p - 3 * RIM) % LANES, 1), pltpu.roll(x, LANES - 1, 1)
    )
    return (below + above) + rows_sum(x) + (left + right) - 6.0 * x


def potential(field, tilt_ref, mu):
    planes = mu.shape[0] - 1
    strip = field(planes)
    mu[planes] = strip * strip * strip - strip - laplace_strip(strip) - tilt_ref[planes]
    for p in range(planes):
        x = field(p)
        lap = laplace_plane(x, field((p - 1) % planes), field((p + 1) % planes), strip, p)
        mu[p] = x * x * x - x - lap - tilt_ref[p]


def force_plane(mu, p):
    planes = mu.shape[0] - 1
    return laplace_plane(mu[p], mu[(p - 1) % planes], mu[(p + 1) % planes], mu[planes], p)


def fold(x):
    total = x[:8]
    for at in range(8, x.shape[0], 8):
        total = total + x[at : at + 8]
    return total


def inner(shape):
    row = lax.broadcasted_iota(jnp.int32, shape, 0)
    return (row >= RIM) & (row < shape[0] - RIM)


def write_sums(acc, out_ref):
    kinds, images = acc.shape[:2]
    row = jnp.zeros((1, LANES), jnp.float32)
    lane = lane_of((images, LANES))
    image = lax.broadcasted_iota(jnp.int32, (images, LANES), 0)
    for q in range(kinds):
        part = jnp.sum(acc[q], axis=1)
        part = jnp.sum(part, axis=1, keepdims=True)
        row = row + jnp.sum(jnp.where(lane == images * q + image, part, 0.0), axis=0, keepdims=True)
    out_ref[...] = row


def first_kernel(phi_ref, tilt_ref, moved_ref, sums_ref, mu, acc):
    images, parts, rows, lanes = phi_ref.shape
    planes = parts - 1
    keep = inner((rows, lanes))

    def body(i, carry):
        after = jnp.minimum(i + 1, images - 1)
        before = jnp.maximum(i - 1, 0)
        potential(lambda p: phi_ref[i, p], tilt_ref, mu)
        moved_ref[i, planes] = phi_ref[i, planes] + DT * laplace_strip(mu[planes])
        product = jnp.zeros((8, lanes), jnp.float32)
        square = jnp.zeros((8, lanes), jnp.float32)
        for p in range(planes):
            force = force_plane(mu, p)
            moved_ref[i, p] = phi_ref[i, p] + DT * force
            diff = jnp.where(keep, phi_ref[after, p] - phi_ref[before, p], 0.0)
            product = product + fold(force * diff)
            square = square + fold(diff * diff)
        acc[0, i] = product
        acc[1, i] = square
        return carry

    lax.fori_loop(0, images, body, 0)
    write_sums(acc, sums_ref)


def first_step(phi, tilt):
    images, parts, rows, lanes = phi.shape
    return pl.pallas_call(
        first_kernel,
        out_shape=[
            jax.ShapeDtypeStruct(phi.shape, jnp.float32),
            jax.ShapeDtypeStruct((1, LANES), jnp.float32),
        ],
        in_specs=[vmem] * 2,
        out_specs=[vmem] * 2,
        scratch_shapes=[
            pltpu.VMEM((parts, rows, lanes), jnp.float32),
            pltpu.VMEM((2, images, 8, lanes), jnp.float32),
        ],
        compiler_params=pltpu.CompilerParams(vmem_limit_bytes=VMEM_LIMIT),
        name="first_step",
    )(phi, tilt)


def second_kernel(coef_ref, phi_ref, moved_ref, tilt_ref, one_ref, two_ref, sums_ref, mu, acc):
    images, parts, rows, lanes = phi_ref.shape
    planes = parts - 1
    keep = inner((rows, lanes))

    def update(i, carry):
        after = jnp.minimum(i + 1, images - 1)
        before = jnp.maximum(i - 1, 0)
        scale = DT * coef_ref[i]
        for p in range(parts):
            one_ref[i, p] = moved_ref[i, p] - scale * (phi_ref[after, p] - phi_ref[before, p])
        return carry

    lax.fori_loop(0, images, update, 0)

    def body(i, carry):
        after = jnp.minimum(i + 1, images - 1)
        before = jnp.maximum(i - 1, 0)
        earlier = jnp.maximum(i - 2, 0)
        potential(lambda p: one_ref[i, p], tilt_ref, mu)
        coef = coef_ref[i]
        sums = [jnp.zeros((8, lanes), jnp.float32)] * 6
        for p in range(planes):
            force = force_plane(mu, p)
            x = one_ref[i, p]
            low = one_ref[before, p]
            diff = jnp.where(keep, one_ref[after, p] - low, 0.0)
            diff_before = x - one_ref[earlier, p]
            two = x + DT * (force - coef * diff)
            two_ref[i, p] = two
            gap = jnp.where(keep, two - two_ref[before, p], 0.0)
            terms = (force * diff, diff * diff, gap * gap, gap * diff, gap * diff_before, diff * diff_before)
            sums = [total + fold(term) for total, term in zip(sums, terms)]
        for q in range(6):
            acc[q, i] = sums[q]
        return carry

    lax.fori_loop(0, images, body, 0)
    write_sums(acc, sums_ref)


def second_step(coef, phi, moved, tilt):
    images, parts, rows, lanes = phi.shape
    return pl.pallas_call(
        second_kernel,
        out_shape=[
            jax.ShapeDtypeStruct(phi.shape, jnp.float32),
            jax.ShapeDtypeStruct((images, parts - 1, rows, lanes), jnp.float32),
            jax.ShapeDtypeStruct((1, LANES), jnp.float32),
        ],
        in_specs=[smem] + [vmem] * 3,
        out_specs=[vmem] * 3,
        scratch_shapes=[
            pltpu.VMEM((parts, rows, lanes), jnp.float32),
            pltpu.VMEM((6, images, 8, lanes), jnp.float32),
        ],
        compiler_params=pltpu.CompilerParams(vmem_limit_bytes=VMEM_LIMIT),
        name="second_step",
    )(coef, phi, moved, tilt)


def mix_kernel(change_ref, lower_ref, share_ref, one_ref, two_ref, out_ref, final):
    images, planes, rows, lanes = two_ref.shape

    def finish(i, carry):
        after = jnp.minimum(i + 1, images - 1)
        before = jnp.maximum(i - 1, 0)
        scale = DT * change_ref[i]
        for p in range(planes):
            final[i, p] = two_ref[i, p] - scale * (one_ref[after, p] - one_ref[before, p])
        return carry

    lax.fori_loop(0, images, finish, 0)

    def body(j, carry):
        lower = lower_ref[j]
        share = share_ref[j]
        for p in range(planes):
            mixed = (1.0 - share) * final[lower, p] + share * final[lower + 1, p]
            out_ref[j, p] = mixed[RIM : rows - RIM]
        return carry

    lax.fori_loop(0, images, body, 0)


def mix(change, lower, share, one, two):
    images, planes, rows, lanes = two.shape
    return pl.pallas_call(
        mix_kernel,
        out_shape=jax.ShapeDtypeStruct((images, planes, rows - 2 * RIM, lanes), jnp.float32),
        in_specs=[smem] * 3 + [vmem] * 2,
        out_specs=vmem,
        scratch_shapes=[pltpu.VMEM(two.shape, jnp.float32)],
        compiler_params=pltpu.CompilerParams(vmem_limit_bytes=VMEM_LIMIT),
        name="mix",
    )(change, lower, share, one, two)


def spacing(dist):
    count = dist.shape[0]
    arc = jnp.cumsum(dist)
    target = jnp.arange(count).astype(dist.dtype) * (arc[count - 1] / (count - 1))
    slots = jnp.arange(count, dtype=jnp.int32)
    inside = (
        (slots[None, :] >= 1) & (slots[None, :] <= count - 2) & (arc[None, :] <= target[:, None])
    )
    lower = jnp.sum(inside.astype(jnp.int32), axis=1)
    pick_low = (slots[None, :] == lower[:, None]).astype(dist.dtype)
    pick_high = (slots[None, :] == lower[:, None] + 1).astype(dist.dtype)
    start = jnp.sum(pick_low * arc[None, :], axis=1)
    length = jnp.sum(pick_high * dist[None, :], axis=1)
    return lower, (target - start) / length


def total_over_all(row, axes):
    count = lax.axis_size(axes)
    spread = jnp.broadcast_to(row[None], (count, *row.shape))
    gathered = lax.all_to_all(spread, axes, split_axis=0, concat_axis=0, tiled=True)
    return jnp.sum(gathered, axis=(0, 1))


def rim_rows(block, axis):
    count = lax.axis_size(axis)
    ahead = [(i, (i + 1) % count) for i in range(count)]
    back = [(target, source) for source, target in ahead]
    return lax.ppermute(block[..., -8:, :], axis, ahead), lax.ppermute(block[..., :8, :], axis, back)


def per_device(axes, path, tilt):
    images = lax.axis_size("img")
    slot = jnp.arange(images)
    interior = (slot > 0) & (slot < images - 1)
    low, high = rim_rows(path[0], "space")
    tilt_low, tilt_high = rim_rows(tilt, "space")
    place = lax.axis_index("img").astype(jnp.int32)[None]
    packed = pack(path[0], low, high)
    tilt_block = pack_one(place, tilt, tilt_low, tilt_high)
    phi = lax.all_to_all(packed, "img", split_axis=0, concat_axis=0, tiled=True)
    moved, sums = first_step(phi, tilt_block)
    sums = total_over_all(sums, axes)
    coef = jnp.where(interior, sums[:images] / (sums[images : 2 * images] + EPS), 0.0)
    one, two, sums = second_step(coef, phi, moved, tilt_block)
    sums = total_over_all(sums, axes)[: 6 * images].reshape(6, images)
    products, squares, gaps, gap_diff, gap_before, diff_before = sums
    change = jnp.where(interior, products / (squares + EPS) - coef, 0.0)
    change_before = jnp.concatenate([jnp.zeros((1,), jnp.float32), change[:-1]])
    squares_before = jnp.concatenate([jnp.zeros((1,), jnp.float32), squares[:-1]])
    cross = change * gap_diff - change_before * gap_before
    tangent = change * change * squares + change_before * change_before * squares_before
    tangent = tangent - 2.0 * change * change_before * diff_before
    length = jnp.maximum(gaps - 2.0 * DT * cross + DT * DT * tangent, 0.0)
    dist = jnp.where(slot > 0, jnp.sqrt(length + EPS), 0.0)
    lower, share = spacing(dist)
    mixed = mix(change, lower, share, one, two)
    back = lax.all_to_all(mixed, "img", split_axis=0, concat_axis=0, tiled=True)
    count, planes, rows, lanes = back.shape
    back = back.reshape(2, count // 2, planes, rows, lanes).transpose(2, 0, 3, 1, 4)
    return back.reshape(1, planes, 2 * rows, count // 2 * lanes)


def solution(mesh):
    return jax.shard_map(
        functools.partial(per_device, tuple(mesh.axis_names)),
        mesh=mesh,
        in_specs=(P("img", None, "space", None), P(None, "space", None)),
        out_specs=P("img", None, "space", None),
        check_vma=False,
    )
```

```python
import functools

import jax
import jax.numpy as jnp
from jax import lax
from jax.experimental import pallas as pl
from jax.experimental.pallas import tpu as pltpu
from jax.sharding import PartitionSpec as P

DT = 0.006
EPS = 1e-06
RIM = 4
TILE = 8
LANES = 128
GROUP = 16
MIB = 1024 * 1024

vmem = pl.BlockSpec(memory_space=pltpu.VMEM)
smem = pl.BlockSpec(memory_space=pltpu.SMEM)
anywhere = pl.BlockSpec(memory_space=pl.ANY)


def lane_of(shape):
    return lax.broadcasted_iota(jnp.int32, shape, len(shape) - 1)


def row_of(shape):
    return lax.broadcasted_iota(jnp.int32, shape, len(shape) - 2)


def edges(tile, p, total):
    place = lane_of(tile.shape) - GROUP * p
    moved = pltpu.roll(tile, GROUP * p + RIM, 1)
    return jnp.where((place >= 0) & (place < 2 * RIM), moved, total)


def strip_of(before, own, after):
    lane = lane_of(own.shape)
    k = lane % GROUP
    left = jnp.where(k < RIM, before, own)
    right = jnp.where(k < RIM, own, after)
    both = jnp.where(k < 2 * RIM, left, pltpu.roll(right, 2 * RIM, 1))
    group = lane - k
    odd = jnp.where(k < 13, group + 8 + (k + 3) // 2, (group + GROUP) % LANES + 8 + (k - 13) // 2)
    source = jnp.where(k % 2 == 0, group + k // 2, odd)
    return jnp.take_along_axis(both, source, axis=1, mode="promise_in_bounds")


def pack_kernel(path_ref, out_ref, held, edge, strips, load_sem, core_sem, strip_sem):
    planes, rows, cols = path_ref.shape
    half = rows // 2
    blocks = cols // LANES
    loads = [pltpu.make_async_copy(path_ref.at[p], held.at[p], load_sem.at[p]) for p in range(planes)]
    for copy in loads:
        copy.start()
    cores = []
    for k in range(2 * blocks):
        r, c = divmod(k, blocks)
        piece = path_ref.at[:, pl.ds(r * half, half), pl.ds(c * LANES, LANES)]
        cores.append(pltpu.make_async_copy(piece, out_ref.at[k, pl.ds(0, planes), pl.ds(0, half)], core_sem.at[k]))
    for copy in cores:
        copy.start()
    for p in range(planes):
        loads[p].wait()
        for c in range(blocks):
            tile = held[p, :, c * LANES : (c + 1) * LANES]
            edge[c] = edges(tile, p, jnp.zeros_like(tile) if p == 0 else edge[c])
    for c in range(blocks):
        strip = strip_of(edge[(c - 1) % blocks], edge[c], edge[(c + 1) % blocks])
        strips[c] = strip[:half]
        strips[blocks + c] = strip[half:]
    copy = pltpu.make_async_copy(strips, out_ref.at[:, planes, pl.ds(0, half)], strip_sem)
    copy.start()
    copy.wait()
    for copy in cores:
        copy.wait()


def pack(path):
    planes, rows, cols = path.shape
    count, half = 2 * cols // LANES, rows // 2
    return pl.pallas_call(
        pack_kernel,
        out_shape=jax.ShapeDtypeStruct((count, planes + 1, half + TILE, LANES), jnp.float32),
        in_specs=[anywhere],
        out_specs=anywhere,
        scratch_shapes=[
            pltpu.VMEM((planes, rows, cols), jnp.float32),
            pltpu.VMEM((count // 2, rows, LANES), jnp.float32),
            pltpu.VMEM((count, half, LANES), jnp.float32),
            pltpu.SemaphoreType.DMA((planes,)),
            pltpu.SemaphoreType.DMA((count,)),
            pltpu.SemaphoreType.DMA,
        ],
        compiler_params=pltpu.CompilerParams(vmem_limit_bytes=12 * MIB),
        cost_estimate=pl.CostEstimate(flops=10_000_000, bytes_accessed=16 * MIB, transcendentals=0),
        name="pack",
    )(path)


def rims_kernel(
    place_ref, path_ref, above_ref, below_ref, tilt_ref, packed_ref, out_ref, tilt_out, own, rims, core, side, edge, sem, out_sem
):
    planes, rows, cols = path_ref.shape
    half = rows // 2
    blocks = cols // LANES
    place = place_ref[0]
    c = place % blocks
    upper = place < blocks
    start = pl.multiple_of((place // blocks) * half, half)
    beside = pl.multiple_of(half - TILE * (place // blocks), TILE)
    middle = path_ref.at[:, pl.ds(half - TILE, 2 * TILE)]
    loads = [
        pltpu.make_async_copy(middle, own.at[:, pl.ds(0, 2 * TILE)], sem.at[0]),
        pltpu.make_async_copy(above_ref.at[0], own.at[:, pl.ds(2 * TILE, TILE)], sem.at[1]),
        pltpu.make_async_copy(below_ref.at[0], own.at[:, pl.ds(3 * TILE, TILE)], sem.at[2]),
    ]
    for at, shift in enumerate((blocks - 1, 0, 1)):
        cut = pl.ds(pl.multiple_of(((c + shift) % blocks) * LANES, LANES), LANES)
        pieces = (
            (tilt_ref.at[:, pl.ds(start, half), cut], core.at[at]),
            (tilt_ref.at[:, pl.ds(beside, TILE), cut], side.at[at, 0]),
            (above_ref.at[1, :, :, cut], side.at[at, 1]),
            (below_ref.at[1, :, :, cut], side.at[at, 2]),
        )
        for k, (source, target) in enumerate(pieces):
            loads.append(pltpu.make_async_copy(source, target, sem.at[3 + 4 * at + k]))
    for copy in loads:
        copy.start()
    for copy in loads:
        copy.wait()
    under = row_of((TILE, LANES)) < RIM
    for r in range(2):
        for b in range(blocks):
            cut = slice(b * LANES, (b + 1) * LANES)
            total = jnp.zeros((TILE, LANES), jnp.float32)
            for p in range(planes):
                if r == 0:
                    tile = jnp.where(under, own[p, TILE : 2 * TILE, cut], own[p, 2 * TILE : 3 * TILE, cut])
                else:
                    tile = jnp.where(under, own[p, 3 * TILE :, cut], own[p, :TILE, cut])
                rims[r * blocks + b, p] = tile
                total = edges(tile, p, total)
            edge[pl.ds(b * TILE, TILE)] = total
        for b in range(blocks):
            tiles = [edge[pl.ds(((b + shift) % blocks) * TILE, TILE)] for shift in (-1, 0, 1)]
            rims[r * blocks + b, planes] = strip_of(*tiles)
    out = pltpu.make_async_copy(rims, out_ref.at[:, :, pl.ds(half, TILE)], out_sem)
    out.start()
    sums = []
    for at in range(3):
        total = jnp.zeros((half + TILE, LANES), jnp.float32)
        for p in range(planes):
            next_to = jnp.where(upper, side[at, 0, p], side[at, 2, p])
            last = jnp.where(upper, side[at, 1, p], side[at, 0, p])
            rim = jnp.where(under, next_to, last)
            full = jnp.concatenate([core[at, p], rim], axis=0)
            if at == 1:
                tilt_out[p] = full
            total = edges(full, p, total)
        sums.append(total)
    tilt_out[planes] = strip_of(*sums)
    out.wait()


def rims(place, path, above, below, tilt, packed):
    planes, rows, cols = path.shape
    count, half = 2 * cols // LANES, rows // 2
    return pl.pallas_call(
        rims_kernel,
        out_shape=[
            jax.ShapeDtypeStruct(packed.shape, jnp.float32),
            jax.ShapeDtypeStruct((planes + 1, half + TILE, LANES), jnp.float32),
        ],
        in_specs=[smem] + [anywhere] * 5,
        out_specs=[anywhere, vmem],
        input_output_aliases={5: 0},
        scratch_shapes=[
            pltpu.VMEM((planes, 4 * TILE, cols), jnp.float32),
            pltpu.VMEM((count, planes + 1, TILE, LANES), jnp.float32),
            pltpu.VMEM((3, planes, half, LANES), jnp.float32),
            pltpu.VMEM((3, 3, planes, TILE, LANES), jnp.float32),
            pltpu.VMEM((cols // LANES * TILE, LANES), jnp.float32),
            pltpu.SemaphoreType.DMA((15,)),
            pltpu.SemaphoreType.DMA,
        ],
        compiler_params=pltpu.CompilerParams(vmem_limit_bytes=8 * MIB),
        cost_estimate=pl.CostEstimate(flops=1_000_000, bytes_accessed=4 * MIB, transcendentals=0),
        name="rims",
    )(place, path, above, below, tilt, packed)


def rows_sum(x):
    return pltpu.roll(x, 1, 0) + pltpu.roll(x, x.shape[0] - 1, 0)


def laplace_strip(s):
    total = pltpu.roll(s, GROUP, 1) + pltpu.roll(s, LANES - GROUP, 1)
    total = total + pltpu.roll(s, 2, 1) + pltpu.roll(s, LANES - 2, 1)
    return total + rows_sum(s) - 6.0 * s


def laplace_plane(x, below, above, strip, p):
    lane = lane_of(x.shape)
    beside = pltpu.roll(strip, (LANES - GROUP * p - 6) % LANES, 1)
    left = jnp.where(lane == 0, beside, pltpu.roll(x, 1, 1))
    right = jnp.where(lane == LANES - 1, beside, pltpu.roll(x, LANES - 1, 1))
    return (below + above) + rows_sum(x) + (left + right) - 6.0 * x


def potential(field, tilt_ref, mu):
    planes = mu.shape[0] - 1
    strip = field(planes)
    mu[planes] = strip * strip * strip - strip - laplace_strip(strip) - tilt_ref[planes]
    for p in range(planes):
        x = field(p)
        lap = laplace_plane(x, field((p - 1) % planes), field((p + 1) % planes), strip, p)
        mu[p] = x * x * x - x - lap - tilt_ref[p]


def force_plane(mu, p):
    planes = mu.shape[0] - 1
    return laplace_plane(mu[p], mu[(p - 1) % planes], mu[(p + 1) % planes], mu[planes], p)


def fold(x):
    total = x[:TILE]
    for at in range(TILE, x.shape[0], TILE):
        total = total + x[at : at + TILE]
    return total


def write_sums(acc, out_ref):
    kinds, images = acc.shape[:2]
    row = jnp.zeros((1, LANES), jnp.float32)
    lane = lane_of((images, LANES))
    image = row_of((images, LANES))
    for q in range(kinds):
        part = jnp.sum(acc[q], axis=1)
        part = jnp.sum(part, axis=1, keepdims=True)
        row = row + jnp.sum(jnp.where(lane == images * q + image, part, 0.0), axis=0, keepdims=True)
    out_ref[...] = jnp.broadcast_to(row[None], out_ref.shape)


def read_sums(sums_ref):
    parts = [sums_ref[k] for k in range(TILE)]
    for k in range(TILE, sums_ref.shape[0]):
        parts[k % TILE] = parts[k % TILE] + sums_ref[k]
    while len(parts) > 1:
        parts = [a + b for a, b in zip(parts[::2], parts[1::2], strict=True)]
    return parts[0]


def spread(row, images):
    shape = (images, LANES)
    picked = jnp.where(lane_of(shape) == row_of(shape), row, 0.0)
    return jnp.broadcast_to(jnp.sum(picked, axis=1, keepdims=True), shape)


def tangent_share(row, images):
    lane = lane_of(row.shape)
    coef = row / (pltpu.roll(row, LANES - images, 1) + EPS)
    return jnp.where((lane > 0) & (lane < images - 1), coef, 0.0)


def first_kernel(phi_ref, tilt_ref, moved_ref, sums_ref, mu, acc):
    images, parts, rows, lanes = phi_ref.shape
    planes = parts - 1
    core = rows - TILE

    def body(i, carry):
        after = jnp.minimum(i + 1, images - 1)
        before = jnp.maximum(i - 1, 0)
        potential(lambda p: phi_ref[i, p], tilt_ref, mu)
        moved_ref[i, planes] = phi_ref[i, planes] + DT * laplace_strip(mu[planes])
        product = jnp.zeros((TILE, lanes), jnp.float32)
        square = jnp.zeros((TILE, lanes), jnp.float32)
        for p in range(planes):
            force = force_plane(mu, p)
            moved_ref[i, p] = phi_ref[i, p] + DT * force
            diff = phi_ref[after, p, :core] - phi_ref[before, p, :core]
            product = product + fold(force[:core] * diff)
            square = square + fold(diff * diff)
        acc[0, i] = product
        acc[1, i] = square
        return carry

    lax.fori_loop(0, images, body, 0)
    write_sums(acc, sums_ref)


def first_step(phi, tilt, devices):
    images, parts, rows, lanes = phi.shape
    return pl.pallas_call(
        first_kernel,
        out_shape=[
            jax.ShapeDtypeStruct(phi.shape, jnp.float32),
            jax.ShapeDtypeStruct((devices, 1, LANES), jnp.float32),
        ],
        in_specs=[vmem] * 2,
        out_specs=[vmem] * 2,
        scratch_shapes=[
            pltpu.VMEM((parts, rows, lanes), jnp.float32),
            pltpu.VMEM((2, images, TILE, lanes), jnp.float32),
        ],
        compiler_params=pltpu.CompilerParams(vmem_limit_bytes=16 * MIB),
        name="first_step",
    )(phi, tilt)


def second_kernel(given_ref, phi_ref, moved_ref, tilt_ref, one_ref, two_ref, coef_ref, sums_ref, mu, acc, coefs):
    images, parts, rows, lanes = phi_ref.shape
    planes = parts - 1
    core = rows - TILE
    coef_row = tangent_share(read_sums(given_ref), images)
    coef_ref[...] = coef_row
    coefs[...] = spread(coef_row, images)

    def update(i, carry):
        after = jnp.minimum(i + 1, images - 1)
        before = jnp.maximum(i - 1, 0)
        scale = DT * coefs[pl.ds(i, 1)]
        for p in range(parts):
            one_ref[i, p] = moved_ref[i, p] - scale * (phi_ref[after, p] - phi_ref[before, p])
        return carry

    lax.fori_loop(0, images, update, 0)

    def body(i, carry):
        after = jnp.minimum(i + 1, images - 1)
        before = jnp.maximum(i - 1, 0)
        earlier = jnp.maximum(i - 2, 0)
        potential(lambda p: one_ref[i, p], tilt_ref, mu)
        coef = coefs[pl.ds(i, 1)]
        sums = [jnp.zeros((TILE, lanes), jnp.float32)] * 6
        for p in range(planes):
            force = force_plane(mu, p)[:core]
            x = one_ref[i, p, :core]
            diff = one_ref[after, p, :core] - one_ref[before, p, :core]
            diff_before = x - one_ref[earlier, p, :core]
            two = x + DT * (force - coef * diff)
            two_ref[i, p] = two
            gap = two - two_ref[before, p]
            terms = (force * diff, diff * diff, gap * gap, gap * diff, gap * diff_before, diff * diff_before)
            sums = [total + fold(term) for total, term in zip(sums, terms, strict=True)]
        for q in range(6):
            acc[q, i] = sums[q]
        return carry

    lax.fori_loop(0, images, body, 0)
    write_sums(acc, sums_ref)


def second_step(given, phi, moved, tilt):
    images, parts, rows, lanes = phi.shape
    return pl.pallas_call(
        second_kernel,
        out_shape=[
            jax.ShapeDtypeStruct(phi.shape, jnp.float32),
            jax.ShapeDtypeStruct((images, parts - 1, rows - TILE, lanes), jnp.float32),
            jax.ShapeDtypeStruct((1, LANES), jnp.float32),
            jax.ShapeDtypeStruct(given.shape, jnp.float32),
        ],
        in_specs=[vmem] * 4,
        out_specs=[vmem] * 4,
        scratch_shapes=[
            pltpu.VMEM((parts, rows, lanes), jnp.float32),
            pltpu.VMEM((6, images, TILE, lanes), jnp.float32),
            pltpu.VMEM((images, lanes), jnp.float32),
        ],
        compiler_params=pltpu.CompilerParams(vmem_limit_bytes=26 * MIB),
        name="second_step",
    )(given, phi, moved, tilt)


def spacing(row, coef, images):
    def quantity(q):
        return pltpu.roll(row, (LANES - images * q) % LANES, 1)

    lane = lane_of(row.shape)
    change = jnp.where((lane > 0) & (lane < images - 1), tangent_share(row, images) - coef, 0.0)
    squares, gaps, gap_diff, gap_before, diff_before = (quantity(q) for q in range(1, 6))
    change_before = pltpu.roll(change, 1, 1)
    squares_before = pltpu.roll(squares, 1, 1)
    cross = change * gap_diff - change_before * gap_before
    tangent = change * change * squares + change_before * change_before * squares_before
    tangent = tangent - 2.0 * change * change_before * diff_before
    length = jnp.maximum(gaps - 2.0 * DT * cross + DT * DT * tangent, 0.0)
    dist = jnp.where((lane > 0) & (lane < images), jnp.sqrt(length + EPS), 0.0)

    shape = (images, LANES)
    slot = lane_of(shape)
    image = row_of(shape)
    arc = jnp.sum(jnp.where(image <= slot, spread(dist, images), 0.0), axis=0, keepdims=True)
    total = jnp.sum(dist, axis=1, keepdims=True)
    target = image.astype(jnp.float32) * (total / (images - 1))
    inside = (slot >= 1) & (slot <= images - 2) & (arc <= target)
    lower = jnp.sum(jnp.where(inside, 1.0, 0.0), axis=1, keepdims=True)
    where = slot.astype(jnp.float32)
    start = jnp.sum(jnp.where(where == lower, arc, 0.0), axis=1, keepdims=True)
    step = jnp.sum(jnp.where(where == lower + 1.0, dist, 0.0), axis=1, keepdims=True)
    return change, lower, (target - start) / step


def mix_kernel(given_ref, coef_ref, one_ref, two_ref, out_ref, final, changes, shares):
    images, planes, core, lanes = two_ref.shape
    change, lower, share = spacing(read_sums(given_ref), coef_ref[...], images)
    changes[...] = spread(change, images)
    shares[...] = share
    image = row_of(lower.shape)
    lowers = [jnp.sum(jnp.where(image == j, lower, 0.0)).astype(jnp.int32) for j in range(images)]

    def finish(i, carry):
        after = jnp.minimum(i + 1, images - 1)
        before = jnp.maximum(i - 1, 0)
        scale = DT * changes[pl.ds(i, 1)]
        for p in range(planes):
            final[i, p] = two_ref[i, p] - scale * (one_ref[after, p, :core] - one_ref[before, p, :core])
        return carry

    lax.fori_loop(0, images, finish, 0)
    for j in range(images):
        portion = shares[j : j + 1]
        for p in range(planes):
            out_ref[j, p] = (1.0 - portion) * final[lowers[j], p] + portion * final[lowers[j] + 1, p]


def mix(given, coef, one, two):
    images, planes, core, lanes = two.shape
    return pl.pallas_call(
        mix_kernel,
        out_shape=jax.ShapeDtypeStruct(two.shape, jnp.float32),
        in_specs=[vmem] * 4,
        out_specs=vmem,
        scratch_shapes=[
            pltpu.VMEM(two.shape, jnp.float32),
            pltpu.VMEM((images, lanes), jnp.float32),
            pltpu.VMEM((images, lanes), jnp.float32),
        ],
        compiler_params=pltpu.CompilerParams(vmem_limit_bytes=20 * MIB),
        name="mix",
    )(given, coef, one, two)


def place_kernel(blocks_ref, out_ref, sem):
    count, planes, half, lanes = blocks_ref.shape
    copies = []
    for k in range(count):
        r, c = divmod(k, count // 2)
        piece = out_ref.at[0, :, pl.ds(r * half, half), pl.ds(c * lanes, lanes)]
        copies.append(pltpu.make_async_copy(blocks_ref.at[k], piece, sem.at[k]))
    for copy in copies:
        copy.start()
    for copy in copies:
        copy.wait()


def put_in_place(blocks):
    count, planes, half, lanes = blocks.shape
    return pl.pallas_call(
        place_kernel,
        out_shape=jax.ShapeDtypeStruct((1, planes, 2 * half, count // 2 * lanes), jnp.float32),
        in_specs=[anywhere],
        out_specs=anywhere,
        scratch_shapes=[pltpu.SemaphoreType.DMA((count,))],
        compiler_params=pltpu.CompilerParams(vmem_limit_bytes=MIB),
        name="put_in_place",
    )(blocks)


def exchange(block, axes):
    return lax.all_to_all(block, axes, split_axis=0, concat_axis=0, tiled=True)


def rim_rows(path, tilt, axis):
    count = lax.axis_size(axis)
    ahead = [(i, (i + 1) % count) for i in range(count)]
    back = [(target, source) for source, target in ahead]
    first = jnp.concatenate([path[..., :TILE, :], tilt[None, ..., :TILE, :]])
    last = jnp.concatenate([path[..., -TILE:, :], tilt[None, ..., -TILE:, :]])
    return lax.ppermute(last, axis, ahead), lax.ppermute(first, axis, back)


def per_device(axes, path, tilt):
    devices = lax.axis_size(axes)
    place = lax.axis_index("img").astype(jnp.int32)[None]
    above, below = rim_rows(path, tilt, "space")
    packed = pack(path[0])
    packed, tilt_block = rims(place, path[0], above, below, tilt, packed)
    packed, tilt_block = lax.optimization_barrier((packed, tilt_block))
    phi = exchange(packed, "img")
    moved, sums = first_step(phi, tilt_block, devices)
    one, two, coef, sums = second_step(exchange(sums, axes), phi, moved, tilt_block)
    mixed = mix(exchange(sums, axes), coef, one, two)
    return put_in_place(exchange(mixed, "img"))


def solution(mesh):
    return jax.shard_map(
        functools.partial(per_device, tuple(mesh.axis_names)),
        mesh=mesh,
        in_specs=(P("img", None, "space", None), P(None, "space", None)),
        out_specs=P("img", None, "space", None),
        check_vma=False,
    )
```

```python
import functools

import jax
import jax.numpy as jnp
from jax import lax
from jax.experimental import pallas as pl
from jax.experimental.pallas import tpu as pltpu
from jax.sharding import PartitionSpec as P

DT = 0.006
EPS = 1e-06
RIM = 4
TILE = 8
LANES = 128
GROUP = 16
MIB = 1024 * 1024

vmem = pl.BlockSpec(memory_space=pltpu.VMEM)
smem = pl.BlockSpec(memory_space=pltpu.SMEM)
anywhere = pl.BlockSpec(memory_space=pl.ANY)


def lane_of(shape):
    return lax.broadcasted_iota(jnp.int32, shape, len(shape) - 1)


def row_of(shape):
    return lax.broadcasted_iota(jnp.int32, shape, len(shape) - 2)


def edges(tile, p, total):
    place = lane_of(tile.shape) - GROUP * p
    moved = pltpu.roll(tile, GROUP * p + RIM, 1)
    return jnp.where((place >= 0) & (place < 2 * RIM), moved, total)


def strip_of(before, own, after):
    lane = lane_of(own.shape)
    k = lane % GROUP
    left = jnp.where(k < RIM, before, own)
    right = jnp.where(k < RIM, own, after)
    both = jnp.where(k < 2 * RIM, left, pltpu.roll(right, 2 * RIM, 1))
    group = lane - k
    odd = jnp.where(k < 13, group + 8 + (k + 3) // 2, (group + GROUP) % LANES + 8 + (k - 13) // 2)
    source = jnp.where(k % 2 == 0, group + k // 2, odd)
    return jnp.take_along_axis(both, source, axis=1, mode="promise_in_bounds")


def pack_kernel(place_ref, path_ref, tilt_ref, out_ref, tilt_out, edge, core_sem, rim_sem, tilt_sem):
    planes, rows, cols = path_ref.shape
    half = rows // 2
    blocks = cols // LANES
    place = place_ref[0]
    copies = []
    for k in range(2 * blocks):
        r, c = divmod(k, blocks)
        cut = pl.ds(c * LANES, LANES)
        core = out_ref.at[k, pl.ds(0, planes), pl.ds(0, half)]
        rim = out_ref.at[k, pl.ds(0, planes), pl.ds(half, TILE)]
        own = pl.ds(half - TILE * r, TILE)
        copies.append(pltpu.make_async_copy(path_ref.at[:, pl.ds(r * half, half), cut], core, core_sem.at[k]))
        copies.append(pltpu.make_async_copy(path_ref.at[:, own, cut], rim, rim_sem.at[k]))
    rest = []
    start = pl.multiple_of((place // blocks) * half, half)
    beside = pl.multiple_of(half - TILE * (place // blocks), TILE)
    for at, shift in enumerate((blocks - 1, 0, 1)):
        cut = pl.ds(pl.multiple_of(((place + shift) % blocks) * LANES, LANES), LANES)
        core = tilt_out.at[at, :, pl.ds(0, half)]
        rim = tilt_out.at[at, :, pl.ds(half, TILE)]
        rest.append(pltpu.make_async_copy(tilt_ref.at[:, pl.ds(start, half), cut], core, tilt_sem.at[2 * at]))
        rest.append(pltpu.make_async_copy(tilt_ref.at[:, pl.ds(beside, TILE), cut], rim, tilt_sem.at[2 * at + 1]))
    for copy in copies + rest:
        copy.start()
    for r in range(2):
        for c in range(blocks):
            k = r * blocks + c
            copies[2 * k].wait()
            copies[2 * k + 1].wait()
            total = jnp.zeros((half, LANES), jnp.float32)
            for p in range(planes):
                total = edges(out_ref[k, p, :half], p, total)
            edge[c] = total
        for c in range(blocks):
            strip = strip_of(edge[(c - 1) % blocks], edge[c], edge[(c + 1) % blocks])
            out_ref[r * blocks + c, planes, :half] = strip
    for copy in rest:
        copy.wait()


def pack(place, path, tilt):
    planes, rows, cols = path.shape
    count, half = 2 * cols // LANES, rows // 2
    return pl.pallas_call(
        pack_kernel,
        out_shape=[
            pltpu.VMEM((count, planes + 1, half + TILE, LANES), jnp.float32),
            pltpu.VMEM((3, planes, half + TILE, LANES), jnp.float32),
        ],
        in_specs=[smem] + [anywhere] * 2,
        out_specs=[vmem] * 2,
        scratch_shapes=[
            pltpu.VMEM((count // 2, half, LANES), jnp.float32),
            pltpu.SemaphoreType.DMA((count,)),
            pltpu.SemaphoreType.DMA((count,)),
            pltpu.SemaphoreType.DMA((6,)),
        ],
        compiler_params=pltpu.CompilerParams(vmem_limit_bytes=12 * MIB),
        cost_estimate=pl.CostEstimate(flops=10_000_000, bytes_accessed=16 * MIB, transcendentals=0),
        name="pack",
    )(place, path, tilt)


def rim_kernel(path_ref, tilt_ref, first_ref, last_ref, held, sem):
    rows = path_ref.shape[1]
    copies = []
    for k, ref in enumerate((path_ref, tilt_ref)):
        for at, start in enumerate((0, rows - TILE)):
            copies.append(pltpu.make_async_copy(ref.at[:, pl.ds(start, TILE)], held.at[k, at], sem.at[2 * k + at]))
    for copy in copies:
        copy.start()
    for copy in copies:
        copy.wait()
    for p in range(path_ref.shape[0]):
        upper = row_of(held.shape[3:]) < RIM
        first_ref[p] = jnp.where(upper, held[0, 0, p], pltpu.roll(held[1, 0, p], RIM, 0))
        last_ref[p] = jnp.where(upper, pltpu.roll(held[0, 1, p], RIM, 0), held[1, 1, p])


def rim_rows(path, tilt):
    planes, rows, cols = path.shape
    return pl.pallas_call(
        rim_kernel,
        out_shape=[jax.ShapeDtypeStruct((planes, TILE, cols), jnp.float32)] * 2,
        in_specs=[anywhere] * 2,
        out_specs=[vmem] * 2,
        scratch_shapes=[pltpu.VMEM((2, 2, planes, TILE, cols), jnp.float32), pltpu.SemaphoreType.DMA((4,))],
        compiler_params=pltpu.CompilerParams(vmem_limit_bytes=4 * MIB),
        name="rim_rows",
    )(path, tilt)


def rims_kernel(place_ref, above_ref, below_ref, tilt_ref, packed_ref, out_ref, tilt_out, edge):
    planes, _, cols = above_ref.shape
    count = out_ref.shape[0]
    half = out_ref.shape[2] - TILE
    blocks = count // 2
    place = place_ref[0]
    upper = place < blocks
    under = row_of((TILE, LANES)) < RIM
    for r in range(2):
        for c in range(blocks):
            k = r * blocks + c
            cut = slice(c * LANES, (c + 1) * LANES)
            total = jnp.zeros((TILE, LANES), jnp.float32)
            for p in range(planes):
                own = packed_ref[k, p, half:]
                if r == 0:
                    tile = jnp.where(under, own, pltpu.roll(above_ref[p, :, cut], RIM, 0))
                else:
                    tile = jnp.where(under, below_ref[p, :, cut], own)
                out_ref[k, p, half:] = tile
                total = edges(tile, p, total)
            edge[c] = total
        for c in range(blocks):
            strip = strip_of(edge[(c - 1) % blocks], edge[c], edge[(c + 1) % blocks])
            out_ref[r * blocks + c, planes, half:] = strip
    sums = []
    for at, shift in enumerate((blocks - 1, 0, 1)):
        cut = pl.ds(pl.multiple_of(((place + shift) % blocks) * LANES, LANES), LANES)
        total = jnp.zeros((half + TILE, LANES), jnp.float32)
        for p in range(planes):
            own = tilt_ref[at, p, half:]
            next_to = jnp.where(upper, own, pltpu.roll(below_ref[p, :, cut], RIM, 0))
            last = jnp.where(upper, above_ref[p, :, cut], own)
            full = jnp.concatenate([tilt_ref[at, p, :half], jnp.where(under, next_to, last)], axis=0)
            if at == 1:
                tilt_out[p] = full
            total = edges(full, p, total)
        sums.append(total)
    tilt_out[planes] = strip_of(*sums)


def rims(place, above, below, tilt, packed):
    planes, _, cols = above.shape
    return pl.pallas_call(
        rims_kernel,
        out_shape=[
            pltpu.VMEM(packed.shape, jnp.float32),
            pltpu.VMEM((planes + 1, *packed.shape[2:]), jnp.float32),
        ],
        in_specs=[smem] + [vmem] * 4,
        out_specs=[vmem] * 2,
        input_output_aliases={4: 0},
        scratch_shapes=[pltpu.VMEM((cols // LANES, TILE, LANES), jnp.float32)],
        compiler_params=pltpu.CompilerParams(vmem_limit_bytes=12 * MIB),
        cost_estimate=pl.CostEstimate(flops=1_000_000, bytes_accessed=4 * MIB, transcendentals=0),
        name="rims",
    )(place, above, below, tilt, packed)


def rows_sum(x):
    return pltpu.roll(x, 1, 0) + pltpu.roll(x, x.shape[0] - 1, 0)


def laplace_strip(s):
    total = pltpu.roll(s, GROUP, 1) + pltpu.roll(s, LANES - GROUP, 1)
    total = total + pltpu.roll(s, 2, 1) + pltpu.roll(s, LANES - 2, 1)
    return total + rows_sum(s) - 6.0 * s


def laplace_plane(x, below, above, strip, p):
    lane = lane_of(x.shape)
    beside = pltpu.roll(strip, (LANES - GROUP * p - 6) % LANES, 1)
    left = jnp.where(lane == 0, beside, pltpu.roll(x, 1, 1))
    right = jnp.where(lane == LANES - 1, beside, pltpu.roll(x, LANES - 1, 1))
    return (below + above) + rows_sum(x) + (left + right) - 6.0 * x


def potential(field, tilt_ref, mu):
    planes = mu.shape[0] - 1
    strip = field(planes)
    mu[planes] = strip * strip * strip - strip - laplace_strip(strip) - tilt_ref[planes]
    for p in range(planes):
        x = field(p)
        lap = laplace_plane(x, field((p - 1) % planes), field((p + 1) % planes), strip, p)
        mu[p] = x * x * x - x - lap - tilt_ref[p]


def force_plane(mu, p):
    planes = mu.shape[0] - 1
    return laplace_plane(mu[p], mu[(p - 1) % planes], mu[(p + 1) % planes], mu[planes], p)


def fold(x):
    total = x[:TILE]
    for at in range(TILE, x.shape[0], TILE):
        total = total + x[at : at + TILE]
    return total


def write_sums(acc, out_ref):
    kinds, images = acc.shape[:2]
    row = jnp.zeros((1, LANES), jnp.float32)
    lane = lane_of((images, LANES))
    image = row_of((images, LANES))
    for q in range(kinds):
        part = jnp.sum(acc[q], axis=1)
        part = jnp.sum(part, axis=1, keepdims=True)
        row = row + jnp.sum(jnp.where(lane == images * q + image, part, 0.0), axis=0, keepdims=True)
    out_ref[...] = jnp.broadcast_to(row[None], out_ref.shape)


def read_sums(sums_ref):
    parts = [sums_ref[k] for k in range(TILE)]
    for k in range(TILE, sums_ref.shape[0]):
        parts[k % TILE] = parts[k % TILE] + sums_ref[k]
    while len(parts) > 1:
        parts = [a + b for a, b in zip(parts[::2], parts[1::2], strict=True)]
    return parts[0]


def spread(row, images):
    shape = (images, LANES)
    picked = jnp.where(lane_of(shape) == row_of(shape), row, 0.0)
    return jnp.broadcast_to(jnp.sum(picked, axis=1, keepdims=True), shape)


def tangent_share(row, images):
    lane = lane_of(row.shape)
    coef = row / (pltpu.roll(row, LANES - images, 1) + EPS)
    return jnp.where((lane > 0) & (lane < images - 1), coef, 0.0)


def first_kernel(phi_ref, tilt_ref, moved_ref, sums_ref, mu, acc):
    images, parts, rows, lanes = phi_ref.shape
    planes = parts - 1
    core = rows - TILE

    def body(i, carry):
        after = jnp.minimum(i + 1, images - 1)
        before = jnp.maximum(i - 1, 0)
        potential(lambda p: phi_ref[i, p], tilt_ref, mu)
        moved_ref[i, planes] = phi_ref[i, planes] + DT * laplace_strip(mu[planes])
        product = jnp.zeros((TILE, lanes), jnp.float32)
        square = jnp.zeros((TILE, lanes), jnp.float32)
        for p in range(planes):
            force = force_plane(mu, p)
            moved_ref[i, p] = phi_ref[i, p] + DT * force
            diff = phi_ref[after, p, :core] - phi_ref[before, p, :core]
            product = product + fold(force[:core] * diff)
            square = square + fold(diff * diff)
        acc[0, i] = product
        acc[1, i] = square
        return carry

    lax.fori_loop(0, images, body, 0, unroll=2)
    write_sums(acc, sums_ref)


def first_step(phi, tilt, devices):
    images, parts, rows, lanes = phi.shape
    return pl.pallas_call(
        first_kernel,
        out_shape=[
            jax.ShapeDtypeStruct(phi.shape, jnp.float32),
            jax.ShapeDtypeStruct((devices, 1, LANES), jnp.float32),
        ],
        in_specs=[vmem] * 2,
        out_specs=[vmem] * 2,
        scratch_shapes=[
            pltpu.VMEM((parts, rows, lanes), jnp.float32),
            pltpu.VMEM((2, images, TILE, lanes), jnp.float32),
        ],
        compiler_params=pltpu.CompilerParams(vmem_limit_bytes=16 * MIB),
        name="first_step",
    )(phi, tilt)


def second_kernel(given_ref, phi_ref, moved_ref, tilt_ref, one_ref, two_ref, coef_ref, sums_ref, mu, acc, coefs):
    images, parts, rows, lanes = phi_ref.shape
    planes = parts - 1
    core = rows - TILE
    coef_row = tangent_share(read_sums(given_ref), images)
    coef_ref[...] = coef_row
    coefs[...] = spread(coef_row, images)

    def update(i, carry):
        after = jnp.minimum(i + 1, images - 1)
        before = jnp.maximum(i - 1, 0)
        scale = DT * coefs[pl.ds(i, 1)]
        for p in range(parts):
            one_ref[i, p] = moved_ref[i, p] - scale * (phi_ref[after, p] - phi_ref[before, p])
        return carry

    lax.fori_loop(0, images, update, 0)

    def body(i, carry):
        after = jnp.minimum(i + 1, images - 1)
        before = jnp.maximum(i - 1, 0)
        earlier = jnp.maximum(i - 2, 0)
        potential(lambda p: one_ref[i, p], tilt_ref, mu)
        coef = coefs[pl.ds(i, 1)]
        sums = [jnp.zeros((TILE, lanes), jnp.float32)] * 6
        for p in range(planes):
            force = force_plane(mu, p)[:core]
            x = one_ref[i, p, :core]
            diff = one_ref[after, p, :core] - one_ref[before, p, :core]
            diff_before = x - one_ref[earlier, p, :core]
            two = x + DT * (force - coef * diff)
            two_ref[i, p] = two
            gap = two - two_ref[before, p]
            terms = (force * diff, diff * diff, gap * gap, gap * diff, gap * diff_before, diff * diff_before)
            sums = [total + fold(term) for total, term in zip(sums, terms, strict=True)]
        for q in range(6):
            acc[q, i] = sums[q]
        return carry

    lax.fori_loop(0, images, body, 0, unroll=2)
    write_sums(acc, sums_ref)


def second_step(given, phi, moved, tilt):
    images, parts, rows, lanes = phi.shape
    return pl.pallas_call(
        second_kernel,
        out_shape=[
            jax.ShapeDtypeStruct(phi.shape, jnp.float32),
            jax.ShapeDtypeStruct((images, parts - 1, rows - TILE, lanes), jnp.float32),
            jax.ShapeDtypeStruct((1, LANES), jnp.float32),
            jax.ShapeDtypeStruct(given.shape, jnp.float32),
        ],
        in_specs=[vmem] * 4,
        out_specs=[vmem] * 4,
        scratch_shapes=[
            pltpu.VMEM((parts, rows, lanes), jnp.float32),
            pltpu.VMEM((6, images, TILE, lanes), jnp.float32),
            pltpu.VMEM((images, lanes), jnp.float32),
        ],
        compiler_params=pltpu.CompilerParams(vmem_limit_bytes=26 * MIB),
        name="second_step",
    )(given, phi, moved, tilt)


def spacing(row, coef, images):
    def quantity(q):
        return pltpu.roll(row, (LANES - images * q) % LANES, 1)

    lane = lane_of(row.shape)
    change = jnp.where((lane > 0) & (lane < images - 1), tangent_share(row, images) - coef, 0.0)
    squares, gaps, gap_diff, gap_before, diff_before = (quantity(q) for q in range(1, 6))
    change_before = pltpu.roll(change, 1, 1)
    squares_before = pltpu.roll(squares, 1, 1)
    cross = change * gap_diff - change_before * gap_before
    tangent = change * change * squares + change_before * change_before * squares_before
    tangent = tangent - 2.0 * change * change_before * diff_before
    length = jnp.maximum(gaps - 2.0 * DT * cross + DT * DT * tangent, 0.0)
    dist = jnp.where((lane > 0) & (lane < images), jnp.sqrt(length + EPS), 0.0)

    shape = (images, LANES)
    slot = lane_of(shape)
    image = row_of(shape)
    arc = jnp.sum(jnp.where(image <= slot, spread(dist, images), 0.0), axis=0, keepdims=True)
    total = jnp.sum(dist, axis=1, keepdims=True)
    target = image.astype(jnp.float32) * (total / (images - 1))
    inside = (slot >= 1) & (slot <= images - 2) & (arc <= target)
    lower = jnp.sum(jnp.where(inside, 1.0, 0.0), axis=1, keepdims=True)
    where = slot.astype(jnp.float32)
    start = jnp.sum(jnp.where(where == lower, arc, 0.0), axis=1, keepdims=True)
    step = jnp.sum(jnp.where(where == lower + 1.0, dist, 0.0), axis=1, keepdims=True)
    return change, lower, (target - start) / step


def mix_kernel(given_ref, coef_ref, one_ref, two_ref, out_ref, final, changes, shares):
    images, planes, core, lanes = two_ref.shape
    change, lower, share = spacing(read_sums(given_ref), coef_ref[...], images)
    changes[...] = spread(change, images)
    shares[...] = share
    image = row_of(lower.shape)
    lowers = [jnp.sum(jnp.where(image == j, lower, 0.0)).astype(jnp.int32) for j in range(images)]

    def finish(i, carry):
        after = jnp.minimum(i + 1, images - 1)
        before = jnp.maximum(i - 1, 0)
        scale = DT * changes[pl.ds(i, 1)]
        for p in range(planes):
            final[i, p] = two_ref[i, p] - scale * (one_ref[after, p, :core] - one_ref[before, p, :core])
        return carry

    lax.fori_loop(0, images, finish, 0)
    for j in range(images):
        portion = shares[j : j + 1]
        for p in range(planes):
            out_ref[j, p] = (1.0 - portion) * final[lowers[j], p] + portion * final[lowers[j] + 1, p]


def mix(given, coef, one, two):
    images, planes, core, lanes = two.shape
    return pl.pallas_call(
        mix_kernel,
        out_shape=jax.ShapeDtypeStruct(two.shape, jnp.float32),
        in_specs=[vmem] * 4,
        out_specs=vmem,
        scratch_shapes=[
            pltpu.VMEM(two.shape, jnp.float32),
            pltpu.VMEM((images, lanes), jnp.float32),
            pltpu.VMEM((images, lanes), jnp.float32),
        ],
        compiler_params=pltpu.CompilerParams(vmem_limit_bytes=20 * MIB),
        name="mix",
    )(given, coef, one, two)


def place_kernel(blocks_ref, out_ref, sem):
    count, planes, half, lanes = blocks_ref.shape
    copies = []
    for k in range(count):
        r, c = divmod(k, count // 2)
        piece = out_ref.at[0, :, pl.ds(r * half, half), pl.ds(c * lanes, lanes)]
        copies.append(pltpu.make_async_copy(blocks_ref.at[k], piece, sem.at[k]))
    for copy in copies:
        copy.start()
    for copy in copies:
        copy.wait()


def put_in_place(blocks):
    count, planes, half, lanes = blocks.shape
    return pl.pallas_call(
        place_kernel,
        out_shape=jax.ShapeDtypeStruct((1, planes, 2 * half, count // 2 * lanes), jnp.float32),
        in_specs=[anywhere],
        out_specs=anywhere,
        scratch_shapes=[pltpu.SemaphoreType.DMA((count,))],
        compiler_params=pltpu.CompilerParams(vmem_limit_bytes=MIB),
        name="put_in_place",
    )(blocks)


def exchange(block, axes):
    return lax.all_to_all(block, axes, split_axis=0, concat_axis=0, tiled=True)


def per_device(axes, path, tilt):
    devices = lax.axis_size(axes)
    place = lax.axis_index("img").astype(jnp.int32)[None]
    own = pltpu.with_memory_space_constraint(path[0], pltpu.HBM)
    tilt = pltpu.with_memory_space_constraint(tilt, pltpu.HBM)
    first, last = rim_rows(own, tilt)
    count = lax.axis_size("space")
    ahead = [(i, (i + 1) % count) for i in range(count)]
    above = lax.ppermute(last, "space", ahead)
    below = lax.ppermute(first, "space", [(target, source) for source, target in ahead])
    packed, tilt_near = pack(place, own, tilt)
    packed, tilt_block = rims(place, above, below, tilt_near, packed)
    packed, tilt_block = lax.optimization_barrier((packed, tilt_block))
    phi = exchange(packed, "img")
    moved, sums = first_step(phi, tilt_block, devices)
    one, two, coef, sums = second_step(exchange(sums, axes), phi, moved, tilt_block)
    mixed = mix(exchange(sums, axes), coef, one, two)
    return put_in_place(exchange(mixed, "img"))


def solution(mesh):
    return jax.shard_map(
        functools.partial(per_device, tuple(mesh.axis_names)),
        mesh=mesh,
        in_specs=(P("img", None, "space", None), P(None, "space", None)),
        out_specs=P("img", None, "space", None),
        check_vma=False,
    )
```

```python
import functools

import jax
import jax.numpy as jnp
from jax import lax
from jax.experimental import pallas as pl
from jax.experimental.pallas import tpu as pltpu
from jax.sharding import PartitionSpec as P

DT = 0.006
EPS = 1e-06
RIM = 4
TILE = 8
LANES = 128
GROUP = 16
MIB = 1024 * 1024

vmem = pl.BlockSpec(memory_space=pltpu.VMEM)
smem = pl.BlockSpec(memory_space=pltpu.SMEM)
anywhere = pl.BlockSpec(memory_space=pl.ANY)


def lane_of(shape):
    return lax.broadcasted_iota(jnp.int32, shape, len(shape) - 1)


def row_of(shape):
    return lax.broadcasted_iota(jnp.int32, shape, len(shape) - 2)


def edges(tile, p, total):
    place = lane_of(tile.shape) - GROUP * p
    moved = pltpu.roll(tile, GROUP * p + RIM, 1)
    return jnp.where((place >= 0) & (place < 2 * RIM), moved, total)


def strip_of(before, own, after):
    lane = lane_of(own.shape)
    k = lane % GROUP
    left = jnp.where(k < RIM, before, own)
    right = jnp.where(k < RIM, own, after)
    both = jnp.where(k < 2 * RIM, left, pltpu.roll(right, 2 * RIM, 1))
    group = lane - k
    odd = jnp.where(k < 13, group + 8 + (k + 3) // 2, (group + GROUP) % LANES + 8 + (k - 13) // 2)
    source = jnp.where(k % 2 == 0, group + k // 2, odd)
    return jnp.take_along_axis(both, source, axis=1, mode="promise_in_bounds")


def pack_kernel(place_ref, path_ref, tilt_ref, out_ref, tilt_out, edge, core_sem, rim_sem, tilt_sem):
    planes, rows, cols = path_ref.shape
    half = rows // 2
    blocks = cols // LANES
    place = place_ref[0]
    copies = []
    for k in range(2 * blocks):
        r, c = divmod(k, blocks)
        cut = pl.ds(c * LANES, LANES)
        core = out_ref.at[k, pl.ds(0, planes), pl.ds(0, half)]
        rim = out_ref.at[k, pl.ds(0, planes), pl.ds(half, TILE)]
        own = pl.ds(half - TILE * r, TILE)
        copies.append(pltpu.make_async_copy(path_ref.at[:, pl.ds(r * half, half), cut], core, core_sem.at[k]))
        copies.append(pltpu.make_async_copy(path_ref.at[:, own, cut], rim, rim_sem.at[k]))
    rest = []
    start = pl.multiple_of((place // blocks) * half, half)
    beside = pl.multiple_of(half - TILE * (place // blocks), TILE)
    for at, shift in enumerate((blocks - 1, 0, 1)):
        cut = pl.ds(pl.multiple_of(((place + shift) % blocks) * LANES, LANES), LANES)
        core = tilt_out.at[at, :, pl.ds(0, half)]
        rim = tilt_out.at[at, :, pl.ds(half, TILE)]
        rest.append(pltpu.make_async_copy(tilt_ref.at[:, pl.ds(start, half), cut], core, tilt_sem.at[2 * at]))
        rest.append(pltpu.make_async_copy(tilt_ref.at[:, pl.ds(beside, TILE), cut], rim, tilt_sem.at[2 * at + 1]))
    for copy in copies + rest:
        copy.start()
    for r in range(2):
        for c in range(blocks):
            k = r * blocks + c
            copies[2 * k].wait()
            copies[2 * k + 1].wait()
            total = jnp.zeros((half, LANES), jnp.float32)
            for p in range(planes):
                total = edges(out_ref[k, p, :half], p, total)
            edge[c] = total
        for c in range(blocks):
            strip = strip_of(edge[(c - 1) % blocks], edge[c], edge[(c + 1) % blocks])
            out_ref[r * blocks + c, planes, :half] = strip
    for copy in rest:
        copy.wait()


def pack(place, path, tilt):
    planes, rows, cols = path.shape
    count, half = 2 * cols // LANES, rows // 2
    return pl.pallas_call(
        pack_kernel,
        out_shape=[
            pltpu.VMEM((count, planes + 1, half + TILE, LANES), jnp.float32),
            pltpu.VMEM((3, planes, half + TILE, LANES), jnp.float32),
        ],
        in_specs=[smem] + [anywhere] * 2,
        out_specs=[vmem] * 2,
        scratch_shapes=[
            pltpu.VMEM((count // 2, half, LANES), jnp.float32),
            pltpu.SemaphoreType.DMA((count,)),
            pltpu.SemaphoreType.DMA((count,)),
            pltpu.SemaphoreType.DMA((6,)),
        ],
        compiler_params=pltpu.CompilerParams(vmem_limit_bytes=12 * MIB),
        cost_estimate=pl.CostEstimate(flops=10_000_000, bytes_accessed=16 * MIB, transcendentals=0),
        name="pack",
    )(place, path, tilt)


def rim_kernel(path_ref, tilt_ref, first_ref, last_ref, held, sem):
    rows = path_ref.shape[1]
    copies = []
    for k, ref in enumerate((path_ref, tilt_ref)):
        for at, start in enumerate((0, rows - TILE)):
            copies.append(pltpu.make_async_copy(ref.at[:, pl.ds(start, TILE)], held.at[k, at], sem.at[2 * k + at]))
    for copy in copies:
        copy.start()
    for copy in copies:
        copy.wait()
    for p in range(path_ref.shape[0]):
        upper = row_of(held.shape[3:]) < RIM
        first_ref[p] = jnp.where(upper, held[0, 0, p], pltpu.roll(held[1, 0, p], RIM, 0))
        last_ref[p] = jnp.where(upper, pltpu.roll(held[0, 1, p], RIM, 0), held[1, 1, p])


def rim_rows(path, tilt):
    planes, rows, cols = path.shape
    return pl.pallas_call(
        rim_kernel,
        out_shape=[jax.ShapeDtypeStruct((planes, TILE, cols), jnp.float32)] * 2,
        in_specs=[anywhere] * 2,
        out_specs=[vmem] * 2,
        scratch_shapes=[pltpu.VMEM((2, 2, planes, TILE, cols), jnp.float32), pltpu.SemaphoreType.DMA((4,))],
        compiler_params=pltpu.CompilerParams(vmem_limit_bytes=4 * MIB),
        name="rim_rows",
    )(path, tilt)


def rims_kernel(place_ref, above_ref, below_ref, tilt_ref, packed_ref, out_ref, tilt_out, edge):
    planes, _, cols = above_ref.shape
    count = out_ref.shape[0]
    half = out_ref.shape[2] - TILE
    blocks = count // 2
    place = place_ref[0]
    upper = place < blocks
    under = row_of((TILE, LANES)) < RIM
    for r in range(2):
        for c in range(blocks):
            k = r * blocks + c
            cut = slice(c * LANES, (c + 1) * LANES)
            total = jnp.zeros((TILE, LANES), jnp.float32)
            for p in range(planes):
                own = packed_ref[k, p, half:]
                if r == 0:
                    tile = jnp.where(under, own, pltpu.roll(above_ref[p, :, cut], RIM, 0))
                else:
                    tile = jnp.where(under, below_ref[p, :, cut], own)
                out_ref[k, p, half:] = tile
                total = edges(tile, p, total)
            edge[c] = total
        for c in range(blocks):
            strip = strip_of(edge[(c - 1) % blocks], edge[c], edge[(c + 1) % blocks])
            out_ref[r * blocks + c, planes, half:] = strip
    sums = []
    for at, shift in enumerate((blocks - 1, 0, 1)):
        cut = pl.ds(pl.multiple_of(((place + shift) % blocks) * LANES, LANES), LANES)
        total = jnp.zeros((half + TILE, LANES), jnp.float32)
        for p in range(planes):
            own = tilt_ref[at, p, half:]
            next_to = jnp.where(upper, own, pltpu.roll(below_ref[p, :, cut], RIM, 0))
            last = jnp.where(upper, above_ref[p, :, cut], own)
            full = jnp.concatenate([tilt_ref[at, p, :half], jnp.where(under, next_to, last)], axis=0)
            if at == 1:
                tilt_out[p] = full
            total = edges(full, p, total)
        sums.append(total)
    tilt_out[planes] = strip_of(*sums)


def rims(place, above, below, tilt, packed):
    planes, _, cols = above.shape
    return pl.pallas_call(
        rims_kernel,
        out_shape=[
            pltpu.VMEM(packed.shape, jnp.float32),
            pltpu.VMEM((planes + 1, *packed.shape[2:]), jnp.float32),
        ],
        in_specs=[smem] + [vmem] * 4,
        out_specs=[vmem] * 2,
        input_output_aliases={4: 0},
        scratch_shapes=[pltpu.VMEM((cols // LANES, TILE, LANES), jnp.float32)],
        compiler_params=pltpu.CompilerParams(vmem_limit_bytes=12 * MIB),
        cost_estimate=pl.CostEstimate(flops=1_000_000, bytes_accessed=4 * MIB, transcendentals=0),
        name="rims",
    )(place, above, below, tilt, packed)


def rows_sum(x):
    return pltpu.roll(x, 1, 0) + pltpu.roll(x, x.shape[0] - 1, 0)


def neighbours_strip(s):
    total = pltpu.roll(s, GROUP, 1) + pltpu.roll(s, LANES - GROUP, 1)
    total = total + pltpu.roll(s, 2, 1) + pltpu.roll(s, LANES - 2, 1)
    return total + rows_sum(s)


def split(x):
    high = x.astype(jnp.bfloat16)
    rest = x - high.astype(jnp.float32)
    middle = rest.astype(jnp.bfloat16)
    low = (rest - middle.astype(jnp.float32)).astype(jnp.bfloat16)
    return jnp.concatenate([high, middle, low], axis=1)


def write_band(band):
    shape = band.shape
    apart = row_of(shape) % LANES - lane_of(shape)
    band[...] = jnp.where((apart == 1) | (apart == -1), 1.0, 0.0).astype(jnp.bfloat16)


def beside_all(planes, band, beside):
    count, rows, lanes = planes.shape
    parts = split(planes.reshape(count * rows, lanes))
    total = jnp.dot(parts, band[...], preferred_element_type=jnp.float32)
    beside[...] = total.reshape(planes.shape)


def neighbours_given(x, below, above, strip, p, within):
    lane = lane_of(x.shape)
    rim = pltpu.roll(strip, (LANES - GROUP * p - 6) % LANES, 1)
    rim = jnp.where((lane == 0) | (lane == LANES - 1), rim, 0.0)
    return (below + above) + rows_sum(x) + (within + rim)


def neighbours_plane(x, below, above, strip, p):
    lane = lane_of(x.shape)
    beside = pltpu.roll(strip, (LANES - GROUP * p - 6) % LANES, 1)
    left = jnp.where(lane == 0, beside, pltpu.roll(x, 1, 1))
    right = jnp.where(lane == LANES - 1, beside, pltpu.roll(x, LANES - 1, 1))
    return (below + above) + rows_sum(x) + (left + right)


def potential(field, whole, tilt_ref, mu, band, beside):
    planes = mu.shape[0] - 1
    strip = field(planes)
    mu[planes] = strip * (strip * strip + 5.0) - (neighbours_strip(strip) + tilt_ref[planes])
    if whole is not None:
        beside_all(whole, band, beside)
    for p in range(planes):
        x = field(p)
        below, above = field((p - 1) % planes), field((p + 1) % planes)
        if whole is None:
            around = neighbours_plane(x, below, above, strip, p)
        else:
            around = neighbours_given(x, below, above, strip, p, beside[p])
        mu[p] = x * (x * x + 5.0) - (around + tilt_ref[p])


def force_plane(mu, p):
    planes = mu.shape[0] - 1
    return neighbours_plane(mu[p], mu[(p - 1) % planes], mu[(p + 1) % planes], mu[planes], p) - 6.0 * mu[p]


def fold(x):
    total = x[:TILE]
    for at in range(TILE, x.shape[0], TILE):
        total = total + x[at : at + TILE]
    return total


def write_sums(acc, out_ref):
    kinds, images = acc.shape[:2]
    row = jnp.zeros((1, LANES), jnp.float32)
    lane = lane_of((images, LANES))
    image = row_of((images, LANES))
    for q in range(kinds):
        part = jnp.sum(acc[q], axis=1)
        part = jnp.sum(part, axis=1, keepdims=True)
        row = row + jnp.sum(jnp.where(lane == images * q + image, part, 0.0), axis=0, keepdims=True)
    out_ref[...] = jnp.broadcast_to(row[None], out_ref.shape)


def read_sums(sums_ref):
    parts = [sums_ref[k] for k in range(TILE)]
    for k in range(TILE, sums_ref.shape[0]):
        parts[k % TILE] = parts[k % TILE] + sums_ref[k]
    while len(parts) > 1:
        parts = [a + b for a, b in zip(parts[::2], parts[1::2], strict=True)]
    return parts[0]


def spread(row, images):
    shape = (images, LANES)
    picked = jnp.where(lane_of(shape) == row_of(shape), row, 0.0)
    return jnp.broadcast_to(jnp.sum(picked, axis=1, keepdims=True), shape)


def tangent_share(row, images):
    lane = lane_of(row.shape)
    coef = row / (pltpu.roll(row, LANES - images, 1) + EPS)
    return jnp.where((lane > 0) & (lane < images - 1), coef, 0.0)


def first_kernel(phi_ref, tilt_ref, moved_ref, sums_ref, mu, acc, band, beside):
    images, parts, rows, lanes = phi_ref.shape
    planes = parts - 1
    core = rows - TILE
    write_band(band)

    def body(i, carry):
        after = jnp.minimum(i + 1, images - 1)
        before = jnp.maximum(i - 1, 0)
        potential(lambda p: phi_ref[i, p], phi_ref[i, :planes], tilt_ref, mu, band, beside)
        moved_ref[i, planes] = phi_ref[i, planes] + DT * (neighbours_strip(mu[planes]) - 6.0 * mu[planes])
        product = jnp.zeros((TILE, lanes), jnp.float32)
        square = jnp.zeros((TILE, lanes), jnp.float32)
        for p in range(planes):
            force = force_plane(mu, p)
            moved_ref[i, p] = phi_ref[i, p] + DT * force
            diff = phi_ref[after, p, :core] - phi_ref[before, p, :core]
            product = product + fold(force[:core] * diff)
            square = square + fold(diff * diff)
        acc[0, i] = product
        acc[1, i] = square
        return carry

    lax.fori_loop(0, images, body, 0, unroll=2)
    write_sums(acc, sums_ref)


def first_step(phi, tilt, devices):
    images, parts, rows, lanes = phi.shape
    return pl.pallas_call(
        first_kernel,
        out_shape=[
            jax.ShapeDtypeStruct(phi.shape, jnp.float32),
            jax.ShapeDtypeStruct((devices, 1, LANES), jnp.float32),
        ],
        in_specs=[vmem] * 2,
        out_specs=[vmem] * 2,
        scratch_shapes=[
            pltpu.VMEM((parts, rows, lanes), jnp.float32),
            pltpu.VMEM((2, images, TILE, lanes), jnp.float32),
            pltpu.VMEM((3 * LANES, LANES), jnp.bfloat16),
            pltpu.VMEM((parts - 1, rows, lanes), jnp.float32),
        ],
        compiler_params=pltpu.CompilerParams(vmem_limit_bytes=16 * MIB),
        name="first_step",
    )(phi, tilt)


def second_kernel(given_ref, phi_ref, moved_ref, tilt_ref, one_ref, two_ref, coef_ref, sums_ref, mu, acc, coefs):
    images, parts, rows, lanes = phi_ref.shape
    planes = parts - 1
    core = rows - TILE
    coef_row = tangent_share(read_sums(given_ref), images)
    coef_ref[...] = coef_row
    coefs[...] = spread(coef_row, images)

    def update(i):
        after = jnp.minimum(i + 1, images - 1)
        before = jnp.maximum(i - 1, 0)
        scale = DT * coefs[pl.ds(i, 1)]
        for p in range(parts):
            one_ref[i, p] = moved_ref[i, p] - scale * (phi_ref[after, p] - phi_ref[before, p])

    update(0)

    def body(i, carry):
        after = jnp.minimum(i + 1, images - 1)
        before = jnp.maximum(i - 1, 0)
        earlier = jnp.maximum(i - 2, 0)
        update(after)
        potential(lambda p: one_ref[i, p], None, tilt_ref, mu, None, None)
        coef = coefs[pl.ds(i, 1)]
        sums = [jnp.zeros((TILE, lanes), jnp.float32)] * 6
        for p in range(planes):
            force = force_plane(mu, p)[:core]
            x = one_ref[i, p, :core]
            diff = one_ref[after, p, :core] - one_ref[before, p, :core]
            diff_before = x - one_ref[earlier, p, :core]
            two = x + DT * (force - coef * diff)
            two_ref[i, p] = two
            gap = two - two_ref[before, p]
            terms = (force * diff, diff * diff, gap * gap, gap * diff, gap * diff_before, diff * diff_before)
            sums = [total + fold(term) for total, term in zip(sums, terms, strict=True)]
        for q in range(6):
            acc[q, i] = sums[q]
        return carry

    lax.fori_loop(0, images, body, 0, unroll=4)
    write_sums(acc, sums_ref)


def second_step(given, phi, moved, tilt):
    images, parts, rows, lanes = phi.shape
    return pl.pallas_call(
        second_kernel,
        out_shape=[
            jax.ShapeDtypeStruct(phi.shape, jnp.float32),
            jax.ShapeDtypeStruct((images, parts - 1, rows - TILE, lanes), jnp.float32),
            jax.ShapeDtypeStruct((1, LANES), jnp.float32),
            jax.ShapeDtypeStruct(given.shape, jnp.float32),
        ],
        in_specs=[vmem] * 4,
        out_specs=[vmem] * 4,
        scratch_shapes=[
            pltpu.VMEM((parts, rows, lanes), jnp.float32),
            pltpu.VMEM((6, images, TILE, lanes), jnp.float32),
            pltpu.VMEM((images, lanes), jnp.float32),
        ],
        compiler_params=pltpu.CompilerParams(vmem_limit_bytes=26 * MIB),
        name="second_step",
    )(given, phi, moved, tilt)


def spacing(row, coef, images):
    def quantity(q):
        return pltpu.roll(row, (LANES - images * q) % LANES, 1)

    lane = lane_of(row.shape)
    change = jnp.where((lane > 0) & (lane < images - 1), tangent_share(row, images) - coef, 0.0)
    squares, gaps, gap_diff, gap_before, diff_before = (quantity(q) for q in range(1, 6))
    change_before = pltpu.roll(change, 1, 1)
    squares_before = pltpu.roll(squares, 1, 1)
    cross = change * gap_diff - change_before * gap_before
    tangent = change * change * squares + change_before * change_before * squares_before
    tangent = tangent - 2.0 * change * change_before * diff_before
    length = jnp.maximum(gaps - 2.0 * DT * cross + DT * DT * tangent, 0.0)
    dist = jnp.where((lane > 0) & (lane < images), jnp.sqrt(length + EPS), 0.0)

    shape = (images, LANES)
    slot = lane_of(shape)
    image = row_of(shape)
    arc = jnp.sum(jnp.where(image <= slot, spread(dist, images), 0.0), axis=0, keepdims=True)
    total = jnp.sum(dist, axis=1, keepdims=True)
    target = image.astype(jnp.float32) * (total / (images - 1))
    inside = (slot >= 1) & (slot <= images - 2) & (arc <= target)
    lower = jnp.sum(jnp.where(inside, 1.0, 0.0), axis=1, keepdims=True)
    where = slot.astype(jnp.float32)
    start = jnp.sum(jnp.where(where == lower, arc, 0.0), axis=1, keepdims=True)
    step = jnp.sum(jnp.where(where == lower + 1.0, dist, 0.0), axis=1, keepdims=True)
    return change, lower, (target - start) / step


def mix_kernel(given_ref, coef_ref, one_ref, two_ref, out_ref, final, changes, shares):
    images, planes, core, lanes = two_ref.shape
    change, lower, share = spacing(read_sums(given_ref), coef_ref[...], images)
    changes[...] = spread(change, images)
    shares[...] = share
    image = row_of(lower.shape)
    lowers = [jnp.sum(jnp.where(image == j, lower, 0.0)).astype(jnp.int32) for j in range(images)]

    def finish(i, carry):
        after = jnp.minimum(i + 1, images - 1)
        before = jnp.maximum(i - 1, 0)
        scale = DT * changes[pl.ds(i, 1)]
        for p in range(planes):
            final[i, p] = two_ref[i, p] - scale * (one_ref[after, p, :core] - one_ref[before, p, :core])
        return carry

    lax.fori_loop(0, images, finish, 0)
    for j in range(images):
        portion = shares[j : j + 1]
        for p in range(planes):
            out_ref[j, p] = (1.0 - portion) * final[lowers[j], p] + portion * final[lowers[j] + 1, p]


def mix(given, coef, one, two):
    images, planes, core, lanes = two.shape
    return pl.pallas_call(
        mix_kernel,
        out_shape=jax.ShapeDtypeStruct(two.shape, jnp.float32),
        in_specs=[vmem] * 4,
        out_specs=vmem,
        scratch_shapes=[
            pltpu.VMEM(two.shape, jnp.float32),
            pltpu.VMEM((images, lanes), jnp.float32),
            pltpu.VMEM((images, lanes), jnp.float32),
        ],
        compiler_params=pltpu.CompilerParams(vmem_limit_bytes=20 * MIB),
        name="mix",
    )(given, coef, one, two)


def place_kernel(blocks_ref, out_ref, sem):
    count, planes, half, lanes = blocks_ref.shape
    copies = []
    for k in range(count):
        r, c = divmod(k, count // 2)
        piece = out_ref.at[0, :, pl.ds(r * half, half), pl.ds(c * lanes, lanes)]
        copies.append(pltpu.make_async_copy(blocks_ref.at[k], piece, sem.at[k]))
    for copy in copies:
        copy.start()
    for copy in copies:
        copy.wait()


def put_in_place(blocks):
    count, planes, half, lanes = blocks.shape
    return pl.pallas_call(
        place_kernel,
        out_shape=jax.ShapeDtypeStruct((1, planes, 2 * half, count // 2 * lanes), jnp.float32),
        in_specs=[anywhere],
        out_specs=anywhere,
        scratch_shapes=[pltpu.SemaphoreType.DMA((count,))],
        compiler_params=pltpu.CompilerParams(vmem_limit_bytes=MIB),
        name="put_in_place",
    )(blocks)


def exchange(block, axes):
    return lax.all_to_all(block, axes, split_axis=0, concat_axis=0, tiled=True)


def per_device(axes, path, tilt):
    devices = lax.axis_size(axes)
    place = lax.axis_index("img").astype(jnp.int32)[None]
    own = pltpu.with_memory_space_constraint(path[0], pltpu.HBM)
    tilt = pltpu.with_memory_space_constraint(tilt, pltpu.HBM)
    first, last = rim_rows(own, tilt)
    count = lax.axis_size("space")
    ahead = [(i, (i + 1) % count) for i in range(count)]
    above = lax.ppermute(last, "space", ahead)
    below = lax.ppermute(first, "space", [(target, source) for source, target in ahead])
    packed, tilt_near = pack(place, own, tilt)
    packed, tilt_block = rims(place, above, below, tilt_near, packed)
    packed, tilt_block = lax.optimization_barrier((packed, tilt_block))
    phi = exchange(packed, "img")
    moved, sums = first_step(phi, tilt_block, devices)
    one, two, coef, sums = second_step(exchange(sums, axes), phi, moved, tilt_block)
    mixed = mix(exchange(sums, axes), coef, one, two)
    return put_in_place(exchange(mixed, "img"))


def solution(mesh):
    return jax.shard_map(
        functools.partial(per_device, tuple(mesh.axis_names)),
        mesh=mesh,
        in_specs=(P("img", None, "space", None), P(None, "space", None)),
        out_specs=P("img", None, "space", None),
        check_vma=False,
    )
```

```python
import functools

import jax
import jax.numpy as jnp
from jax import lax
from jax.experimental import pallas as pl
from jax.experimental.pallas import tpu as pltpu
from jax.sharding import PartitionSpec as P

DT = 0.006
EPS = 1e-06
RIM = 4
TILE = 8
LANES = 128
GROUP = 16
MIB = 1024 * 1024
SLOTS = 4

vmem = pl.BlockSpec(memory_space=pltpu.VMEM)
smem = pl.BlockSpec(memory_space=pltpu.SMEM)
anywhere = pl.BlockSpec(memory_space=pl.ANY)


def lane_of(shape):
    return lax.broadcasted_iota(jnp.int32, shape, len(shape) - 1)


def row_of(shape):
    return lax.broadcasted_iota(jnp.int32, shape, len(shape) - 2)


def edges(tile, p, total):
    place = lane_of(tile.shape) - GROUP * p
    moved = pltpu.roll(tile, GROUP * p + RIM, 1)
    return jnp.where((place >= 0) & (place < 2 * RIM), moved, total)


def strip_of(before, own, after):
    lane = lane_of(own.shape)
    k = lane % GROUP
    left = jnp.where(k < RIM, before, own)
    right = jnp.where(k < RIM, own, after)
    both = jnp.where(k < 2 * RIM, left, pltpu.roll(right, 2 * RIM, 1))
    group = lane - k
    odd = jnp.where(k < 13, group + 8 + (k + 3) // 2, (group + GROUP) % LANES + 8 + (k - 13) // 2)
    source = jnp.where(k % 2 == 0, group + k // 2, odd)
    return jnp.take_along_axis(both, source, axis=1, mode="promise_in_bounds")


def own_plane(shape):
    lane = lane_of(shape)
    k = lane % GROUP
    group = lane // GROUP
    even = (k % 2 == 0) & (k >= 2 * RIM)
    here = even | (k == 1) | (k == 3)
    there = (k == 13) | (k == 15)
    return jnp.where(here, group, jnp.where(there, (group + 1) % (LANES // GROUP), -1))


def outer(before, after):
    lane = lane_of(before.shape)
    k = lane % GROUP
    both = jnp.where(k < RIM, before, after)
    source = lane - k + jnp.where(k % 2 == 0, k // 2, (k + 3) // 2) % (2 * RIM)
    return jnp.take_along_axis(both, source, axis=1, mode="promise_in_bounds")


def beside(first, second):
    return jnp.where(own_plane(first.shape) < 0, first, pltpu.roll(second, 2 * RIM, 1))


def pack_kernel(place_ref, path_ref, tilt_ref, out_ref, tilt_out, held, edge, load_sem, tilt_sem):
    planes, rows, cols = path_ref.shape
    half = rows // 2
    ring = half + TILE
    near = (ring // TILE + 1) // 2 * TILE
    blocks = cols // LANES
    place = place_ref[0]
    loads = [pltpu.make_async_copy(path_ref.at[p], held.at[p], load_sem.at[p]) for p in range(planes)]
    rest = []
    start = pl.multiple_of((place // blocks) * half, half)
    next_to = pl.multiple_of(half - TILE * (place // blocks), TILE)
    for at, shift in enumerate((blocks - 1, 0, 1)):
        cut = pl.ds(pl.multiple_of(((place + shift) % blocks) * LANES, LANES), LANES)
        core = tilt_out.at[at, :, pl.ds(0, half)]
        rim = tilt_out.at[at, :, pl.ds(half, TILE)]
        rest.append(pltpu.make_async_copy(tilt_ref.at[:, pl.ds(start, half), cut], core, tilt_sem.at[2 * at]))
        rest.append(pltpu.make_async_copy(tilt_ref.at[:, pl.ds(next_to, TILE), cut], rim, tilt_sem.at[2 * at + 1]))
    for copy in loads + rest:
        copy.start()
    for p in range(planes):
        loads[p].wait()
        for c in range(blocks):
            cut = slice(c * LANES, (c + 1) * LANES)
            tile = held[p, :, cut]
            edge[c] = edges(tile, p, jnp.zeros_like(tile) if p == 0 else edge[c])
            for r in range(2):
                out_ref[r * blocks + c, ring * p : ring * p + half] = tile[r * half : (r + 1) * half]
                own = half - TILE * r
                out_ref[r * blocks + c, ring * p + half : ring * (p + 1)] = tile[own : own + TILE]
    for c in range(blocks):
        columns = outer(edge[(c - 1) % blocks], edge[(c + 1) % blocks])
        for r in range(2):
            part = columns[r * half : (r + 1) * half]
            at = ring * planes
            far = half - near
            out_ref[r * blocks + c, at : at + far] = beside(part[:far], part[near:])
            out_ref[r * blocks + c, at + far : at + near] = part[far:near]
    for copy in rest:
        copy.wait()


def pack(place, path, tilt):
    planes, rows, cols = path.shape
    count, half = 2 * cols // LANES, rows // 2
    ring = half + TILE
    near = (ring // TILE + 1) // 2 * TILE
    return pl.pallas_call(
        pack_kernel,
        out_shape=[
            pltpu.VMEM((count, ring * planes + near, LANES), jnp.float32),
            pltpu.VMEM((3, planes, ring, LANES), jnp.float32),
        ],
        in_specs=[smem] + [anywhere] * 2,
        out_specs=[vmem] * 2,
        scratch_shapes=[
            pltpu.VMEM((planes, rows, cols), jnp.float32),
            pltpu.VMEM((count // 2, rows, LANES), jnp.float32),
            pltpu.SemaphoreType.DMA((planes,)),
            pltpu.SemaphoreType.DMA((6,)),
        ],
        compiler_params=pltpu.CompilerParams(vmem_limit_bytes=14 * MIB),
        cost_estimate=pl.CostEstimate(flops=10_000_000, bytes_accessed=16 * MIB, transcendentals=0),
        name="pack",
    )(place, path, tilt)


def rim_kernel(path_ref, tilt_ref, first_ref, last_ref, held, sem):
    rows = path_ref.shape[1]
    copies = []
    for k, ref in enumerate((path_ref, tilt_ref)):
        for at, start in enumerate((0, rows - TILE)):
            copies.append(pltpu.make_async_copy(ref.at[:, pl.ds(start, TILE)], held.at[k, at], sem.at[2 * k + at]))
    for copy in copies:
        copy.start()
    for copy in copies:
        copy.wait()
    for p in range(path_ref.shape[0]):
        upper = row_of(held.shape[3:]) < RIM
        first_ref[p] = jnp.where(upper, held[0, 0, p], pltpu.roll(held[1, 0, p], RIM, 0))
        last_ref[p] = jnp.where(upper, pltpu.roll(held[0, 1, p], RIM, 0), held[1, 1, p])


def rim_rows(path, tilt):
    planes, rows, cols = path.shape
    return pl.pallas_call(
        rim_kernel,
        out_shape=[jax.ShapeDtypeStruct((planes, TILE, cols), jnp.float32)] * 2,
        in_specs=[anywhere] * 2,
        out_specs=[vmem] * 2,
        scratch_shapes=[pltpu.VMEM((2, 2, planes, TILE, cols), jnp.float32), pltpu.SemaphoreType.DMA((4,))],
        compiler_params=pltpu.CompilerParams(vmem_limit_bytes=4 * MIB),
        name="rim_rows",
    )(path, tilt)


def rims_kernel(place_ref, above_ref, below_ref, tilt_ref, packed_ref, out_ref, tilt_out, edge):
    planes, _, cols = above_ref.shape
    count = out_ref.shape[0]
    ring = tilt_out.shape[1]
    half = ring - TILE
    near = out_ref.shape[1] - ring * planes
    blocks = count // 2
    place = place_ref[0]
    upper = place < blocks
    under = row_of((TILE, LANES)) < RIM
    for r in range(2):
        for c in range(blocks):
            k = r * blocks + c
            cut = slice(c * LANES, (c + 1) * LANES)
            total = jnp.zeros((TILE, LANES), jnp.float32)
            for p in range(planes):
                at = slice(ring * p + half, ring * (p + 1))
                own = packed_ref[k, at]
                if r == 0:
                    tile = jnp.where(under, own, pltpu.roll(above_ref[p, :, cut], RIM, 0))
                else:
                    tile = jnp.where(under, below_ref[p, :, cut], own)
                out_ref[k, at] = tile
                total = edges(tile, p, total)
            edge[c] = total
        for c in range(blocks):
            columns = outer(edge[(c - 1) % blocks], edge[(c + 1) % blocks])
            at = ring * planes + half - near
            place_at = slice(at, at + TILE)
            out_ref[r * blocks + c, place_at] = beside(packed_ref[r * blocks + c, place_at], columns)
    sums = []
    for at, shift in enumerate((blocks - 1, 0, 1)):
        cut = pl.ds(pl.multiple_of(((place + shift) % blocks) * LANES, LANES), LANES)
        total = jnp.zeros((half + TILE, LANES), jnp.float32)
        for p in range(planes):
            own = tilt_ref[at, p, half:]
            next_to = jnp.where(upper, own, pltpu.roll(below_ref[p, :, cut], RIM, 0))
            last = jnp.where(upper, above_ref[p, :, cut], own)
            full = jnp.concatenate([tilt_ref[at, p, :half], jnp.where(under, next_to, last)], axis=0)
            if at == 1:
                tilt_out[p] = full
            total = edges(full, p, total)
        sums.append(total)
    tilt_out[planes] = strip_of(*sums)


def rims(place, above, below, tilt, packed):
    planes, _, cols = above.shape
    return pl.pallas_call(
        rims_kernel,
        out_shape=[
            pltpu.VMEM(packed.shape, jnp.float32),
            pltpu.VMEM((planes + 1, tilt.shape[2], LANES), jnp.float32),
        ],
        in_specs=[smem] + [vmem] * 4,
        out_specs=[vmem] * 2,
        input_output_aliases={4: 0},
        scratch_shapes=[pltpu.VMEM((cols // LANES, TILE, LANES), jnp.float32)],
        compiler_params=pltpu.CompilerParams(vmem_limit_bytes=12 * MIB),
        cost_estimate=pl.CostEstimate(flops=1_000_000, bytes_accessed=4 * MIB, transcendentals=0),
        name="rims",
    )(place, above, below, tilt, packed)


def rows_sum(x):
    return pltpu.roll(x, 1, 0) + pltpu.roll(x, x.shape[0] - 1, 0)


def neighbours_strip(s):
    total = pltpu.roll(s, GROUP, 1) + pltpu.roll(s, LANES - GROUP, 1)
    total = total + pltpu.roll(s, 2, 1) + pltpu.roll(s, LANES - 2, 1)
    return total + rows_sum(s)


def split(x):
    high = x.astype(jnp.bfloat16)
    rest = x - high.astype(jnp.float32)
    middle = rest.astype(jnp.bfloat16)
    low = (rest - middle.astype(jnp.float32)).astype(jnp.bfloat16)
    return jnp.concatenate([high, middle, low], axis=1)


def write_band(band):
    shape = (band.shape[0], LANES)
    row = row_of(shape) % LANES
    lane = lane_of(shape)
    apart = row - lane
    band[:, :LANES] = jnp.where((apart == 1) | (apart == -1), 1.0, 0.0).astype(jnp.bfloat16)
    k = lane % GROUP
    right = jnp.where(k > 2 * RIM, k - 13, k + 3) // 2 + LANES - RIM
    column = jnp.where(k % 2 == 0, k // 2 - RIM, right)
    band[:, LANES:] = jnp.where((row == column) & (own_plane(shape) >= 0), 1.0, 0.0).astype(jnp.bfloat16)


def neighbours_given(x, below, above, strip, p, within):
    lane = lane_of(x.shape)
    rim = pltpu.roll(strip, (LANES - GROUP * p - 6) % LANES, 1)
    rim = jnp.where((lane == 0) | (lane == LANES - 1), rim, 0.0)
    return (below + above) + rows_sum(x) + (within + rim)


def neighbours_plane(x, below, above, strip, p):
    lane = lane_of(x.shape)
    beside = pltpu.roll(strip, (LANES - GROUP * p - 6) % LANES, 1)
    left = jnp.where(lane == 0, beside, pltpu.roll(x, 1, 1))
    right = jnp.where(lane == LANES - 1, beside, pltpu.roll(x, LANES - 1, 1))
    return (below + above) + rows_sum(x) + (left + right)


def potential(field, sides, tilt_ref, mu):
    planes = mu.shape[0] - 1
    strip = field(planes)
    mu[planes] = strip * (strip * strip + 5.0) - (neighbours_strip(strip) + tilt_ref[planes])
    for p in range(planes):
        x = field(p)
        below, above = field((p - 1) % planes), field((p + 1) % planes)
        if sides is None:
            around = neighbours_plane(x, below, above, strip, p)
        else:
            around = neighbours_given(x, below, above, strip, p, sides(p))
        mu[p] = x * (x * x + 5.0) - (around + tilt_ref[p])


def force_plane(mu, p):
    planes = mu.shape[0] - 1
    return neighbours_plane(mu[p], mu[(p - 1) % planes], mu[(p + 1) % planes], mu[planes], p) - 6.0 * mu[p]


def fold(x):
    total = x[:TILE]
    for at in range(TILE, x.shape[0], TILE):
        total = total + x[at : at + TILE]
    return total


def write_sums(acc, out_ref):
    kinds, images = acc.shape[:2]
    row = jnp.zeros((1, LANES), jnp.float32)
    lane = lane_of((images, LANES))
    image = row_of((images, LANES))
    for q in range(kinds):
        part = jnp.sum(acc[q], axis=1)
        part = jnp.sum(part, axis=1, keepdims=True)
        row = row + jnp.sum(jnp.where(lane == images * q + image, part, 0.0), axis=0, keepdims=True)
    out_ref[...] = jnp.broadcast_to(row[None], out_ref.shape)


def read_sums(sums_ref):
    parts = [sums_ref[k] for k in range(TILE)]
    for k in range(TILE, sums_ref.shape[0]):
        parts[k % TILE] = parts[k % TILE] + sums_ref[k]
    while len(parts) > 1:
        parts = [a + b for a, b in zip(parts[::2], parts[1::2], strict=True)]
    return parts[0]


def spread(row, images):
    shape = (images, LANES)
    picked = jnp.where(lane_of(shape) == row_of(shape), row, 0.0)
    return jnp.broadcast_to(jnp.sum(picked, axis=1, keepdims=True), shape)


def tangent_share(row, images):
    lane = lane_of(row.shape)
    coef = row / (pltpu.roll(row, LANES - images, 1) + EPS)
    return jnp.where((lane > 0) & (lane < images - 1), coef, 0.0)


def first_kernel(phi_ref, tilt_ref, moved_ref, strip_ref, sums_ref, mu, acc, band, sides, strips):
    images, parts, rows, lanes = moved_ref.shape
    planes = parts - 1
    core = rows - TILE
    near = phi_ref.shape[1] - rows * planes
    write_band(band)
    owner = own_plane((rows, lanes))

    def plane(i, p):
        return phi_ref[i, rows * p : rows * (p + 1)]

    def prepare(i, slot):
        sides[slot] = jnp.dot(split(phi_ref[i, : rows * planes]), band[...], preferred_element_type=jnp.float32)
        columns = phi_ref[i, rows * planes :]
        far = pltpu.roll(columns[: rows - near], lanes - 2 * RIM, 1)
        strip = jnp.concatenate([columns, far], axis=0)
        for p in range(planes):
            strip = jnp.where(owner == p, sides[slot, rows * p : rows * (p + 1), lanes:], strip)
        strips[slot] = strip
        strip_ref[i] = strip

    def step(i, slot):
        after = jnp.minimum(i + 1, images - 1)
        before = jnp.maximum(i - 1, 0)

        def field(p):
            return strips[slot] if p == planes else plane(i, p)

        potential(field, lambda p: sides[slot, rows * p : rows * (p + 1), :lanes], tilt_ref, mu.at[slot])
        moved_ref[i, planes] = field(planes) + DT * (neighbours_strip(mu[slot, planes]) - 6.0 * mu[slot, planes])
        product = jnp.zeros((TILE, lanes), jnp.float32)
        square = jnp.zeros((TILE, lanes), jnp.float32)
        for p in range(planes):
            force = force_plane(mu.at[slot], p)
            moved_ref[i, p] = field(p) + DT * force
            at = slice(rows * p, rows * p + core)
            diff = phi_ref[after, at] - phi_ref[before, at]
            product = product + fold(force[:core] * diff)
            square = square + fold(diff * diff)
        acc[0, i] = product
        acc[1, i] = square

    slots = mu.shape[0]

    def body(t, carry):
        for slot in range(slots):
            prepare(jnp.minimum(slots * t + slot + 1, images - 1), (slot + 1) % slots)
            step(slots * t + slot, slot)
        return carry

    prepare(0, 0)
    lax.fori_loop(0, images // slots, body, 0)
    write_sums(acc, sums_ref)


def first_step(phi, tilt, devices):
    images = phi.shape[0]
    parts, rows, lanes = tilt.shape
    return pl.pallas_call(
        first_kernel,
        out_shape=[
            jax.ShapeDtypeStruct((images, parts, rows, lanes), jnp.float32),
            jax.ShapeDtypeStruct((images, rows, lanes), jnp.float32),
            jax.ShapeDtypeStruct((devices, 1, LANES), jnp.float32),
        ],
        in_specs=[vmem] * 2,
        out_specs=[vmem] * 3,
        scratch_shapes=[
            pltpu.VMEM((SLOTS, parts, rows, lanes), jnp.float32),
            pltpu.VMEM((2, images, TILE, lanes), jnp.float32),
            pltpu.VMEM((3 * LANES, 2 * LANES), jnp.bfloat16),
            pltpu.VMEM((SLOTS, (parts - 1) * rows, 2 * LANES), jnp.float32),
            pltpu.VMEM((SLOTS, rows, lanes), jnp.float32),
        ],
        compiler_params=pltpu.CompilerParams(vmem_limit_bytes=20 * MIB),
        name="first_step",
    )(phi, tilt)


def second_kernel(given_ref, phi_ref, strip_ref, moved_ref, tilt_ref, one_ref, two_ref, coef_ref, sums_ref, mu, acc, coefs):
    images, parts, rows, lanes = moved_ref.shape
    planes = parts - 1
    core = rows - TILE
    coef_row = tangent_share(read_sums(given_ref), images)
    coef_ref[...] = coef_row
    coefs[...] = spread(coef_row, images)

    def update(i):
        after = jnp.minimum(i + 1, images - 1)
        before = jnp.maximum(i - 1, 0)
        scale = DT * coefs[pl.ds(i, 1)]
        for p in range(planes):
            at = slice(rows * p, rows * (p + 1))
            one_ref[i, p] = moved_ref[i, p] - scale * (phi_ref[after, at] - phi_ref[before, at])
        one_ref[i, planes] = moved_ref[i, planes] - scale * (strip_ref[after] - strip_ref[before])

    update(0)

    def body(i, carry):
        after = jnp.minimum(i + 1, images - 1)
        before = jnp.maximum(i - 1, 0)
        earlier = jnp.maximum(i - 2, 0)
        update(after)
        potential(lambda p: one_ref[i, p], None, tilt_ref, mu)
        coef = coefs[pl.ds(i, 1)]
        sums = [jnp.zeros((TILE, lanes), jnp.float32)] * 6
        for p in range(planes):
            force = force_plane(mu, p)[:core]
            x = one_ref[i, p, :core]
            diff = one_ref[after, p, :core] - one_ref[before, p, :core]
            diff_before = x - one_ref[earlier, p, :core]
            two = x + DT * (force - coef * diff)
            two_ref[i, p] = two
            gap = two - two_ref[before, p]
            terms = (force * diff, diff * diff, gap * gap, gap * diff, gap * diff_before, diff * diff_before)
            sums = [total + fold(term) for total, term in zip(sums, terms, strict=True)]
        for q in range(6):
            acc[q, i] = sums[q]
        return carry

    lax.fori_loop(0, images, body, 0, unroll=4)
    write_sums(acc, sums_ref)


def second_step(given, phi, strips, moved, tilt):
    images, parts, rows, lanes = moved.shape
    return pl.pallas_call(
        second_kernel,
        out_shape=[
            jax.ShapeDtypeStruct(moved.shape, jnp.float32),
            jax.ShapeDtypeStruct((images, parts - 1, rows - TILE, lanes), jnp.float32),
            jax.ShapeDtypeStruct((1, LANES), jnp.float32),
            jax.ShapeDtypeStruct(given.shape, jnp.float32),
        ],
        in_specs=[vmem] * 5,
        out_specs=[vmem] * 4,
        scratch_shapes=[
            pltpu.VMEM((parts, rows, lanes), jnp.float32),
            pltpu.VMEM((6, images, TILE, lanes), jnp.float32),
            pltpu.VMEM((images, lanes), jnp.float32),
        ],
        compiler_params=pltpu.CompilerParams(vmem_limit_bytes=26 * MIB),
        name="second_step",
    )(given, phi, strips, moved, tilt)


def spacing(row, coef, images):
    def quantity(q):
        return pltpu.roll(row, (LANES - images * q) % LANES, 1)

    lane = lane_of(row.shape)
    change = jnp.where((lane > 0) & (lane < images - 1), tangent_share(row, images) - coef, 0.0)
    squares, gaps, gap_diff, gap_before, diff_before = (quantity(q) for q in range(1, 6))
    change_before = pltpu.roll(change, 1, 1)
    squares_before = pltpu.roll(squares, 1, 1)
    cross = change * gap_diff - change_before * gap_before
    tangent = change * change * squares + change_before * change_before * squares_before
    tangent = tangent - 2.0 * change * change_before * diff_before
    length = jnp.maximum(gaps - 2.0 * DT * cross + DT * DT * tangent, 0.0)
    dist = jnp.where((lane > 0) & (lane < images), jnp.sqrt(length + EPS), 0.0)

    shape = (images, LANES)
    slot = lane_of(shape)
    image = row_of(shape)
    arc = jnp.sum(jnp.where(image <= slot, spread(dist, images), 0.0), axis=0, keepdims=True)
    total = jnp.sum(dist, axis=1, keepdims=True)
    target = image.astype(jnp.float32) * (total / (images - 1))
    inside = (slot >= 1) & (slot <= images - 2) & (arc <= target)
    lower = jnp.sum(jnp.where(inside, 1.0, 0.0), axis=1, keepdims=True)
    where = slot.astype(jnp.float32)
    start = jnp.sum(jnp.where(where == lower, arc, 0.0), axis=1, keepdims=True)
    step = jnp.sum(jnp.where(where == lower + 1.0, dist, 0.0), axis=1, keepdims=True)
    return change, lower, (target - start) / step


def mix_kernel(given_ref, coef_ref, one_ref, two_ref, out_ref, final, changes, shares):
    images, planes, core, lanes = two_ref.shape
    change, lower, share = spacing(read_sums(given_ref), coef_ref[...], images)
    changes[...] = spread(change, images)
    shares[...] = share
    image = row_of(lower.shape)
    lowers = [jnp.sum(jnp.where(image == j, lower, 0.0)).astype(jnp.int32) for j in range(images)]

    def finish(i, carry):
        after = jnp.minimum(i + 1, images - 1)
        before = jnp.maximum(i - 1, 0)
        scale = DT * changes[pl.ds(i, 1)]
        for p in range(planes):
            final[i, p] = two_ref[i, p] - scale * (one_ref[after, p, :core] - one_ref[before, p, :core])
        return carry

    lax.fori_loop(0, images, finish, 0)
    for j in range(images):
        portion = shares[j : j + 1]
        for p in range(planes):
            out_ref[j, p] = (1.0 - portion) * final[lowers[j], p] + portion * final[lowers[j] + 1, p]


def mix(given, coef, one, two):
    images, planes, core, lanes = two.shape
    return pl.pallas_call(
        mix_kernel,
        out_shape=jax.ShapeDtypeStruct(two.shape, jnp.float32),
        in_specs=[vmem] * 4,
        out_specs=vmem,
        scratch_shapes=[
            pltpu.VMEM(two.shape, jnp.float32),
            pltpu.VMEM((images, lanes), jnp.float32),
            pltpu.VMEM((images, lanes), jnp.float32),
        ],
        compiler_params=pltpu.CompilerParams(vmem_limit_bytes=20 * MIB),
        name="mix",
    )(given, coef, one, two)


def place_kernel(blocks_ref, out_ref, sem):
    count, planes, half, lanes = blocks_ref.shape
    copies = []
    for k in range(count):
        r, c = divmod(k, count // 2)
        piece = out_ref.at[0, :, pl.ds(r * half, half), pl.ds(c * lanes, lanes)]
        copies.append(pltpu.make_async_copy(blocks_ref.at[k], piece, sem.at[k]))
    for copy in copies:
        copy.start()
    for copy in copies:
        copy.wait()


def put_in_place(blocks):
    count, planes, half, lanes = blocks.shape
    return pl.pallas_call(
        place_kernel,
        out_shape=jax.ShapeDtypeStruct((1, planes, 2 * half, count // 2 * lanes), jnp.float32),
        in_specs=[anywhere],
        out_specs=anywhere,
        scratch_shapes=[pltpu.SemaphoreType.DMA((count,))],
        compiler_params=pltpu.CompilerParams(vmem_limit_bytes=MIB),
        name="put_in_place",
    )(blocks)


def exchange(block, axes):
    return lax.all_to_all(block, axes, split_axis=0, concat_axis=0, tiled=True)


def per_device(axes, path, tilt):
    devices = lax.axis_size(axes)
    place = lax.axis_index("img").astype(jnp.int32)[None]
    own = pltpu.with_memory_space_constraint(path[0], pltpu.HBM)
    tilt = pltpu.with_memory_space_constraint(tilt, pltpu.HBM)
    first, last = rim_rows(own, tilt)
    count = lax.axis_size("space")
    ahead = [(i, (i + 1) % count) for i in range(count)]
    above = lax.ppermute(last, "space", ahead)
    below = lax.ppermute(first, "space", [(target, source) for source, target in ahead])
    packed, tilt_near = pack(place, own, tilt)
    packed, tilt_block = rims(place, above, below, tilt_near, packed)
    packed, tilt_block = lax.optimization_barrier((packed, tilt_block))
    phi = exchange(packed, "img")
    moved, strips, sums = first_step(phi, tilt_block, devices)
    one, two, coef, sums = second_step(exchange(sums, axes), phi, strips, moved, tilt_block)
    mixed = mix(exchange(sums, axes), coef, one, two)
    return put_in_place(exchange(mixed, "img"))


def solution(mesh):
    return jax.shard_map(
        functools.partial(per_device, tuple(mesh.axis_names)),
        mesh=mesh,
        in_specs=(P("img", None, "space", None), P(None, "space", None)),
        out_specs=P("img", None, "space", None),
        check_vma=False,
    )
```

```python
import functools

import jax
import jax.numpy as jnp
from jax import lax
from jax.experimental import pallas as pl
from jax.experimental.pallas import tpu as pltpu
from jax.sharding import PartitionSpec as P

DT = 0.006
EPS = 1e-06
RIM = 4
TILE = 8
LANES = 128
GROUP = 16
MIB = 1024 * 1024
SLOTS = 4

vmem = pl.BlockSpec(memory_space=pltpu.VMEM)
smem = pl.BlockSpec(memory_space=pltpu.SMEM)
anywhere = pl.BlockSpec(memory_space=pl.ANY)


def lane_of(shape):
    return lax.broadcasted_iota(jnp.int32, shape, len(shape) - 1)


def row_of(shape):
    return lax.broadcasted_iota(jnp.int32, shape, len(shape) - 2)


def edges(tile, p, total):
    place = lane_of(tile.shape) - GROUP * p
    moved = pltpu.roll(tile, GROUP * p + RIM, 1)
    return jnp.where((place >= 0) & (place < 2 * RIM), moved, total)


def strip_of(before, own, after):
    lane = lane_of(own.shape)
    k = lane % GROUP
    left = jnp.where(k < RIM, before, own)
    right = jnp.where(k < RIM, own, after)
    both = jnp.where(k < 2 * RIM, left, pltpu.roll(right, 2 * RIM, 1))
    group = lane - k
    odd = jnp.where(k < 13, group + 8 + (k + 3) // 2, (group + GROUP) % LANES + 8 + (k - 13) // 2)
    source = jnp.where(k % 2 == 0, group + k // 2, odd)
    return jnp.take_along_axis(both, source, axis=1, mode="promise_in_bounds")


def own_plane(shape):
    lane = lane_of(shape)
    k = lane % GROUP
    group = lane // GROUP
    even = (k % 2 == 0) & (k >= 2 * RIM)
    here = even | (k == 1) | (k == 3)
    there = (k == 13) | (k == 15)
    return jnp.where(here, group, jnp.where(there, (group + 1) % (LANES // GROUP), -1))


def outer(before, after):
    lane = lane_of(before.shape)
    k = lane % GROUP
    both = jnp.where(k < RIM, before, after)
    source = lane - k + jnp.where(k % 2 == 0, k // 2, (k + 3) // 2) % (2 * RIM)
    return jnp.take_along_axis(both, source, axis=1, mode="promise_in_bounds")


def beside(first, second):
    return jnp.where(own_plane(first.shape) < 0, first, pltpu.roll(second, 2 * RIM, 1))


def pack_kernel(place_ref, path_ref, tilt_ref, out_ref, tilt_out, rim_out, held, near_tilt, edge, load_sem, tilt_sem):
    planes, rows, cols = path_ref.shape
    half = rows // 2
    ring = half + TILE
    near = (ring // TILE + 1) // 2 * TILE
    blocks = cols // LANES
    place = place_ref[0]
    loads = [pltpu.make_async_copy(path_ref.at[p], held.at[p], load_sem.at[p]) for p in range(planes)]
    rest = []
    start = pl.multiple_of((place // blocks) * half, half)
    next_to = pl.multiple_of(half - TILE * (place // blocks), TILE)
    for at, shift in enumerate((blocks - 1, 0, 1)):
        cut = pl.ds(pl.multiple_of(((place + shift) % blocks) * LANES, LANES), LANES)
        core = near_tilt.at[at, :, pl.ds(0, half)]
        rim = near_tilt.at[at, :, pl.ds(half, TILE)]
        rest.append(pltpu.make_async_copy(tilt_ref.at[:, pl.ds(start, half), cut], core, tilt_sem.at[2 * at]))
        rest.append(pltpu.make_async_copy(tilt_ref.at[:, pl.ds(next_to, TILE), cut], rim, tilt_sem.at[2 * at + 1]))
    for copy in loads + rest:
        copy.start()
    for p in range(planes):
        loads[p].wait()
        for c in range(blocks):
            cut = slice(c * LANES, (c + 1) * LANES)
            tile = held[p, :, cut]
            edge[c] = edges(tile, p, jnp.zeros_like(tile) if p == 0 else edge[c])
            for r in range(2):
                out_ref[r * blocks + c, ring * p : ring * p + half] = tile[r * half : (r + 1) * half]
                own = half - TILE * r
                out_ref[r * blocks + c, ring * p + half : ring * (p + 1)] = tile[own : own + TILE]
    for c in range(blocks):
        columns = outer(edge[(c - 1) % blocks], edge[(c + 1) % blocks])
        for r in range(2):
            part = columns[r * half : (r + 1) * half]
            at = ring * planes
            far = half - near
            out_ref[r * blocks + c, at : at + far] = beside(part[:far], part[near:])
            out_ref[r * blocks + c, at + far : at + near] = part[far:near]
    for copy in rest:
        copy.wait()
    sums = []
    for at in range(3):
        rim_out[at] = near_tilt[at, :, half:]
        total = jnp.zeros((half, LANES), jnp.float32)
        for p in range(planes):
            total = edges(near_tilt[at, p, :half], p, total)
        sums.append(total)
    tilt_out[:planes] = near_tilt[1]
    tilt_out[planes, :half] = strip_of(*sums)


def pack(place, path, tilt):
    planes, rows, cols = path.shape
    count, half = 2 * cols // LANES, rows // 2
    ring = half + TILE
    near = (ring // TILE + 1) // 2 * TILE
    return pl.pallas_call(
        pack_kernel,
        out_shape=[
            pltpu.VMEM((count, ring * planes + near, LANES), jnp.float32),
            pltpu.VMEM((planes + 1, ring, LANES), jnp.float32),
            pltpu.VMEM((3, planes, TILE, LANES), jnp.float32),
        ],
        in_specs=[smem] + [anywhere] * 2,
        out_specs=[vmem] * 3,
        scratch_shapes=[
            pltpu.VMEM((planes, rows, cols), jnp.float32),
            pltpu.VMEM((3, planes, ring, LANES), jnp.float32),
            pltpu.VMEM((count // 2, rows, LANES), jnp.float32),
            pltpu.SemaphoreType.DMA((planes,)),
            pltpu.SemaphoreType.DMA((6,)),
        ],
        compiler_params=pltpu.CompilerParams(vmem_limit_bytes=14 * MIB),
        cost_estimate=pl.CostEstimate(flops=10_000_000, bytes_accessed=16 * MIB, transcendentals=0),
        name="pack",
    )(place, path, tilt)


def rim_kernel(place_ref, path_ref, tilt_ref, first_ref, last_ref, side_ref, held, near, sem, near_sem):
    planes, rows, cols = path_ref.shape
    blocks = cols // LANES
    place = place_ref[0]
    upper = place < blocks
    start = pl.multiple_of((1 - place // blocks) * (rows - TILE), TILE)
    copies = []
    for at, row in enumerate((0, rows - TILE)):
        copies.append(pltpu.make_async_copy(path_ref.at[:, pl.ds(row, TILE)], held.at[at], sem.at[at]))
    for at, shift in enumerate((blocks - 1, 0, 1)):
        cut = pl.ds(pl.multiple_of(((place + shift) % blocks) * LANES, LANES), LANES)
        copies.append(pltpu.make_async_copy(tilt_ref.at[:, pl.ds(start, TILE), cut], near.at[at], near_sem.at[at]))
    for copy in copies:
        copy.start()
    for copy in copies:
        copy.wait()
    under = row_of((TILE, cols // 2)) < RIM
    for p in range(planes):
        left, right = slice(0, cols // 2), slice(cols // 2, cols)
        first_ref[p] = jnp.where(under, held[0, p, :, left], pltpu.roll(held[0, p, :, right], RIM, 0))
        last_ref[p] = jnp.where(under, pltpu.roll(held[1, p, :, left], RIM, 0), held[1, p, :, right])
        tiles = [jnp.where(upper, pltpu.roll(near[at, p], RIM, 0), near[at, p]) for at in range(3)]
        side_ref[p, :, :LANES] = jnp.where(under[:, :LANES], tiles[0], pltpu.roll(tiles[1], RIM, 0))
        side_ref[p, :, LANES:] = tiles[2]


def rim_rows(place, path, tilt):
    planes, rows, cols = path.shape
    half = jax.ShapeDtypeStruct((planes, TILE, cols // 2), jnp.float32)
    return pl.pallas_call(
        rim_kernel,
        out_shape=[half, half, jax.ShapeDtypeStruct((planes, TILE, 2 * LANES), jnp.float32)],
        in_specs=[smem] + [anywhere] * 2,
        out_specs=[vmem] * 3,
        scratch_shapes=[
            pltpu.VMEM((2, planes, TILE, cols), jnp.float32),
            pltpu.VMEM((3, planes, TILE, LANES), jnp.float32),
            pltpu.SemaphoreType.DMA((2,)),
            pltpu.SemaphoreType.DMA((3,)),
        ],
        compiler_params=pltpu.CompilerParams(vmem_limit_bytes=4 * MIB),
        name="rim_rows",
    )(place, path, tilt)


def rims_kernel(
    place_ref, above_ref, below_ref, side_ref, tilt_rim, tilt_ref, packed_ref, out_ref, tilt_out, edge
):
    planes, _, width = above_ref.shape
    count = out_ref.shape[0]
    ring = tilt_out.shape[1]
    half = ring - TILE
    near = out_ref.shape[1] - ring * planes
    blocks = count // 2
    upper = place_ref[0] < blocks
    under = row_of((TILE, LANES)) < RIM
    for r in range(2):
        for c in range(blocks):
            k = r * blocks + c
            turned = c * LANES // width
            cut = slice(c * LANES - turned * width, (c + 1) * LANES - turned * width)
            total = jnp.zeros((TILE, LANES), jnp.float32)
            for p in range(planes):
                at = slice(ring * p + half, ring * (p + 1))
                own = packed_ref[k, at]
                other = above_ref[p, :, cut] if r == 0 else below_ref[p, :, cut]
                if turned != 1 - r:
                    other = pltpu.roll(other, RIM, 0)
                tile = jnp.where(under, own, other) if r == 0 else jnp.where(under, other, own)
                out_ref[k, at] = tile
                total = edges(tile, p, total)
            edge[c] = total
        for c in range(blocks):
            columns = outer(edge[(c - 1) % blocks], edge[(c + 1) % blocks])
            at = ring * planes + half - near
            place_at = slice(at, at + TILE)
            out_ref[r * blocks + c, place_at] = beside(packed_ref[r * blocks + c, place_at], columns)
    sums = []
    for at in range(3):
        total = jnp.zeros((TILE, LANES), jnp.float32)
        for p in range(planes):
            own = tilt_rim[at, p]
            other = side_ref[p, :, LANES:] if at == 2 else side_ref[p, :, :LANES]
            turned = pltpu.roll(other, RIM, 0)
            if at == 1:
                other, turned = turned, other
            rim = jnp.where(upper, jnp.where(under, own, turned), jnp.where(under, other, own))
            if at == 1:
                tilt_out[p, half:] = rim
            total = edges(rim, p, total)
        sums.append(total)
    tilt_out[planes, half:] = strip_of(*sums)


def rims(place, above, below, side, tilt_rim, tilt, packed):
    return pl.pallas_call(
        rims_kernel,
        out_shape=[pltpu.VMEM(packed.shape, jnp.float32), pltpu.VMEM(tilt.shape, jnp.float32)],
        in_specs=[smem] + [vmem] * 6,
        out_specs=[vmem] * 2,
        input_output_aliases={6: 0, 5: 1},
        scratch_shapes=[pltpu.VMEM((packed.shape[0] // 2, TILE, LANES), jnp.float32)],
        compiler_params=pltpu.CompilerParams(vmem_limit_bytes=12 * MIB),
        cost_estimate=pl.CostEstimate(flops=1_000_000, bytes_accessed=4 * MIB, transcendentals=0),
        name="rims",
    )(place, above, below, side, tilt_rim, tilt, packed)


def rows_sum(x):
    return pltpu.roll(x, 1, 0) + pltpu.roll(x, x.shape[0] - 1, 0)


def neighbours_strip(s):
    total = pltpu.roll(s, GROUP, 1) + pltpu.roll(s, LANES - GROUP, 1)
    total = total + pltpu.roll(s, 2, 1) + pltpu.roll(s, LANES - 2, 1)
    return total + rows_sum(s)


def split(x):
    high = x.astype(jnp.bfloat16)
    rest = x - high.astype(jnp.float32)
    middle = rest.astype(jnp.bfloat16)
    low = (rest - middle.astype(jnp.float32)).astype(jnp.bfloat16)
    return jnp.concatenate([high, middle, low], axis=1)


def write_band(band):
    shape = (band.shape[0], LANES)
    row = row_of(shape) % LANES
    lane = lane_of(shape)
    apart = row - lane
    band[:, :LANES] = jnp.where((apart == 1) | (apart == -1), 1.0, 0.0).astype(jnp.bfloat16)
    k = lane % GROUP
    right = jnp.where(k > 2 * RIM, k - 13, k + 3) // 2 + LANES - RIM
    column = jnp.where(k % 2 == 0, k // 2 - RIM, right)
    band[:, LANES:] = jnp.where((row == column) & (own_plane(shape) >= 0), 1.0, 0.0).astype(jnp.bfloat16)


def neighbours_given(x, below, above, strip, p, within):
    lane = lane_of(x.shape)
    rim = pltpu.roll(strip, (LANES - GROUP * p - 6) % LANES, 1)
    rim = jnp.where((lane == 0) | (lane == LANES - 1), rim, 0.0)
    return (below + above) + rows_sum(x) + (within + rim)


def neighbours_plane(x, below, above, strip, p):
    lane = lane_of(x.shape)
    beside = pltpu.roll(strip, (LANES - GROUP * p - 6) % LANES, 1)
    left = jnp.where(lane == 0, beside, pltpu.roll(x, 1, 1))
    right = jnp.where(lane == LANES - 1, beside, pltpu.roll(x, LANES - 1, 1))
    return (below + above) + rows_sum(x) + (left + right)


def potential(field, sides, tilt_ref, mu):
    planes = mu.shape[0] - 1
    strip = field(planes)
    mu[planes] = strip * (strip * strip + 5.0) - (neighbours_strip(strip) + tilt_ref[planes])
    for p in range(planes):
        x = field(p)
        below, above = field((p - 1) % planes), field((p + 1) % planes)
        if sides is None:
            around = neighbours_plane(x, below, above, strip, p)
        else:
            around = neighbours_given(x, below, above, strip, p, sides(p))
        mu[p] = x * (x * x + 5.0) - (around + tilt_ref[p])


def force_plane(mu, p):
    planes = mu.shape[0] - 1
    return neighbours_plane(mu[p], mu[(p - 1) % planes], mu[(p + 1) % planes], mu[planes], p) - 6.0 * mu[p]


def fold(x):
    total = x[:TILE]
    for at in range(TILE, x.shape[0], TILE):
        total = total + x[at : at + TILE]
    return total


def write_sums(acc, out_ref):
    kinds, images = acc.shape[:2]
    row = jnp.zeros((1, LANES), jnp.float32)
    lane = lane_of((images, LANES))
    image = row_of((images, LANES))
    for q in range(kinds):
        part = jnp.sum(acc[q], axis=1)
        part = jnp.sum(part, axis=1, keepdims=True)
        row = row + jnp.sum(jnp.where(lane == images * q + image, part, 0.0), axis=0, keepdims=True)
    out_ref[...] = jnp.broadcast_to(row[None], out_ref.shape)


def read_sums(sums_ref):
    parts = [sums_ref[k] for k in range(TILE)]
    for k in range(TILE, sums_ref.shape[0]):
        parts[k % TILE] = parts[k % TILE] + sums_ref[k]
    while len(parts) > 1:
        parts = [a + b for a, b in zip(parts[::2], parts[1::2], strict=True)]
    return parts[0]


def spread(row, images):
    shape = (images, LANES)
    picked = jnp.where(lane_of(shape) == row_of(shape), row, 0.0)
    return jnp.broadcast_to(jnp.sum(picked, axis=1, keepdims=True), shape)


def tangent_share(row, images):
    lane = lane_of(row.shape)
    coef = row / (pltpu.roll(row, LANES - images, 1) + EPS)
    return jnp.where((lane > 0) & (lane < images - 1), coef, 0.0)


def first_kernel(phi_ref, tilt_ref, moved_ref, strip_ref, sums_ref, mu, acc, band, sides, strips):
    images, parts, rows, lanes = moved_ref.shape
    planes = parts - 1
    core = rows - TILE
    near = phi_ref.shape[1] - rows * planes
    write_band(band)
    owner = own_plane((rows, lanes))

    def plane(i, p):
        return phi_ref[i, rows * p : rows * (p + 1)]

    def prepare(i, slot):
        sides[slot] = jnp.dot(split(phi_ref[i, : rows * planes]), band[...], preferred_element_type=jnp.float32)
        columns = phi_ref[i, rows * planes :]
        far = pltpu.roll(columns[: rows - near], lanes - 2 * RIM, 1)
        strip = jnp.concatenate([columns, far], axis=0)
        for p in range(planes):
            strip = jnp.where(owner == p, sides[slot, rows * p : rows * (p + 1), lanes:], strip)
        strips[slot] = strip
        strip_ref[i] = strip

    def step(i, slot):
        after = jnp.minimum(i + 1, images - 1)
        before = jnp.maximum(i - 1, 0)

        def field(p):
            return strips[slot] if p == planes else plane(i, p)

        potential(field, lambda p: sides[slot, rows * p : rows * (p + 1), :lanes], tilt_ref, mu.at[slot])
        moved_ref[i, planes] = field(planes) + DT * (neighbours_strip(mu[slot, planes]) - 6.0 * mu[slot, planes])
        product = jnp.zeros((TILE, lanes), jnp.float32)
        square = jnp.zeros((TILE, lanes), jnp.float32)
        for p in range(planes):
            force = force_plane(mu.at[slot], p)
            moved_ref[i, p] = field(p) + DT * force
            at = slice(rows * p, rows * p + core)
            diff = phi_ref[after, at] - phi_ref[before, at]
            product = product + fold(force[:core] * diff)
            square = square + fold(diff * diff)
        acc[0, i] = product
        acc[1, i] = square

    slots = mu.shape[0]

    def body(t, carry):
        for slot in range(slots):
            prepare(jnp.minimum(slots * t + slot + 1, images - 1), (slot + 1) % slots)
            step(slots * t + slot, slot)
        return carry

    prepare(0, 0)
    lax.fori_loop(0, images // slots, body, 0)
    write_sums(acc, sums_ref)


def first_step(phi, tilt, devices):
    images = phi.shape[0]
    parts, rows, lanes = tilt.shape
    return pl.pallas_call(
        first_kernel,
        out_shape=[
            jax.ShapeDtypeStruct((images, parts, rows, lanes), jnp.float32),
            jax.ShapeDtypeStruct((images, rows, lanes), jnp.float32),
            jax.ShapeDtypeStruct((devices, 1, LANES), jnp.float32),
        ],
        in_specs=[vmem] * 2,
        out_specs=[vmem] * 3,
        scratch_shapes=[
            pltpu.VMEM((SLOTS, parts, rows, lanes), jnp.float32),
            pltpu.VMEM((2, images, TILE, lanes), jnp.float32),
            pltpu.VMEM((3 * LANES, 2 * LANES), jnp.bfloat16),
            pltpu.VMEM((SLOTS, (parts - 1) * rows, 2 * LANES), jnp.float32),
            pltpu.VMEM((SLOTS, rows, lanes), jnp.float32),
        ],
        compiler_params=pltpu.CompilerParams(vmem_limit_bytes=20 * MIB),
        name="first_step",
    )(phi, tilt)


def second_kernel(given_ref, phi_ref, strip_ref, moved_ref, tilt_ref, one_ref, two_ref, coef_ref, sums_ref, mu, acc, coefs):
    images, parts, rows, lanes = moved_ref.shape
    planes = parts - 1
    core = rows - TILE
    coef_row = tangent_share(read_sums(given_ref), images)
    coef_ref[...] = coef_row
    coefs[...] = spread(coef_row, images)

    def update(i):
        after = jnp.minimum(i + 1, images - 1)
        before = jnp.maximum(i - 1, 0)
        scale = DT * coefs[pl.ds(i, 1)]
        for p in range(planes):
            at = slice(rows * p, rows * (p + 1))
            one_ref[i, p] = moved_ref[i, p] - scale * (phi_ref[after, at] - phi_ref[before, at])
        one_ref[i, planes] = moved_ref[i, planes] - scale * (strip_ref[after] - strip_ref[before])

    update(0)

    def body(i, carry):
        after = jnp.minimum(i + 1, images - 1)
        before = jnp.maximum(i - 1, 0)
        earlier = jnp.maximum(i - 2, 0)
        update(after)
        potential(lambda p: one_ref[i, p], None, tilt_ref, mu)
        coef = coefs[pl.ds(i, 1)]
        sums = [jnp.zeros((TILE, lanes), jnp.float32)] * 6
        for p in range(planes):
            force = force_plane(mu, p)[:core]
            x = one_ref[i, p, :core]
            diff = one_ref[after, p, :core] - one_ref[before, p, :core]
            diff_before = x - one_ref[earlier, p, :core]
            two = x + DT * (force - coef * diff)
            two_ref[i, p] = two
            gap = two - two_ref[before, p]
            terms = (force * diff, diff * diff, gap * gap, gap * diff, gap * diff_before, diff * diff_before)
            sums = [total + fold(term) for total, term in zip(sums, terms, strict=True)]
        for q in range(6):
            acc[q, i] = sums[q]
        return carry

    lax.fori_loop(0, images, body, 0, unroll=4)
    write_sums(acc, sums_ref)


def second_step(given, phi, strips, moved, tilt):
    images, parts, rows, lanes = moved.shape
    return pl.pallas_call(
        second_kernel,
        out_shape=[
            jax.ShapeDtypeStruct(moved.shape, jnp.float32),
            jax.ShapeDtypeStruct((images, parts - 1, rows - TILE, lanes), jnp.float32),
            jax.ShapeDtypeStruct((1, LANES), jnp.float32),
            jax.ShapeDtypeStruct(given.shape, jnp.float32),
        ],
        in_specs=[vmem] * 5,
        out_specs=[vmem] * 4,
        scratch_shapes=[
            pltpu.VMEM((parts, rows, lanes), jnp.float32),
            pltpu.VMEM((6, images, TILE, lanes), jnp.float32),
            pltpu.VMEM((images, lanes), jnp.float32),
        ],
        compiler_params=pltpu.CompilerParams(vmem_limit_bytes=26 * MIB),
        name="second_step",
    )(given, phi, strips, moved, tilt)


def spacing(row, coef, images):
    def quantity(q):
        return pltpu.roll(row, (LANES - images * q) % LANES, 1)

    lane = lane_of(row.shape)
    change = jnp.where((lane > 0) & (lane < images - 1), tangent_share(row, images) - coef, 0.0)
    squares, gaps, gap_diff, gap_before, diff_before = (quantity(q) for q in range(1, 6))
    change_before = pltpu.roll(change, 1, 1)
    squares_before = pltpu.roll(squares, 1, 1)
    cross = change * gap_diff - change_before * gap_before
    tangent = change * change * squares + change_before * change_before * squares_before
    tangent = tangent - 2.0 * change * change_before * diff_before
    length = jnp.maximum(gaps - 2.0 * DT * cross + DT * DT * tangent, 0.0)
    dist = jnp.where((lane > 0) & (lane < images), jnp.sqrt(length + EPS), 0.0)

    shape = (images, LANES)
    slot = lane_of(shape)
    image = row_of(shape)
    arc = jnp.sum(jnp.where(image <= slot, spread(dist, images), 0.0), axis=0, keepdims=True)
    total = jnp.sum(dist, axis=1, keepdims=True)
    target = image.astype(jnp.float32) * (total / (images - 1))
    inside = (slot >= 1) & (slot <= images - 2) & (arc <= target)
    lower = jnp.sum(jnp.where(inside, 1.0, 0.0), axis=1, keepdims=True)
    where = slot.astype(jnp.float32)
    start = jnp.sum(jnp.where(where == lower, arc, 0.0), axis=1, keepdims=True)
    step = jnp.sum(jnp.where(where == lower + 1.0, dist, 0.0), axis=1, keepdims=True)
    return change, lower, (target - start) / step


def mix_kernel(given_ref, coef_ref, one_ref, two_ref, out_ref, final, changes, shares):
    images, planes, core, lanes = two_ref.shape
    change, lower, share = spacing(read_sums(given_ref), coef_ref[...], images)
    changes[...] = spread(change, images)
    shares[...] = share
    image = row_of(lower.shape)
    lowers = [jnp.sum(jnp.where(image == j, lower, 0.0)).astype(jnp.int32) for j in range(images)]

    def finish(i, carry):
        after = jnp.minimum(i + 1, images - 1)
        before = jnp.maximum(i - 1, 0)
        scale = DT * changes[pl.ds(i, 1)]
        for p in range(planes):
            final[i, p] = two_ref[i, p] - scale * (one_ref[after, p, :core] - one_ref[before, p, :core])
        return carry

    lax.fori_loop(0, images, finish, 0)
    for j in range(images):
        portion = shares[j : j + 1]
        for p in range(planes):
            out_ref[j, p] = (1.0 - portion) * final[lowers[j], p] + portion * final[lowers[j] + 1, p]


def mix(given, coef, one, two):
    images, planes, core, lanes = two.shape
    return pl.pallas_call(
        mix_kernel,
        out_shape=jax.ShapeDtypeStruct(two.shape, jnp.float32),
        in_specs=[vmem] * 4,
        out_specs=vmem,
        scratch_shapes=[
            pltpu.VMEM(two.shape, jnp.float32),
            pltpu.VMEM((images, lanes), jnp.float32),
            pltpu.VMEM((images, lanes), jnp.float32),
        ],
        compiler_params=pltpu.CompilerParams(vmem_limit_bytes=20 * MIB),
        name="mix",
    )(given, coef, one, two)


def place_kernel(blocks_ref, out_ref, sem):
    count, planes, half, lanes = blocks_ref.shape
    copies = []
    for k in range(count):
        r, c = divmod(k, count // 2)
        piece = out_ref.at[0, :, pl.ds(r * half, half), pl.ds(c * lanes, lanes)]
        copies.append(pltpu.make_async_copy(blocks_ref.at[k], piece, sem.at[k]))
    for copy in copies:
        copy.start()
    for copy in copies:
        copy.wait()


def put_in_place(blocks):
    count, planes, half, lanes = blocks.shape
    return pl.pallas_call(
        place_kernel,
        out_shape=jax.ShapeDtypeStruct((1, planes, 2 * half, count // 2 * lanes), jnp.float32),
        in_specs=[anywhere],
        out_specs=anywhere,
        scratch_shapes=[pltpu.SemaphoreType.DMA((count,))],
        compiler_params=pltpu.CompilerParams(vmem_limit_bytes=MIB),
        name="put_in_place",
    )(blocks)


def exchange(block, axes):
    return lax.all_to_all(block, axes, split_axis=0, concat_axis=0, tiled=True)


def per_device(axes, path, tilt):
    devices = lax.axis_size(axes)
    place = lax.axis_index("img").astype(jnp.int32)[None]
    own = pltpu.with_memory_space_constraint(path[0], pltpu.HBM)
    tilt = pltpu.with_memory_space_constraint(tilt, pltpu.HBM)
    first, last, side = rim_rows(place, own, tilt)
    images = lax.axis_size("img")
    count = lax.axis_size("space")
    ahead = [(i, (i + 1) % count) for i in range(count)]
    back = [(target, source) for source, target in ahead]
    above = lax.ppermute(last, "space", ahead)
    below = lax.ppermute(first, "space", back)
    sideways = [(b * count + i, b * count + j) for b in range(images) for i, j in (ahead if 2 * b < images else back)]
    side = lax.ppermute(side, ("img", "space"), sideways)
    packed, tilt_block, tilt_rim = pack(place, own, tilt)
    packed, tilt_block = rims(place, above, below, side, tilt_rim, tilt_block, packed)
    packed, tilt_block = lax.optimization_barrier((packed, tilt_block))
    phi = exchange(packed, "img")
    moved, strips, sums = first_step(phi, tilt_block, devices)
    one, two, coef, sums = second_step(exchange(sums, axes), phi, strips, moved, tilt_block)
    mixed = mix(exchange(sums, axes), coef, one, two)
    return put_in_place(exchange(mixed, "img"))


def solution(mesh):
    return jax.shard_map(
        functools.partial(per_device, tuple(mesh.axis_names)),
        mesh=mesh,
        in_specs=(P("img", None, "space", None), P(None, "space", None)),
        out_specs=P("img", None, "space", None),
        check_vma=False,
    )
```

```python
import functools

import jax
import jax.numpy as jnp
from jax import lax
from jax.experimental import pallas as pl
from jax.experimental.pallas import tpu as pltpu
from jax.sharding import PartitionSpec as P

DT = 0.006
EPS = 1e-06
RIM = 4
TILE = 8
LANES = 128
GROUP = 16
MIB = 1024 * 1024
SLOTS = 4

vmem = pl.BlockSpec(memory_space=pltpu.VMEM)
smem = pl.BlockSpec(memory_space=pltpu.SMEM)
anywhere = pl.BlockSpec(memory_space=pl.ANY)


def lane_of(shape):
    return lax.broadcasted_iota(jnp.int32, shape, len(shape) - 1)


def row_of(shape):
    return lax.broadcasted_iota(jnp.int32, shape, len(shape) - 2)


def edges(tile, p, total):
    place = lane_of(tile.shape) - GROUP * p
    moved = pltpu.roll(tile, GROUP * p + RIM, 1)
    return jnp.where((place >= 0) & (place < 2 * RIM), moved, total)


def strip_of(before, own, after):
    lane = lane_of(own.shape)
    k = lane % GROUP
    left = jnp.where(k < RIM, before, own)
    right = jnp.where(k < RIM, own, after)
    both = jnp.where(k < 2 * RIM, left, pltpu.roll(right, 2 * RIM, 1))
    group = lane - k
    odd = jnp.where(k < 13, group + 8 + (k + 3) // 2, (group + GROUP) % LANES + 8 + (k - 13) // 2)
    source = jnp.where(k % 2 == 0, group + k // 2, odd)
    return jnp.take_along_axis(both, source, axis=1, mode="promise_in_bounds")


def own_plane(shape):
    lane = lane_of(shape)
    k = lane % GROUP
    group = lane // GROUP
    even = (k % 2 == 0) & (k >= 2 * RIM)
    here = even | (k == 1) | (k == 3)
    there = (k == 13) | (k == 15)
    return jnp.where(here, group, jnp.where(there, (group + 1) % (LANES // GROUP), -1))


def outer(before, after):
    lane = lane_of(before.shape)
    k = lane % GROUP
    both = jnp.where(k < RIM, before, after)
    source = lane - k + jnp.where(k % 2 == 0, k // 2, (k + 3) // 2) % (2 * RIM)
    return jnp.take_along_axis(both, source, axis=1, mode="promise_in_bounds")


def beside(first, second):
    return jnp.where(own_plane(first.shape) < 0, first, pltpu.roll(second, 2 * RIM, 1))


def pack_kernel(place_ref, path_ref, tilt_ref, out_ref, tilt_out, rim_out, held, near_tilt, edge, load_sem, tilt_sem):
    planes, rows, cols = path_ref.shape
    half = rows // 2
    ring = half + TILE
    near = (ring // TILE + 1) // 2 * TILE
    blocks = cols // LANES
    place = place_ref[0]
    loads = [pltpu.make_async_copy(path_ref.at[p], held.at[p], load_sem.at[p]) for p in range(planes)]
    rest = []
    start = pl.multiple_of((place // blocks) * half, half)
    next_to = pl.multiple_of(half - TILE * (place // blocks), TILE)
    for at, shift in enumerate((blocks - 1, 0, 1)):
        cut = pl.ds(pl.multiple_of(((place + shift) % blocks) * LANES, LANES), LANES)
        core = near_tilt.at[at, :, pl.ds(0, half)]
        rim = near_tilt.at[at, :, pl.ds(half, TILE)]
        rest.append(pltpu.make_async_copy(tilt_ref.at[:, pl.ds(start, half), cut], core, tilt_sem.at[2 * at]))
        rest.append(pltpu.make_async_copy(tilt_ref.at[:, pl.ds(next_to, TILE), cut], rim, tilt_sem.at[2 * at + 1]))
    for copy in loads + rest:
        copy.start()
    for p in range(planes):
        loads[p].wait()
        for c in range(blocks):
            cut = slice(c * LANES, (c + 1) * LANES)
            tile = held[p, :, cut]
            edge[c] = edges(tile, p, jnp.zeros_like(tile) if p == 0 else edge[c])
            for r in range(2):
                out_ref[r * blocks + c, ring * p : ring * p + half] = tile[r * half : (r + 1) * half]
                own = half - TILE * r
                out_ref[r * blocks + c, ring * p + half : ring * (p + 1)] = tile[own : own + TILE]
    for c in range(blocks):
        columns = outer(edge[(c - 1) % blocks], edge[(c + 1) % blocks])
        for r in range(2):
            part = columns[r * half : (r + 1) * half]
            at = ring * planes
            far = half - near
            out_ref[r * blocks + c, at : at + far] = beside(part[:far], part[near:])
            out_ref[r * blocks + c, at + far : at + near] = part[far:near]
    for copy in rest:
        copy.wait()
    sums = []
    for at in range(3):
        rim_out[at] = near_tilt[at, :, half:]
        total = jnp.zeros((half, LANES), jnp.float32)
        for p in range(planes):
            total = edges(near_tilt[at, p, :half], p, total)
        sums.append(total)
    tilt_out[:planes] = near_tilt[1]
    tilt_out[planes, :half] = strip_of(*sums)


def pack(place, path, tilt):
    planes, rows, cols = path.shape
    count, half = 2 * cols // LANES, rows // 2
    ring = half + TILE
    near = (ring // TILE + 1) // 2 * TILE
    return pl.pallas_call(
        pack_kernel,
        out_shape=[
            pltpu.VMEM((count, ring * planes + near, LANES), jnp.float32),
            pltpu.VMEM((planes + 1, ring, LANES), jnp.float32),
            pltpu.VMEM((3, planes, TILE, LANES), jnp.float32),
        ],
        in_specs=[smem] + [anywhere] * 2,
        out_specs=[vmem] * 3,
        scratch_shapes=[
            pltpu.VMEM((planes, rows, cols), jnp.float32),
            pltpu.VMEM((3, planes, ring, LANES), jnp.float32),
            pltpu.VMEM((count // 2, rows, LANES), jnp.float32),
            pltpu.SemaphoreType.DMA((planes,)),
            pltpu.SemaphoreType.DMA((6,)),
        ],
        compiler_params=pltpu.CompilerParams(vmem_limit_bytes=14 * MIB),
        cost_estimate=pl.CostEstimate(flops=10_000_000, bytes_accessed=16 * MIB, transcendentals=0),
        name="pack",
    )(place, path, tilt)


def rim_kernel(place_ref, path_ref, tilt_ref, first_ref, last_ref, side_ref, held, near, sem, near_sem):
    planes, rows, cols = path_ref.shape
    blocks = cols // LANES
    place = place_ref[0]
    upper = place < blocks
    start = pl.multiple_of((1 - place // blocks) * (rows - TILE), TILE)
    copies = []
    for at, row in enumerate((0, rows - TILE)):
        copies.append(pltpu.make_async_copy(path_ref.at[:, pl.ds(row, TILE)], held.at[at], sem.at[at]))
    for at, shift in enumerate((blocks - 1, 0, 1)):
        cut = pl.ds(pl.multiple_of(((place + shift) % blocks) * LANES, LANES), LANES)
        copies.append(pltpu.make_async_copy(tilt_ref.at[:, pl.ds(start, TILE), cut], near.at[at], near_sem.at[at]))
    for copy in copies:
        copy.start()
    for copy in copies:
        copy.wait()
    under = row_of((TILE, cols // 2)) < RIM
    for p in range(planes):
        left, right = slice(0, cols // 2), slice(cols // 2, cols)
        first_ref[p] = jnp.where(under, held[0, p, :, left], pltpu.roll(held[0, p, :, right], RIM, 0))
        last_ref[p] = jnp.where(under, pltpu.roll(held[1, p, :, left], RIM, 0), held[1, p, :, right])
        tiles = [jnp.where(upper, pltpu.roll(near[at, p], RIM, 0), near[at, p]) for at in range(3)]
        side_ref[p, :, :LANES] = jnp.where(under[:, :LANES], tiles[0], pltpu.roll(tiles[1], RIM, 0))
        side_ref[p, :, LANES:] = tiles[2]


def rim_rows(place, path, tilt):
    planes, rows, cols = path.shape
    half = jax.ShapeDtypeStruct((planes, TILE, cols // 2), jnp.float32)
    return pl.pallas_call(
        rim_kernel,
        out_shape=[half, half, jax.ShapeDtypeStruct((planes, TILE, 2 * LANES), jnp.float32)],
        in_specs=[smem] + [anywhere] * 2,
        out_specs=[vmem] * 3,
        scratch_shapes=[
            pltpu.VMEM((2, planes, TILE, cols), jnp.float32),
            pltpu.VMEM((3, planes, TILE, LANES), jnp.float32),
            pltpu.SemaphoreType.DMA((2,)),
            pltpu.SemaphoreType.DMA((3,)),
        ],
        compiler_params=pltpu.CompilerParams(vmem_limit_bytes=4 * MIB),
        name="rim_rows",
    )(place, path, tilt)


def rims_kernel(
    place_ref, above_ref, below_ref, side_ref, tilt_rim, tilt_ref, packed_ref, out_ref, tilt_out, edge
):
    planes, _, width = above_ref.shape
    count = out_ref.shape[0]
    ring = tilt_out.shape[1]
    half = ring - TILE
    near = out_ref.shape[1] - ring * planes
    blocks = count // 2
    upper = place_ref[0] < blocks
    under = row_of((TILE, LANES)) < RIM
    for r in range(2):
        for c in range(blocks):
            k = r * blocks + c
            turned = c * LANES // width
            cut = slice(c * LANES - turned * width, (c + 1) * LANES - turned * width)
            total = jnp.zeros((TILE, LANES), jnp.float32)
            for p in range(planes):
                at = slice(ring * p + half, ring * (p + 1))
                own = packed_ref[k, at]
                other = above_ref[p, :, cut] if r == 0 else below_ref[p, :, cut]
                if turned != 1 - r:
                    other = pltpu.roll(other, RIM, 0)
                tile = jnp.where(under, own, other) if r == 0 else jnp.where(under, other, own)
                out_ref[k, at] = tile
                total = edges(tile, p, total)
            edge[c] = total
        for c in range(blocks):
            columns = outer(edge[(c - 1) % blocks], edge[(c + 1) % blocks])
            at = ring * planes + half - near
            place_at = slice(at, at + TILE)
            out_ref[r * blocks + c, place_at] = beside(packed_ref[r * blocks + c, place_at], columns)
    sums = []
    for at in range(3):
        total = jnp.zeros((TILE, LANES), jnp.float32)
        for p in range(planes):
            own = tilt_rim[at, p]
            other = side_ref[p, :, LANES:] if at == 2 else side_ref[p, :, :LANES]
            turned = pltpu.roll(other, RIM, 0)
            if at == 1:
                other, turned = turned, other
            rim = jnp.where(upper, jnp.where(under, own, turned), jnp.where(under, other, own))
            if at == 1:
                tilt_out[p, half:] = rim
            total = edges(rim, p, total)
        sums.append(total)
    tilt_out[planes, half:] = strip_of(*sums)


def rims(place, above, below, side, tilt_rim, tilt, packed):
    return pl.pallas_call(
        rims_kernel,
        out_shape=[pltpu.VMEM(packed.shape, jnp.float32), pltpu.VMEM(tilt.shape, jnp.float32)],
        in_specs=[smem] + [vmem] * 6,
        out_specs=[vmem] * 2,
        input_output_aliases={6: 0, 5: 1},
        scratch_shapes=[pltpu.VMEM((packed.shape[0] // 2, TILE, LANES), jnp.float32)],
        compiler_params=pltpu.CompilerParams(vmem_limit_bytes=12 * MIB),
        cost_estimate=pl.CostEstimate(flops=1_000_000, bytes_accessed=4 * MIB, transcendentals=0),
        name="rims",
    )(place, above, below, side, tilt_rim, tilt, packed)


def rows_sum(x):
    return pltpu.roll(x, 1, 0) + pltpu.roll(x, x.shape[0] - 1, 0)


def neighbours_strip(s):
    total = pltpu.roll(s, GROUP, 1) + pltpu.roll(s, LANES - GROUP, 1)
    total = total + pltpu.roll(s, 2, 1) + pltpu.roll(s, LANES - 2, 1)
    return total + rows_sum(s)


def split(x):
    high = x.astype(jnp.bfloat16)
    rest = x - high.astype(jnp.float32)
    middle = rest.astype(jnp.bfloat16)
    low = (rest - middle.astype(jnp.float32)).astype(jnp.bfloat16)
    return jnp.concatenate([high, middle, low], axis=1)


def write_band(band):
    shape = (band.shape[0], LANES)
    row = row_of(shape) % LANES
    lane = lane_of(shape)
    apart = row - lane
    band[:, :LANES] = jnp.where((apart == 1) | (apart == -1), 1.0, 0.0).astype(jnp.bfloat16)
    k = lane % GROUP
    right = jnp.where(k > 2 * RIM, k - 13, k + 3) // 2 + LANES - RIM
    column = jnp.where(k % 2 == 0, k // 2 - RIM, right)
    band[:, LANES:] = jnp.where((row == column) & (own_plane(shape) >= 0), 1.0, 0.0).astype(jnp.bfloat16)


def neighbours_given(x, below, above, strip, p, within):
    lane = lane_of(x.shape)
    rim = pltpu.roll(strip, (LANES - GROUP * p - 6) % LANES, 1)
    rim = jnp.where((lane == 0) | (lane == LANES - 1), rim, 0.0)
    return (below + above) + rows_sum(x) + (within + rim)


def neighbours_plane(x, below, above, strip, p):
    lane = lane_of(x.shape)
    beside = pltpu.roll(strip, (LANES - GROUP * p - 6) % LANES, 1)
    left = jnp.where(lane == 0, beside, pltpu.roll(x, 1, 1))
    right = jnp.where(lane == LANES - 1, beside, pltpu.roll(x, LANES - 1, 1))
    return (below + above) + rows_sum(x) + (left + right)


def potential(field, sides, tilt_ref, mu):
    planes = mu.shape[0] - 1
    strip = field(planes)
    mu[planes] = strip * (strip * strip + 5.0) - (neighbours_strip(strip) + tilt_ref[planes])
    for p in range(planes):
        x = field(p)
        below, above = field((p - 1) % planes), field((p + 1) % planes)
        if sides is None:
            around = neighbours_plane(x, below, above, strip, p)
        else:
            around = neighbours_given(x, below, above, strip, p, sides(p))
        mu[p] = x * (x * x + 5.0) - (around + tilt_ref[p])


def force_plane(mu, p):
    planes = mu.shape[0] - 1
    return neighbours_plane(mu[p], mu[(p - 1) % planes], mu[(p + 1) % planes], mu[planes], p) - 6.0 * mu[p]


def fold(x):
    total = x[:TILE]
    for at in range(TILE, x.shape[0], TILE):
        total = total + x[at : at + TILE]
    return total


def write_sums(acc, out_ref):
    kinds, images = acc.shape[:2]
    row = jnp.zeros((1, LANES), jnp.float32)
    lane = lane_of((images, LANES))
    image = row_of((images, LANES))
    for q in range(kinds):
        part = jnp.sum(acc[q], axis=1)
        part = jnp.sum(part, axis=1, keepdims=True)
        row = row + jnp.sum(jnp.where(lane == images * q + image, part, 0.0), axis=0, keepdims=True)
    out_ref[...] = jnp.broadcast_to(row[None], out_ref.shape)


def read_sums(sums_ref):
    parts = [sums_ref[k] for k in range(TILE)]
    for k in range(TILE, sums_ref.shape[0]):
        parts[k % TILE] = parts[k % TILE] + sums_ref[k]
    while len(parts) > 1:
        parts = [a + b for a, b in zip(parts[::2], parts[1::2], strict=True)]
    return parts[0]


def spread(row, images):
    shape = (images, LANES)
    picked = jnp.where(lane_of(shape) == row_of(shape), row, 0.0)
    return jnp.broadcast_to(jnp.sum(picked, axis=1, keepdims=True), shape)


def tangent_share(row, images):
    lane = lane_of(row.shape)
    coef = row / (pltpu.roll(row, LANES - images, 1) + EPS)
    return jnp.where((lane > 0) & (lane < images - 1), coef, 0.0)


def first_kernel(phi_ref, tilt_ref, moved_ref, strip_ref, sums_ref, mu, acc, band, sides, strips):
    images, parts, rows, lanes = moved_ref.shape
    planes = parts - 1
    core = rows - TILE
    near = phi_ref.shape[1] - rows * planes
    write_band(band)
    owner = own_plane((rows, lanes))

    def plane(i, p):
        return phi_ref[i, rows * p : rows * (p + 1)]

    def prepare(i, slot):
        sides[slot] = jnp.dot(split(phi_ref[i, : rows * planes]), band[...], preferred_element_type=jnp.float32)
        columns = phi_ref[i, rows * planes :]
        far = pltpu.roll(columns[: rows - near], lanes - 2 * RIM, 1)
        strip = jnp.concatenate([columns, far], axis=0)
        for p in range(planes):
            strip = jnp.where(owner == p, sides[slot, rows * p : rows * (p + 1), lanes:], strip)
        strips[slot] = strip
        strip_ref[i] = strip

    def step(i, slot):
        after = jnp.minimum(i + 1, images - 1)
        before = jnp.maximum(i - 1, 0)

        def field(p):
            return strips[slot] if p == planes else plane(i, p)

        potential(field, lambda p: sides[slot, rows * p : rows * (p + 1), :lanes], tilt_ref, mu.at[slot])
        moved_ref[i, planes] = field(planes) + DT * (neighbours_strip(mu[slot, planes]) - 6.0 * mu[slot, planes])
        product = jnp.zeros((TILE, lanes), jnp.float32)
        square = jnp.zeros((TILE, lanes), jnp.float32)
        for p in range(planes):
            force = force_plane(mu.at[slot], p)
            moved_ref[i, p] = field(p) + DT * force
            at = slice(rows * p, rows * p + core)
            diff = phi_ref[after, at] - phi_ref[before, at]
            product = product + fold(force[:core] * diff)
            square = square + fold(diff * diff)
        acc[0, i] = product
        acc[1, i] = square

    slots = mu.shape[0]

    def body(t, carry):
        for slot in range(slots):
            prepare(jnp.minimum(slots * t + slot + 1, images - 1), (slot + 1) % slots)
            step(slots * t + slot, slot)
        return carry

    prepare(0, 0)
    lax.fori_loop(0, images // slots, body, 0)
    write_sums(acc, sums_ref)


def first_step(phi, tilt, devices):
    images = phi.shape[0]
    parts, rows, lanes = tilt.shape
    return pl.pallas_call(
        first_kernel,
        out_shape=[
            jax.ShapeDtypeStruct((images, parts, rows, lanes), jnp.float32),
            jax.ShapeDtypeStruct((images, rows, lanes), jnp.float32),
            jax.ShapeDtypeStruct((devices, 1, LANES), jnp.float32),
        ],
        in_specs=[vmem] * 2,
        out_specs=[vmem] * 3,
        scratch_shapes=[
            pltpu.VMEM((SLOTS, parts, rows, lanes), jnp.float32),
            pltpu.VMEM((2, images, TILE, lanes), jnp.float32),
            pltpu.VMEM((3 * LANES, 2 * LANES), jnp.bfloat16),
            pltpu.VMEM((SLOTS, (parts - 1) * rows, 2 * LANES), jnp.float32),
            pltpu.VMEM((SLOTS, rows, lanes), jnp.float32),
        ],
        compiler_params=pltpu.CompilerParams(vmem_limit_bytes=20 * MIB),
        name="first_step",
    )(phi, tilt)


def second_kernel(
    given_ref, phi_ref, strip_ref, moved_ref, tilt_ref, one_ref, two_ref, coef_ref, sums_ref, mu, acc, coefs, ones, twos
):
    images, parts, rows, lanes = moved_ref.shape
    planes = parts - 1
    core = rows - TILE
    slots = ones.shape[0]
    coef_row = tangent_share(read_sums(given_ref), images)
    coef_ref[...] = coef_row
    coefs[...] = spread(coef_row, images)
    ones[...] = jnp.zeros_like(ones)
    twos[...] = jnp.zeros_like(twos)

    def update(i, slot):
        after = jnp.minimum(i + 1, images - 1)
        before = jnp.maximum(i - 1, 0)
        scale = DT * coefs[pl.ds(i, 1)]
        for p in range(planes):
            at = slice(rows * p, rows * (p + 1))
            one = moved_ref[i, p] - scale * (phi_ref[after, at] - phi_ref[before, at])
            ones[slot, p] = one
            one_ref[i, p] = one[:core]
        ones[slot, planes] = moved_ref[i, planes] - scale * (strip_ref[after] - strip_ref[before])

    update(0, 0)

    def step(i, slot):
        update(jnp.minimum(i + 1, images - 1), (slot + 1) % slots)
        after, before, earlier = (ones.at[(slot + k) % slots] for k in (1, -1, -2))
        potential(lambda p: ones[slot, p], None, tilt_ref, mu.at[slot])
        coef = coefs[pl.ds(i, 1)]
        sums = [jnp.zeros((TILE, lanes), jnp.float32)] * 6
        for p in range(planes):
            force = force_plane(mu.at[slot], p)
            for start in range(0, core, 8):
                at = slice(start, start + 8)
                x = ones[slot, p, at]
                diff = after[p, at] - before[p, at]
                diff_before = x - earlier[p, at]
                two = x + DT * (force[at] - coef * diff)
                twos[slot, p, at] = two
                two_ref[i, p, at] = two
                gap = two - twos[(slot - 1) % slots, p, at]
                terms = (force[at] * diff, diff * diff, gap * gap, gap * diff, gap * diff_before, diff * diff_before)
                sums = [total + fold(term) for total, term in zip(sums, terms, strict=True)]
        for q in range(6):
            acc[q, i] = sums[q]

    def body(t, carry):
        for slot in range(slots):
            step(slots * t + slot, slot)
        return carry

    lax.fori_loop(0, images // slots, body, 0)
    write_sums(acc, sums_ref)


def second_step(given, phi, strips, moved, tilt):
    images, parts, rows, lanes = moved.shape
    core = (images, parts - 1, rows - TILE, lanes)
    return pl.pallas_call(
        second_kernel,
        out_shape=[
            jax.ShapeDtypeStruct(core, jnp.float32),
            jax.ShapeDtypeStruct(core, jnp.float32),
            jax.ShapeDtypeStruct((1, LANES), jnp.float32),
            jax.ShapeDtypeStruct(given.shape, jnp.float32),
        ],
        in_specs=[vmem] * 5,
        out_specs=[vmem] * 4,
        scratch_shapes=[
            pltpu.VMEM((SLOTS, parts, rows, lanes), jnp.float32),
            pltpu.VMEM((6, images, TILE, lanes), jnp.float32),
            pltpu.VMEM((images, lanes), jnp.float32),
            pltpu.VMEM((SLOTS, parts, rows, lanes), jnp.float32),
            pltpu.VMEM((SLOTS, parts - 1, rows - TILE, lanes), jnp.float32),
        ],
        compiler_params=pltpu.CompilerParams(vmem_limit_bytes=30 * MIB),
        name="second_step",
    )(given, phi, strips, moved, tilt)


def spacing(row, coef, images):
    def quantity(q):
        return pltpu.roll(row, (LANES - images * q) % LANES, 1)

    lane = lane_of(row.shape)
    change = jnp.where((lane > 0) & (lane < images - 1), tangent_share(row, images) - coef, 0.0)
    squares, gaps, gap_diff, gap_before, diff_before = (quantity(q) for q in range(1, 6))
    change_before = pltpu.roll(change, 1, 1)
    squares_before = pltpu.roll(squares, 1, 1)
    cross = change * gap_diff - change_before * gap_before
    tangent = change * change * squares + change_before * change_before * squares_before
    tangent = tangent - 2.0 * change * change_before * diff_before
    length = jnp.maximum(gaps - 2.0 * DT * cross + DT * DT * tangent, 0.0)
    dist = jnp.where((lane > 0) & (lane < images), jnp.sqrt(length + EPS), 0.0)

    shape = (images, LANES)
    slot = lane_of(shape)
    image = row_of(shape)
    arc = jnp.sum(jnp.where(image <= slot, spread(dist, images), 0.0), axis=0, keepdims=True)
    total = jnp.sum(dist, axis=1, keepdims=True)
    target = image.astype(jnp.float32) * (total / (images - 1))
    inside = (slot >= 1) & (slot <= images - 2) & (arc <= target)
    lower = jnp.sum(jnp.where(inside, 1.0, 0.0), axis=1, keepdims=True)
    where = slot.astype(jnp.float32)
    start = jnp.sum(jnp.where(where == lower, arc, 0.0), axis=1, keepdims=True)
    step = jnp.sum(jnp.where(where == lower + 1.0, dist, 0.0), axis=1, keepdims=True)
    return change, lower, (target - start) / step


def mix_kernel(given_ref, coef_ref, one_ref, two_ref, out_ref, final, changes, shares):
    images, planes, core, lanes = two_ref.shape
    change, lower, share = spacing(read_sums(given_ref), coef_ref[...], images)
    changes[...] = spread(change, images)
    shares[...] = share
    image = row_of(lower.shape)
    lowers = [jnp.sum(jnp.where(image == j, lower, 0.0)).astype(jnp.int32) for j in range(images)]

    def finish(i, carry):
        after = jnp.minimum(i + 1, images - 1)
        before = jnp.maximum(i - 1, 0)
        scale = DT * changes[pl.ds(i, 1)]
        for p in range(planes):
            final[i, p] = two_ref[i, p] - scale * (one_ref[after, p, :core] - one_ref[before, p, :core])
        return carry

    lax.fori_loop(0, images, finish, 0)
    for j in range(images):
        portion = shares[j : j + 1]
        for p in range(planes):
            out_ref[j, p] = (1.0 - portion) * final[lowers[j], p] + portion * final[lowers[j] + 1, p]


def mix(given, coef, one, two):
    images, planes, core, lanes = two.shape
    return pl.pallas_call(
        mix_kernel,
        out_shape=jax.ShapeDtypeStruct(two.shape, jnp.float32),
        in_specs=[vmem] * 4,
        out_specs=vmem,
        scratch_shapes=[
            pltpu.VMEM(two.shape, jnp.float32),
            pltpu.VMEM((images, lanes), jnp.float32),
            pltpu.VMEM((images, lanes), jnp.float32),
        ],
        compiler_params=pltpu.CompilerParams(vmem_limit_bytes=20 * MIB),
        name="mix",
    )(given, coef, one, two)


def place_kernel(blocks_ref, out_ref, sem):
    count, planes, half, lanes = blocks_ref.shape
    copies = []
    for k in range(count):
        r, c = divmod(k, count // 2)
        piece = out_ref.at[0, :, pl.ds(r * half, half), pl.ds(c * lanes, lanes)]
        copies.append(pltpu.make_async_copy(blocks_ref.at[k], piece, sem.at[k]))
    for copy in copies:
        copy.start()
    for copy in copies:
        copy.wait()


def put_in_place(blocks):
    count, planes, half, lanes = blocks.shape
    return pl.pallas_call(
        place_kernel,
        out_shape=jax.ShapeDtypeStruct((1, planes, 2 * half, count // 2 * lanes), jnp.float32),
        in_specs=[anywhere],
        out_specs=anywhere,
        scratch_shapes=[pltpu.SemaphoreType.DMA((count,))],
        compiler_params=pltpu.CompilerParams(vmem_limit_bytes=MIB),
        name="put_in_place",
    )(blocks)


def exchange(block, axes):
    return lax.all_to_all(block, axes, split_axis=0, concat_axis=0, tiled=True)


def per_device(axes, path, tilt):
    devices = lax.axis_size(axes)
    place = lax.axis_index("img").astype(jnp.int32)[None]
    own = pltpu.with_memory_space_constraint(path[0], pltpu.HBM)
    tilt = pltpu.with_memory_space_constraint(tilt, pltpu.HBM)
    first, last, side = rim_rows(place, own, tilt)
    images = lax.axis_size("img")
    count = lax.axis_size("space")
    ahead = [(i, (i + 1) % count) for i in range(count)]
    back = [(target, source) for source, target in ahead]
    above = lax.ppermute(last, "space", ahead)
    below = lax.ppermute(first, "space", back)
    sideways = [(b * count + i, b * count + j) for b in range(images) for i, j in (ahead if 2 * b < images else back)]
    side = lax.ppermute(side, ("img", "space"), sideways)
    packed, tilt_block, tilt_rim = pack(place, own, tilt)
    packed, tilt_block = rims(place, above, below, side, tilt_rim, tilt_block, packed)
    packed, tilt_block = lax.optimization_barrier((packed, tilt_block))
    phi = exchange(packed, "img")
    moved, strips, sums = first_step(phi, tilt_block, devices)
    one, two, coef, sums = second_step(exchange(sums, axes), phi, strips, moved, tilt_block)
    mixed = mix(exchange(sums, axes), coef, one, two)
    return put_in_place(exchange(mixed, "img"))


def solution(mesh):
    return jax.shard_map(
        functools.partial(per_device, tuple(mesh.axis_names)),
        mesh=mesh,
        in_specs=(P("img", None, "space", None), P(None, "space", None)),
        out_specs=P("img", None, "space", None),
        check_vma=False,
    )
```

```python
import functools

import jax
import jax.numpy as jnp
from jax import lax
from jax.experimental import pallas as pl
from jax.experimental.pallas import tpu as pltpu
from jax.sharding import PartitionSpec as P

DT = 0.006
EPS = 1e-06
RIM = 4
TILE = 8
LANES = 128
GROUP = 16
MIB = 1024 * 1024
SLOTS = 4

vmem = pl.BlockSpec(memory_space=pltpu.VMEM)
smem = pl.BlockSpec(memory_space=pltpu.SMEM)
anywhere = pl.BlockSpec(memory_space=pl.ANY)


def lane_of(shape):
    return lax.broadcasted_iota(jnp.int32, shape, len(shape) - 1)


def row_of(shape):
    return lax.broadcasted_iota(jnp.int32, shape, len(shape) - 2)


def edges(tile, p, total):
    place = lane_of(tile.shape) - GROUP * p
    moved = pltpu.roll(tile, GROUP * p + RIM, 1)
    return jnp.where((place >= 0) & (place < 2 * RIM), moved, total)


def strip_of(before, own, after):
    lane = lane_of(own.shape)
    k = lane % GROUP
    left = jnp.where(k < RIM, before, own)
    right = jnp.where(k < RIM, own, after)
    both = jnp.where(k < 2 * RIM, left, pltpu.roll(right, 2 * RIM, 1))
    group = lane - k
    odd = jnp.where(k < 13, group + 8 + (k + 3) // 2, (group + GROUP) % LANES + 8 + (k - 13) // 2)
    source = jnp.where(k % 2 == 0, group + k // 2, odd)
    return jnp.take_along_axis(both, source, axis=1, mode="promise_in_bounds")


def own_plane(shape):
    lane = lane_of(shape)
    k = lane % GROUP
    group = lane // GROUP
    even = (k % 2 == 0) & (k >= 2 * RIM)
    here = even | (k == 1) | (k == 3)
    there = (k == 13) | (k == 15)
    return jnp.where(here, group, jnp.where(there, (group + 1) % (LANES // GROUP), -1))


def outer(before, after):
    lane = lane_of(before.shape)
    k = lane % GROUP
    both = jnp.where(k < RIM, before, after)
    source = lane - k + jnp.where(k % 2 == 0, k // 2, (k + 3) // 2) % (2 * RIM)
    return jnp.take_along_axis(both, source, axis=1, mode="promise_in_bounds")


def beside(first, second):
    return jnp.where(own_plane(first.shape) < 0, first, pltpu.roll(second, 2 * RIM, 1))


def pack_kernel(place_ref, path_ref, tilt_ref, out_ref, tilt_out, rim_out, held, near_tilt, edge, load_sem, tilt_sem):
    planes, rows, cols = path_ref.shape
    half = rows // 2
    ring = half + TILE
    near = (ring // TILE + 1) // 2 * TILE
    blocks = cols // LANES
    place = place_ref[0]
    loads = [pltpu.make_async_copy(path_ref.at[p], held.at[p], load_sem.at[p]) for p in range(planes)]
    rest = []
    start = pl.multiple_of((place // blocks) * half, half)
    next_to = pl.multiple_of(half - TILE * (place // blocks), TILE)
    for at, shift in enumerate((blocks - 1, 0, 1)):
        cut = pl.ds(pl.multiple_of(((place + shift) % blocks) * LANES, LANES), LANES)
        core = near_tilt.at[at, :, pl.ds(0, half)]
        rim = near_tilt.at[at, :, pl.ds(half, TILE)]
        rest.append(pltpu.make_async_copy(tilt_ref.at[:, pl.ds(start, half), cut], core, tilt_sem.at[2 * at]))
        rest.append(pltpu.make_async_copy(tilt_ref.at[:, pl.ds(next_to, TILE), cut], rim, tilt_sem.at[2 * at + 1]))
    for copy in loads + rest:
        copy.start()
    for p in range(planes):
        loads[p].wait()
        for c in range(blocks):
            cut = slice(c * LANES, (c + 1) * LANES)
            tile = held[p, :, cut]
            edge[c] = edges(tile, p, jnp.zeros_like(tile) if p == 0 else edge[c])
            for r in range(2):
                out_ref[r * blocks + c, ring * p : ring * p + half] = tile[r * half : (r + 1) * half]
                own = half - TILE * r
                out_ref[r * blocks + c, ring * p + half : ring * (p + 1)] = tile[own : own + TILE]
    for c in range(blocks):
        columns = outer(edge[(c - 1) % blocks], edge[(c + 1) % blocks])
        for r in range(2):
            part = columns[r * half : (r + 1) * half]
            at = ring * planes
            far = half - near
            out_ref[r * blocks + c, at : at + far] = beside(part[:far], part[near:])
            out_ref[r * blocks + c, at + far : at + near] = part[far:near]
    for copy in rest:
        copy.wait()
    sums = []
    for at in range(3):
        rim_out[at] = near_tilt[at, :, half:]
        total = jnp.zeros((half, LANES), jnp.float32)
        for p in range(planes):
            total = edges(near_tilt[at, p, :half], p, total)
        sums.append(total)
    tilt_out[:planes] = near_tilt[1]
    tilt_out[planes, :half] = strip_of(*sums)


def pack(place, path, tilt):
    planes, rows, cols = path.shape
    count, half = 2 * cols // LANES, rows // 2
    ring = half + TILE
    near = (ring // TILE + 1) // 2 * TILE
    return pl.pallas_call(
        pack_kernel,
        out_shape=[
            pltpu.VMEM((count, ring * planes + near, LANES), jnp.float32),
            pltpu.VMEM((planes + 1, ring, LANES), jnp.float32),
            pltpu.VMEM((3, planes, TILE, LANES), jnp.float32),
        ],
        in_specs=[smem] + [anywhere] * 2,
        out_specs=[vmem] * 3,
        scratch_shapes=[
            pltpu.VMEM((planes, rows, cols), jnp.float32),
            pltpu.VMEM((3, planes, ring, LANES), jnp.float32),
            pltpu.VMEM((count // 2, rows, LANES), jnp.float32),
            pltpu.SemaphoreType.DMA((planes,)),
            pltpu.SemaphoreType.DMA((6,)),
        ],
        compiler_params=pltpu.CompilerParams(vmem_limit_bytes=14 * MIB),
        cost_estimate=pl.CostEstimate(flops=10_000_000, bytes_accessed=16 * MIB, transcendentals=0),
        name="pack",
    )(place, path, tilt)


def rim_kernel(place_ref, path_ref, tilt_ref, first_ref, last_ref, side_ref, held, near, sem, near_sem):
    planes, rows, cols = path_ref.shape
    blocks = cols // LANES
    place = place_ref[0]
    upper = place < blocks
    start = pl.multiple_of((1 - place // blocks) * (rows - TILE), TILE)
    copies = []
    for at, row in enumerate((0, rows - TILE)):
        copies.append(pltpu.make_async_copy(path_ref.at[:, pl.ds(row, TILE)], held.at[at], sem.at[at]))
    for at, shift in enumerate((blocks - 1, 0, 1)):
        cut = pl.ds(pl.multiple_of(((place + shift) % blocks) * LANES, LANES), LANES)
        copies.append(pltpu.make_async_copy(tilt_ref.at[:, pl.ds(start, TILE), cut], near.at[at], near_sem.at[at]))
    for copy in copies:
        copy.start()
    for copy in copies:
        copy.wait()
    under = row_of((TILE, cols // 2)) < RIM
    for p in range(planes):
        left, right = slice(0, cols // 2), slice(cols // 2, cols)
        first_ref[p] = jnp.where(under, held[0, p, :, left], pltpu.roll(held[0, p, :, right], RIM, 0))
        last_ref[p] = jnp.where(under, pltpu.roll(held[1, p, :, left], RIM, 0), held[1, p, :, right])
        tiles = [jnp.where(upper, pltpu.roll(near[at, p], RIM, 0), near[at, p]) for at in range(3)]
        side_ref[p, :, :LANES] = jnp.where(under[:, :LANES], tiles[0], pltpu.roll(tiles[1], RIM, 0))
        side_ref[p, :, LANES:] = tiles[2]


def rim_rows(place, path, tilt):
    planes, rows, cols = path.shape
    half = jax.ShapeDtypeStruct((planes, TILE, cols // 2), jnp.float32)
    return pl.pallas_call(
        rim_kernel,
        out_shape=[half, half, jax.ShapeDtypeStruct((planes, TILE, 2 * LANES), jnp.float32)],
        in_specs=[smem] + [anywhere] * 2,
        out_specs=[vmem] * 3,
        scratch_shapes=[
            pltpu.VMEM((2, planes, TILE, cols), jnp.float32),
            pltpu.VMEM((3, planes, TILE, LANES), jnp.float32),
            pltpu.SemaphoreType.DMA((2,)),
            pltpu.SemaphoreType.DMA((3,)),
        ],
        compiler_params=pltpu.CompilerParams(vmem_limit_bytes=4 * MIB),
        name="rim_rows",
    )(place, path, tilt)


def rims_kernel(
    place_ref, above_ref, below_ref, side_ref, tilt_rim, tilt_ref, packed_ref, out_ref, tilt_out, edge
):
    planes, _, width = above_ref.shape
    count = out_ref.shape[0]
    ring = tilt_out.shape[1]
    half = ring - TILE
    near = out_ref.shape[1] - ring * planes
    blocks = count // 2
    upper = place_ref[0] < blocks
    under = row_of((TILE, LANES)) < RIM
    for r in range(2):
        for c in range(blocks):
            k = r * blocks + c
            turned = c * LANES // width
            cut = slice(c * LANES - turned * width, (c + 1) * LANES - turned * width)
            total = jnp.zeros((TILE, LANES), jnp.float32)
            for p in range(planes):
                at = slice(ring * p + half, ring * (p + 1))
                own = packed_ref[k, at]
                other = above_ref[p, :, cut] if r == 0 else below_ref[p, :, cut]
                if turned != 1 - r:
                    other = pltpu.roll(other, RIM, 0)
                tile = jnp.where(under, own, other) if r == 0 else jnp.where(under, other, own)
                out_ref[k, at] = tile
                total = edges(tile, p, total)
            edge[c] = total
        for c in range(blocks):
            columns = outer(edge[(c - 1) % blocks], edge[(c + 1) % blocks])
            at = ring * planes + half - near
            place_at = slice(at, at + TILE)
            out_ref[r * blocks + c, place_at] = beside(packed_ref[r * blocks + c, place_at], columns)
    sums = []
    for at in range(3):
        total = jnp.zeros((TILE, LANES), jnp.float32)
        for p in range(planes):
            own = tilt_rim[at, p]
            other = side_ref[p, :, LANES:] if at == 2 else side_ref[p, :, :LANES]
            turned = pltpu.roll(other, RIM, 0)
            if at == 1:
                other, turned = turned, other
            rim = jnp.where(upper, jnp.where(under, own, turned), jnp.where(under, other, own))
            if at == 1:
                tilt_out[p, half:] = rim
            total = edges(rim, p, total)
        sums.append(total)
    tilt_out[planes, half:] = strip_of(*sums)


def rims(place, above, below, side, tilt_rim, tilt, packed):
    return pl.pallas_call(
        rims_kernel,
        out_shape=[pltpu.VMEM(packed.shape, jnp.float32), pltpu.VMEM(tilt.shape, jnp.float32)],
        in_specs=[smem] + [vmem] * 6,
        out_specs=[vmem] * 2,
        input_output_aliases={6: 0, 5: 1},
        scratch_shapes=[pltpu.VMEM((packed.shape[0] // 2, TILE, LANES), jnp.float32)],
        compiler_params=pltpu.CompilerParams(vmem_limit_bytes=12 * MIB),
        cost_estimate=pl.CostEstimate(flops=1_000_000, bytes_accessed=4 * MIB, transcendentals=0),
        name="rims",
    )(place, above, below, side, tilt_rim, tilt, packed)


def rows_sum(x):
    return pltpu.roll(x, 1, 0) + pltpu.roll(x, x.shape[0] - 1, 0)


def neighbours_strip(s):
    total = pltpu.roll(s, GROUP, 1) + pltpu.roll(s, LANES - GROUP, 1)
    total = total + pltpu.roll(s, 2, 1) + pltpu.roll(s, LANES - 2, 1)
    return total + rows_sum(s)


def split(x):
    high = x.astype(jnp.bfloat16)
    rest = x - high.astype(jnp.float32)
    middle = rest.astype(jnp.bfloat16)
    low = (rest - middle.astype(jnp.float32)).astype(jnp.bfloat16)
    return jnp.concatenate([high, middle, low], axis=1)


def write_band(band):
    shape = (band.shape[0], LANES)
    row = row_of(shape) % LANES
    lane = lane_of(shape)
    apart = row - lane
    band[:, :LANES] = jnp.where((apart == 1) | (apart == -1), 1.0, 0.0).astype(jnp.bfloat16)
    k = lane % GROUP
    right = jnp.where(k > 2 * RIM, k - 13, k + 3) // 2 + LANES - RIM
    column = jnp.where(k % 2 == 0, k // 2 - RIM, right)
    band[:, LANES:] = jnp.where((row == column) & (own_plane(shape) >= 0), 1.0, 0.0).astype(jnp.bfloat16)


def neighbours_given(x, below, above, strip, p, within):
    lane = lane_of(x.shape)
    rim = pltpu.roll(strip, (LANES - GROUP * p - 6) % LANES, 1)
    rim = jnp.where((lane == 0) | (lane == LANES - 1), rim, 0.0)
    return (below + above) + rows_sum(x) + (within + rim)


def neighbours_plane(x, below, above, strip, p):
    lane = lane_of(x.shape)
    beside = pltpu.roll(strip, (LANES - GROUP * p - 6) % LANES, 1)
    left = jnp.where(lane == 0, beside, pltpu.roll(x, 1, 1))
    right = jnp.where(lane == LANES - 1, beside, pltpu.roll(x, LANES - 1, 1))
    return (below + above) + rows_sum(x) + (left + right)


def potential(field, sides, tilt_ref, mu):
    planes = mu.shape[0] - 1
    strip = field(planes)
    mu[planes] = strip * (strip * strip + 5.0) - (neighbours_strip(strip) + tilt_ref[planes])
    for p in range(planes):
        x = field(p)
        below, above = field((p - 1) % planes), field((p + 1) % planes)
        if sides is None:
            around = neighbours_plane(x, below, above, strip, p)
        else:
            around = neighbours_given(x, below, above, strip, p, sides(p))
        mu[p] = x * (x * x + 5.0) - (around + tilt_ref[p])


def force_plane(mu, p):
    planes = mu.shape[0] - 1
    return neighbours_plane(mu[p], mu[(p - 1) % planes], mu[(p + 1) % planes], mu[planes], p) - 6.0 * mu[p]


def fold(x):
    total = x[:TILE]
    for at in range(TILE, x.shape[0], TILE):
        total = total + x[at : at + TILE]
    return total


def write_sums(acc, out_ref):
    kinds, images = acc.shape[:2]
    row = jnp.zeros((1, LANES), jnp.float32)
    lane = lane_of((images, LANES))
    image = row_of((images, LANES))
    for q in range(kinds):
        part = jnp.sum(acc[q], axis=1)
        part = jnp.sum(part, axis=1, keepdims=True)
        row = row + jnp.sum(jnp.where(lane == images * q + image, part, 0.0), axis=0, keepdims=True)
    out_ref[...] = jnp.broadcast_to(row[None], out_ref.shape)


def read_sums(sums_ref):
    parts = [sums_ref[k] for k in range(TILE)]
    for k in range(TILE, sums_ref.shape[0]):
        parts[k % TILE] = parts[k % TILE] + sums_ref[k]
    while len(parts) > 1:
        parts = [a + b for a, b in zip(parts[::2], parts[1::2], strict=True)]
    return parts[0]


def spread(row, images):
    shape = (images, LANES)
    picked = jnp.where(lane_of(shape) == row_of(shape), row, 0.0)
    return jnp.broadcast_to(jnp.sum(picked, axis=1, keepdims=True), shape)


def tangent_share(row, images):
    lane = lane_of(row.shape)
    coef = row / (pltpu.roll(row, LANES - images, 1) + EPS)
    return jnp.where((lane > 0) & (lane < images - 1), coef, 0.0)


def first_kernel(phi_ref, tilt_ref, moved_ref, strip_ref, sums_ref, mu, acc, band, sides, strips):
    images, parts, rows, lanes = moved_ref.shape
    planes = parts - 1
    core = rows - TILE
    near = phi_ref.shape[1] - rows * planes
    write_band(band)
    owner = own_plane((rows, lanes))

    def plane(i, p):
        return phi_ref[i, rows * p : rows * (p + 1)]

    def prepare(i, slot):
        sides[slot] = jnp.dot(split(phi_ref[i, : rows * planes]), band[...], preferred_element_type=jnp.float32)
        columns = phi_ref[i, rows * planes :]
        far = pltpu.roll(columns[: rows - near], lanes - 2 * RIM, 1)
        strip = jnp.concatenate([columns, far], axis=0)
        for p in range(planes):
            strip = jnp.where(owner == p, sides[slot, rows * p : rows * (p + 1), lanes:], strip)
        strips[slot] = strip
        strip_ref[i] = strip

    def step(i, slot):
        after = jnp.minimum(i + 1, images - 1)
        before = jnp.maximum(i - 1, 0)

        def field(p):
            return strips[slot] if p == planes else plane(i, p)

        potential(field, lambda p: sides[slot, rows * p : rows * (p + 1), :lanes], tilt_ref, mu.at[slot])
        moved_ref[i, planes] = field(planes) + DT * (neighbours_strip(mu[slot, planes]) - 6.0 * mu[slot, planes])
        product = jnp.zeros((TILE, lanes), jnp.float32)
        square = jnp.zeros((TILE, lanes), jnp.float32)
        for p in range(planes):
            force = force_plane(mu.at[slot], p)
            moved_ref[i, p] = field(p) + DT * force
            at = slice(rows * p, rows * p + core)
            diff = phi_ref[after, at] - phi_ref[before, at]
            product = product + fold(force[:core] * diff)
            square = square + fold(diff * diff)
        acc[0, i] = product
        acc[1, i] = square

    slots = mu.shape[0]

    def body(t, carry):
        for slot in range(slots):
            prepare(jnp.minimum(slots * t + slot + 1, images - 1), (slot + 1) % slots)
            step(slots * t + slot, slot)
        return carry

    prepare(0, 0)
    lax.fori_loop(0, images // slots, body, 0)
    write_sums(acc, sums_ref)


def first_step(phi, tilt, devices):
    images = phi.shape[0]
    parts, rows, lanes = tilt.shape
    return pl.pallas_call(
        first_kernel,
        out_shape=[
            jax.ShapeDtypeStruct((images, parts, rows, lanes), jnp.float32),
            jax.ShapeDtypeStruct((images, rows, lanes), jnp.float32),
            jax.ShapeDtypeStruct((devices, 1, LANES), jnp.float32),
        ],
        in_specs=[vmem] * 2,
        out_specs=[vmem] * 3,
        scratch_shapes=[
            pltpu.VMEM((SLOTS, parts, rows, lanes), jnp.float32),
            pltpu.VMEM((2, images, TILE, lanes), jnp.float32),
            pltpu.VMEM((3 * LANES, 2 * LANES), jnp.bfloat16),
            pltpu.VMEM((SLOTS, (parts - 1) * rows, 2 * LANES), jnp.float32),
            pltpu.VMEM((SLOTS, rows, lanes), jnp.float32),
        ],
        compiler_params=pltpu.CompilerParams(vmem_limit_bytes=20 * MIB),
        name="first_step",
    )(phi, tilt)


def second_kernel(
    given_ref, phi_ref, strip_ref, moved_ref, tilt_ref, one_ref, two_ref, coef_ref, sums_ref, mu, acc, coefs, ones, twos
):
    images, parts, rows, lanes = moved_ref.shape
    planes = parts - 1
    core = rows - TILE
    slots = ones.shape[0]
    coef_row = tangent_share(read_sums(given_ref), images)
    coef_ref[...] = coef_row
    coefs[...] = spread(coef_row, images)
    ones[...] = jnp.zeros_like(ones)
    twos[...] = jnp.zeros_like(twos)

    def update(i, slot):
        after = jnp.minimum(i + 1, images - 1)
        before = jnp.maximum(i - 1, 0)
        scale = DT * coefs[pl.ds(i, 1)]
        for p in range(planes):
            at = slice(rows * p, rows * (p + 1))
            one = moved_ref[i, p] - scale * (phi_ref[after, at] - phi_ref[before, at])
            ones[slot, p] = one
            one_ref[i, p] = one[:core]
        ones[slot, planes] = moved_ref[i, planes] - scale * (strip_ref[after] - strip_ref[before])

    update(0, 0)

    def step(i, slot):
        update(jnp.minimum(i + 1, images - 1), (slot + 1) % slots)
        after, before, earlier = (ones.at[(slot + k) % slots] for k in (1, -1, -2))
        potential(lambda p: ones[slot, p], None, tilt_ref, mu.at[slot])
        coef = coefs[pl.ds(i, 1)]
        sums = [jnp.zeros((TILE, lanes), jnp.float32)] * 6
        for p in range(planes):
            force = force_plane(mu.at[slot], p)
            parts_of = [None] * 6
            for start in range(0, core, TILE):
                at = slice(start, start + TILE)
                x = ones[slot, p, at]
                diff = after[p, at] - before[p, at]
                diff_before = x - earlier[p, at]
                two = x + DT * (force[at] - coef * diff)
                twos[slot, p, at] = two
                two_ref[i, p, at] = two
                gap = two - twos[(slot - 1) % slots, p, at]
                terms = (force[at] * diff, diff * diff, gap * gap, gap * diff, gap * diff_before, diff * diff_before)
                parts_of = [term if part is None else part + term for part, term in zip(parts_of, terms, strict=True)]
            sums = [total + part for total, part in zip(sums, parts_of, strict=True)]
        for q in range(6):
            acc[q, i] = sums[q]

    def body(t, carry):
        for slot in range(slots):
            step(slots * t + slot, slot)
        return carry

    lax.fori_loop(0, images // slots, body, 0)
    write_sums(acc, sums_ref)


def second_step(given, phi, strips, moved, tilt):
    images, parts, rows, lanes = moved.shape
    core = (images, parts - 1, rows - TILE, lanes)
    return pl.pallas_call(
        second_kernel,
        out_shape=[
            jax.ShapeDtypeStruct(core, jnp.float32),
            jax.ShapeDtypeStruct(core, jnp.float32),
            jax.ShapeDtypeStruct((1, LANES), jnp.float32),
            jax.ShapeDtypeStruct(given.shape, jnp.float32),
        ],
        in_specs=[vmem] * 5,
        out_specs=[vmem] * 4,
        scratch_shapes=[
            pltpu.VMEM((SLOTS, parts, rows, lanes), jnp.float32),
            pltpu.VMEM((6, images, TILE, lanes), jnp.float32),
            pltpu.VMEM((images, lanes), jnp.float32),
            pltpu.VMEM((SLOTS, parts, rows, lanes), jnp.float32),
            pltpu.VMEM((SLOTS, parts - 1, rows - TILE, lanes), jnp.float32),
        ],
        compiler_params=pltpu.CompilerParams(vmem_limit_bytes=30 * MIB),
        name="second_step",
    )(given, phi, strips, moved, tilt)


def spacing(row, coef, images):
    def quantity(q):
        return pltpu.roll(row, (LANES - images * q) % LANES, 1)

    lane = lane_of(row.shape)
    change = jnp.where((lane > 0) & (lane < images - 1), tangent_share(row, images) - coef, 0.0)
    squares, gaps, gap_diff, gap_before, diff_before = (quantity(q) for q in range(1, 6))
    change_before = pltpu.roll(change, 1, 1)
    squares_before = pltpu.roll(squares, 1, 1)
    cross = change * gap_diff - change_before * gap_before
    tangent = change * change * squares + change_before * change_before * squares_before
    tangent = tangent - 2.0 * change * change_before * diff_before
    length = jnp.maximum(gaps - 2.0 * DT * cross + DT * DT * tangent, 0.0)
    dist = jnp.where((lane > 0) & (lane < images), jnp.sqrt(length + EPS), 0.0)

    shape = (images, LANES)
    slot = lane_of(shape)
    image = row_of(shape)
    arc = jnp.sum(jnp.where(image <= slot, spread(dist, images), 0.0), axis=0, keepdims=True)
    total = jnp.sum(dist, axis=1, keepdims=True)
    target = image.astype(jnp.float32) * (total / (images - 1))
    inside = (slot >= 1) & (slot <= images - 2) & (arc <= target)
    lower = jnp.sum(jnp.where(inside, 1.0, 0.0), axis=1, keepdims=True)
    where = slot.astype(jnp.float32)
    start = jnp.sum(jnp.where(where == lower, arc, 0.0), axis=1, keepdims=True)
    step = jnp.sum(jnp.where(where == lower + 1.0, dist, 0.0), axis=1, keepdims=True)
    return change, lower, (target - start) / step


def mix_kernel(given_ref, coef_ref, one_ref, two_ref, out_ref, final, changes, shares):
    images, planes, core, lanes = two_ref.shape
    change, lower, share = spacing(read_sums(given_ref), coef_ref[...], images)
    changes[...] = spread(change, images)
    shares[...] = share
    image = row_of(lower.shape)
    lowers = [jnp.sum(jnp.where(image == j, lower, 0.0)).astype(jnp.int32) for j in range(images)]

    def finish(i, carry):
        after = jnp.minimum(i + 1, images - 1)
        before = jnp.maximum(i - 1, 0)
        scale = DT * changes[pl.ds(i, 1)]
        for p in range(planes):
            final[i, p] = two_ref[i, p] - scale * (one_ref[after, p, :core] - one_ref[before, p, :core])
        return carry

    lax.fori_loop(0, images, finish, 0)
    for j in range(images):
        portion = shares[j : j + 1]
        for p in range(planes):
            out_ref[j, p] = (1.0 - portion) * final[lowers[j], p] + portion * final[lowers[j] + 1, p]


def mix(given, coef, one, two):
    images, planes, core, lanes = two.shape
    return pl.pallas_call(
        mix_kernel,
        out_shape=jax.ShapeDtypeStruct(two.shape, jnp.float32),
        in_specs=[vmem] * 4,
        out_specs=vmem,
        scratch_shapes=[
            pltpu.VMEM(two.shape, jnp.float32),
            pltpu.VMEM((images, lanes), jnp.float32),
            pltpu.VMEM((images, lanes), jnp.float32),
        ],
        compiler_params=pltpu.CompilerParams(vmem_limit_bytes=20 * MIB),
        name="mix",
    )(given, coef, one, two)


def place_kernel(blocks_ref, out_ref, sem):
    count, planes, half, lanes = blocks_ref.shape
    copies = []
    for k in range(count):
        r, c = divmod(k, count // 2)
        piece = out_ref.at[0, :, pl.ds(r * half, half), pl.ds(c * lanes, lanes)]
        copies.append(pltpu.make_async_copy(blocks_ref.at[k], piece, sem.at[k]))
    for copy in copies:
        copy.start()
    for copy in copies:
        copy.wait()


def put_in_place(blocks):
    count, planes, half, lanes = blocks.shape
    return pl.pallas_call(
        place_kernel,
        out_shape=jax.ShapeDtypeStruct((1, planes, 2 * half, count // 2 * lanes), jnp.float32),
        in_specs=[anywhere],
        out_specs=anywhere,
        scratch_shapes=[pltpu.SemaphoreType.DMA((count,))],
        compiler_params=pltpu.CompilerParams(vmem_limit_bytes=MIB),
        name="put_in_place",
    )(blocks)


def exchange(block, axes):
    return lax.all_to_all(block, axes, split_axis=0, concat_axis=0, tiled=True)


def per_device(axes, path, tilt):
    devices = lax.axis_size(axes)
    place = lax.axis_index("img").astype(jnp.int32)[None]
    own = pltpu.with_memory_space_constraint(path[0], pltpu.HBM)
    tilt = pltpu.with_memory_space_constraint(tilt, pltpu.HBM)
    first, last, side = rim_rows(place, own, tilt)
    images = lax.axis_size("img")
    count = lax.axis_size("space")
    ahead = [(i, (i + 1) % count) for i in range(count)]
    back = [(target, source) for source, target in ahead]
    above = lax.ppermute(last, "space", ahead)
    below = lax.ppermute(first, "space", back)
    sideways = [(b * count + i, b * count + j) for b in range(images) for i, j in (ahead if 2 * b < images else back)]
    side = lax.ppermute(side, ("img", "space"), sideways)
    packed, tilt_block, tilt_rim = pack(place, own, tilt)
    packed, tilt_block = rims(place, above, below, side, tilt_rim, tilt_block, packed)
    packed, tilt_block = lax.optimization_barrier((packed, tilt_block))
    phi = exchange(packed, "img")
    moved, strips, sums = first_step(phi, tilt_block, devices)
    one, two, coef, sums = second_step(exchange(sums, axes), phi, strips, moved, tilt_block)
    mixed = mix(exchange(sums, axes), coef, one, two)
    return put_in_place(exchange(mixed, "img"))


def solution(mesh):
    return jax.shard_map(
        functools.partial(per_device, tuple(mesh.axis_names)),
        mesh=mesh,
        in_specs=(P("img", None, "space", None), P(None, "space", None)),
        out_specs=P("img", None, "space", None),
        check_vma=False,
    )
```

```python
import functools

import jax
import jax.numpy as jnp
from jax import lax
from jax.experimental import pallas as pl
from jax.experimental.pallas import tpu as pltpu
from jax.sharding import PartitionSpec as P

DT = 0.006
EPS = 1e-06
RIM = 4
TILE = 8
LANES = 128
GROUP = 16
MIB = 1024 * 1024
SLOTS = 4

vmem = pl.BlockSpec(memory_space=pltpu.VMEM)
smem = pl.BlockSpec(memory_space=pltpu.SMEM)
anywhere = pl.BlockSpec(memory_space=pl.ANY)


def lane_of(shape):
    return lax.broadcasted_iota(jnp.int32, shape, len(shape) - 1)


def row_of(shape):
    return lax.broadcasted_iota(jnp.int32, shape, len(shape) - 2)


def edges(tile, p, total):
    place = lane_of(tile.shape) - GROUP * p
    moved = pltpu.roll(tile, GROUP * p + RIM, 1)
    return jnp.where((place >= 0) & (place < 2 * RIM), moved, total)


def strip_of(before, own, after):
    lane = lane_of(own.shape)
    k = lane % GROUP
    left = jnp.where(k < RIM, before, own)
    right = jnp.where(k < RIM, own, after)
    both = jnp.where(k < 2 * RIM, left, pltpu.roll(right, 2 * RIM, 1))
    group = lane - k
    odd = jnp.where(k < 13, group + 8 + (k + 3) // 2, (group + GROUP) % LANES + 8 + (k - 13) // 2)
    source = jnp.where(k % 2 == 0, group + k // 2, odd)
    return jnp.take_along_axis(both, source, axis=1, mode="promise_in_bounds")


def own_plane(shape):
    lane = lane_of(shape)
    k = lane % GROUP
    group = lane // GROUP
    even = (k % 2 == 0) & (k >= 2 * RIM)
    here = even | (k == 1) | (k == 3)
    there = (k == 13) | (k == 15)
    return jnp.where(here, group, jnp.where(there, (group + 1) % (LANES // GROUP), -1))


def outer(before, after):
    lane = lane_of(before.shape)
    k = lane % GROUP
    both = jnp.where(k < RIM, before, after)
    source = lane - k + jnp.where(k % 2 == 0, k // 2, (k + 3) // 2) % (2 * RIM)
    return jnp.take_along_axis(both, source, axis=1, mode="promise_in_bounds")


def beside(first, second):
    return jnp.where(own_plane(first.shape) < 0, first, pltpu.roll(second, 2 * RIM, 1))


def pack_kernel(place_ref, path_ref, tilt_ref, out_ref, tilt_out, rim_out, held, near_tilt, edge, load_sem, tilt_sem):
    planes, rows, cols = path_ref.shape
    half = rows // 2
    ring = half + TILE
    near = (ring // TILE + 1) // 2 * TILE
    blocks = cols // LANES
    place = place_ref[0]
    loads = [pltpu.make_async_copy(path_ref.at[p], held.at[p], load_sem.at[p]) for p in range(planes)]
    rest = []
    start = pl.multiple_of((place // blocks) * half, half)
    next_to = pl.multiple_of(half - TILE * (place // blocks), TILE)
    for at, shift in enumerate((blocks - 1, 0, 1)):
        cut = pl.ds(pl.multiple_of(((place + shift) % blocks) * LANES, LANES), LANES)
        core = near_tilt.at[at, :, pl.ds(0, half)]
        rim = near_tilt.at[at, :, pl.ds(half, TILE)]
        rest.append(pltpu.make_async_copy(tilt_ref.at[:, pl.ds(start, half), cut], core, tilt_sem.at[2 * at]))
        rest.append(pltpu.make_async_copy(tilt_ref.at[:, pl.ds(next_to, TILE), cut], rim, tilt_sem.at[2 * at + 1]))
    for copy in loads + rest:
        copy.start()
    for p in range(planes):
        loads[p].wait()
        for c in range(blocks):
            cut = slice(c * LANES, (c + 1) * LANES)
            tile = held[p, :, cut]
            edge[c] = edges(tile, p, jnp.zeros_like(tile) if p == 0 else edge[c])
            for r in range(2):
                out_ref[r * blocks + c, ring * p : ring * p + half] = tile[r * half : (r + 1) * half]
                own = half - TILE * r
                out_ref[r * blocks + c, ring * p + half : ring * (p + 1)] = tile[own : own + TILE]
    for c in range(blocks):
        columns = outer(edge[(c - 1) % blocks], edge[(c + 1) % blocks])
        for r in range(2):
            part = columns[r * half : (r + 1) * half]
            at = ring * planes
            far = half - near
            out_ref[r * blocks + c, at : at + far] = beside(part[:far], part[near:])
            out_ref[r * blocks + c, at + far : at + near] = part[far:near]
    for copy in rest:
        copy.wait()
    sums = []
    for at in range(3):
        rim_out[at] = near_tilt[at, :, half:]
        total = jnp.zeros((half, LANES), jnp.float32)
        for p in range(planes):
            total = edges(near_tilt[at, p, :half], p, total)
        sums.append(total)
    tilt_out[:planes] = near_tilt[1]
    tilt_out[planes, :half] = strip_of(*sums)


def pack(place, path, tilt):
    planes, rows, cols = path.shape
    count, half = 2 * cols // LANES, rows // 2
    ring = half + TILE
    near = (ring // TILE + 1) // 2 * TILE
    return pl.pallas_call(
        pack_kernel,
        out_shape=[
            pltpu.VMEM((count, ring * planes + near, LANES), jnp.float32),
            pltpu.VMEM((planes + 1, ring, LANES), jnp.float32),
            pltpu.VMEM((3, planes, TILE, LANES), jnp.float32),
        ],
        in_specs=[smem] + [anywhere] * 2,
        out_specs=[vmem] * 3,
        scratch_shapes=[
            pltpu.VMEM((planes, rows, cols), jnp.float32),
            pltpu.VMEM((3, planes, ring, LANES), jnp.float32),
            pltpu.VMEM((count // 2, rows, LANES), jnp.float32),
            pltpu.SemaphoreType.DMA((planes,)),
            pltpu.SemaphoreType.DMA((6,)),
        ],
        compiler_params=pltpu.CompilerParams(vmem_limit_bytes=14 * MIB),
        cost_estimate=pl.CostEstimate(flops=10_000_000, bytes_accessed=16 * MIB, transcendentals=0),
        name="pack",
    )(place, path, tilt)


def rim_kernel(place_ref, path_ref, tilt_ref, first_ref, last_ref, side_ref, held, near, sem, near_sem):
    planes, rows, cols = path_ref.shape
    blocks = cols // LANES
    place = place_ref[0]
    upper = place < blocks
    start = pl.multiple_of((1 - place // blocks) * (rows - TILE), TILE)
    copies = []
    for at, row in enumerate((0, rows - TILE)):
        copies.append(pltpu.make_async_copy(path_ref.at[:, pl.ds(row, TILE)], held.at[at], sem.at[at]))
    for at, shift in enumerate((blocks - 1, 0, 1)):
        cut = pl.ds(pl.multiple_of(((place + shift) % blocks) * LANES, LANES), LANES)
        copies.append(pltpu.make_async_copy(tilt_ref.at[:, pl.ds(start, TILE), cut], near.at[at], near_sem.at[at]))
    for copy in copies:
        copy.start()
    for copy in copies:
        copy.wait()
    under = row_of((TILE, cols // 2)) < RIM
    for p in range(planes):
        left, right = slice(0, cols // 2), slice(cols // 2, cols)
        first_ref[p] = jnp.where(under, held[0, p, :, left], pltpu.roll(held[0, p, :, right], RIM, 0))
        last_ref[p] = jnp.where(under, pltpu.roll(held[1, p, :, left], RIM, 0), held[1, p, :, right])
        tiles = [jnp.where(upper, pltpu.roll(near[at, p], RIM, 0), near[at, p]) for at in range(3)]
        side_ref[p, :, :LANES] = jnp.where(under[:, :LANES], tiles[0], pltpu.roll(tiles[1], RIM, 0))
        side_ref[p, :, LANES:] = tiles[2]


def rim_rows(place, path, tilt):
    planes, rows, cols = path.shape
    half = jax.ShapeDtypeStruct((planes, TILE, cols // 2), jnp.float32)
    return pl.pallas_call(
        rim_kernel,
        out_shape=[half, half, jax.ShapeDtypeStruct((planes, TILE, 2 * LANES), jnp.float32)],
        in_specs=[smem] + [anywhere] * 2,
        out_specs=[vmem] * 3,
        scratch_shapes=[
            pltpu.VMEM((2, planes, TILE, cols), jnp.float32),
            pltpu.VMEM((3, planes, TILE, LANES), jnp.float32),
            pltpu.SemaphoreType.DMA((2,)),
            pltpu.SemaphoreType.DMA((3,)),
        ],
        compiler_params=pltpu.CompilerParams(vmem_limit_bytes=4 * MIB),
        name="rim_rows",
    )(place, path, tilt)


def rims_kernel(
    place_ref, above_ref, below_ref, side_ref, tilt_rim, tilt_ref, packed_ref, out_ref, tilt_out, edge
):
    planes, _, width = above_ref.shape
    count = out_ref.shape[0]
    ring = tilt_out.shape[1]
    half = ring - TILE
    near = out_ref.shape[1] - ring * planes
    blocks = count // 2
    upper = place_ref[0] < blocks
    under = row_of((TILE, LANES)) < RIM
    for r in range(2):
        for c in range(blocks):
            k = r * blocks + c
            turned = c * LANES // width
            cut = slice(c * LANES - turned * width, (c + 1) * LANES - turned * width)
            total = jnp.zeros((TILE, LANES), jnp.float32)
            for p in range(planes):
                at = slice(ring * p + half, ring * (p + 1))
                own = packed_ref[k, at]
                other = above_ref[p, :, cut] if r == 0 else below_ref[p, :, cut]
                if turned != 1 - r:
                    other = pltpu.roll(other, RIM, 0)
                tile = jnp.where(under, own, other) if r == 0 else jnp.where(under, other, own)
                out_ref[k, at] = tile
                total = edges(tile, p, total)
            edge[c] = total
        for c in range(blocks):
            columns = outer(edge[(c - 1) % blocks], edge[(c + 1) % blocks])
            at = ring * planes + half - near
            place_at = slice(at, at + TILE)
            out_ref[r * blocks + c, place_at] = beside(packed_ref[r * blocks + c, place_at], columns)
    sums = []
    for at in range(3):
        total = jnp.zeros((TILE, LANES), jnp.float32)
        for p in range(planes):
            own = tilt_rim[at, p]
            other = side_ref[p, :, LANES:] if at == 2 else side_ref[p, :, :LANES]
            turned = pltpu.roll(other, RIM, 0)
            if at == 1:
                other, turned = turned, other
            rim = jnp.where(upper, jnp.where(under, own, turned), jnp.where(under, other, own))
            if at == 1:
                tilt_out[p, half:] = rim
            total = edges(rim, p, total)
        sums.append(total)
    tilt_out[planes, half:] = strip_of(*sums)


def rims(place, above, below, side, tilt_rim, tilt, packed):
    return pl.pallas_call(
        rims_kernel,
        out_shape=[pltpu.VMEM(packed.shape, jnp.float32), pltpu.VMEM(tilt.shape, jnp.float32)],
        in_specs=[smem] + [vmem] * 6,
        out_specs=[vmem] * 2,
        input_output_aliases={6: 0, 5: 1},
        scratch_shapes=[pltpu.VMEM((packed.shape[0] // 2, TILE, LANES), jnp.float32)],
        compiler_params=pltpu.CompilerParams(vmem_limit_bytes=12 * MIB),
        cost_estimate=pl.CostEstimate(flops=1_000_000, bytes_accessed=4 * MIB, transcendentals=0),
        name="rims",
    )(place, above, below, side, tilt_rim, tilt, packed)


def rows_sum(x):
    return pltpu.roll(x, 1, 0) + pltpu.roll(x, x.shape[0] - 1, 0)


def neighbours_strip(s):
    total = pltpu.roll(s, GROUP, 1) + pltpu.roll(s, LANES - GROUP, 1)
    total = total + pltpu.roll(s, 2, 1) + pltpu.roll(s, LANES - 2, 1)
    return total + rows_sum(s)


def split(x):
    high = x.astype(jnp.bfloat16)
    rest = x - high.astype(jnp.float32)
    middle = rest.astype(jnp.bfloat16)
    low = (rest - middle.astype(jnp.float32)).astype(jnp.bfloat16)
    return jnp.concatenate([high, middle, low], axis=1)


def write_band(band):
    shape = (band.shape[0], LANES)
    row = row_of(shape) % LANES
    lane = lane_of(shape)
    apart = row - lane
    band[:, :LANES] = jnp.where((apart == 1) | (apart == -1), 1.0, 0.0).astype(jnp.bfloat16)
    k = lane % GROUP
    right = jnp.where(k > 2 * RIM, k - 13, k + 3) // 2 + LANES - RIM
    column = jnp.where(k % 2 == 0, k // 2 - RIM, right)
    band[:, LANES:] = jnp.where((row == column) & (own_plane(shape) >= 0), 1.0, 0.0).astype(jnp.bfloat16)


def neighbours_given(x, below, above, strip, p, within):
    lane = lane_of(x.shape)
    rim = pltpu.roll(strip, (LANES - GROUP * p - 6) % LANES, 1)
    rim = jnp.where((lane == 0) | (lane == LANES - 1), rim, 0.0)
    return (below + above) + rows_sum(x) + (within + rim)


def neighbours_plane(x, below, above, strip, p):
    lane = lane_of(x.shape)
    beside = pltpu.roll(strip, (LANES - GROUP * p - 6) % LANES, 1)
    left = jnp.where(lane == 0, beside, pltpu.roll(x, 1, 1))
    right = jnp.where(lane == LANES - 1, beside, pltpu.roll(x, LANES - 1, 1))
    return (below + above) + rows_sum(x) + (left + right)


def potential(field, sides, tilt_ref, mu):
    planes = mu.shape[0] - 1
    strip = field(planes)
    mu[planes] = strip * (strip * strip + 5.0) - (neighbours_strip(strip) + tilt_ref[planes])
    for p in range(planes):
        x = field(p)
        below, above = field((p - 1) % planes), field((p + 1) % planes)
        if sides is None:
            around = neighbours_plane(x, below, above, strip, p)
        else:
            around = neighbours_given(x, below, above, strip, p, sides(p))
        mu[p] = x * (x * x + 5.0) - (around + tilt_ref[p])


def force_plane(mu, p):
    planes = mu.shape[0] - 1
    return neighbours_plane(mu[p], mu[(p - 1) % planes], mu[(p + 1) % planes], mu[planes], p) - 6.0 * mu[p]


def fold(x):
    total = x[:TILE]
    for at in range(TILE, x.shape[0], TILE):
        total = total + x[at : at + TILE]
    return total


def write_sums(acc, out_ref):
    kinds, images = acc.shape[:2]
    row = jnp.zeros((1, LANES), jnp.float32)
    lane = lane_of((images, LANES))
    image = row_of((images, LANES))
    for q in range(kinds):
        part = jnp.sum(acc[q], axis=1)
        part = jnp.sum(part, axis=1, keepdims=True)
        row = row + jnp.sum(jnp.where(lane == images * q + image, part, 0.0), axis=0, keepdims=True)
    out_ref[...] = jnp.broadcast_to(row[None], out_ref.shape)


def read_sums(sums_ref):
    parts = [sums_ref[k] for k in range(TILE)]
    for k in range(TILE, sums_ref.shape[0]):
        parts[k % TILE] = parts[k % TILE] + sums_ref[k]
    while len(parts) > 1:
        parts = [a + b for a, b in zip(parts[::2], parts[1::2], strict=True)]
    return parts[0]


def spread(row, images):
    shape = (images, LANES)
    picked = jnp.where(lane_of(shape) == row_of(shape), row, 0.0)
    return jnp.broadcast_to(jnp.sum(picked, axis=1, keepdims=True), shape)


def tangent_share(row, images):
    lane = lane_of(row.shape)
    coef = row / (pltpu.roll(row, LANES - images, 1) + EPS)
    return jnp.where((lane > 0) & (lane < images - 1), coef, 0.0)


def first_kernel(phi_ref, tilt_ref, moved_ref, strip_ref, sums_ref, mu, acc, band, sides, strips):
    images, parts, rows, lanes = moved_ref.shape
    planes = parts - 1
    core = rows - TILE
    near = phi_ref.shape[1] - rows * planes
    write_band(band)
    owner = own_plane((rows, lanes))

    def plane(i, p):
        return phi_ref[i, rows * p : rows * (p + 1)]

    def prepare(i, slot):
        sides[slot] = jnp.dot(split(phi_ref[i, : rows * planes]), band[...], preferred_element_type=jnp.float32)
        columns = phi_ref[i, rows * planes :]
        far = pltpu.roll(columns[: rows - near], lanes - 2 * RIM, 1)
        strip = jnp.concatenate([columns, far], axis=0)
        for p in range(planes):
            strip = jnp.where(owner == p, sides[slot, rows * p : rows * (p + 1), lanes:], strip)
        strips[slot] = strip
        strip_ref[i] = strip

    def step(i, slot):
        after = jnp.minimum(i + 1, images - 1)
        before = jnp.maximum(i - 1, 0)

        def field(p):
            return strips[slot] if p == planes else plane(i, p)

        potential(field, lambda p: sides[slot, rows * p : rows * (p + 1), :lanes], tilt_ref, mu.at[slot])
        moved_ref[i, planes] = field(planes) + DT * (neighbours_strip(mu[slot, planes]) - 6.0 * mu[slot, planes])
        product = jnp.zeros((TILE, lanes), jnp.float32)
        square = jnp.zeros((TILE, lanes), jnp.float32)
        for p in range(planes):
            force = force_plane(mu.at[slot], p)
            moved_ref[i, p] = field(p) + DT * force
            at = slice(rows * p, rows * p + core)
            diff = phi_ref[after, at] - phi_ref[before, at]
            product = product + fold(force[:core] * diff)
            square = square + fold(diff * diff)
        acc[0, i] = product
        acc[1, i] = square

    slots = mu.shape[0]

    def body(t, carry):
        for slot in range(slots):
            prepare(jnp.minimum(slots * t + slot + 1, images - 1), (slot + 1) % slots)
            step(slots * t + slot, slot)
        return carry

    prepare(0, 0)
    lax.fori_loop(0, images // slots, body, 0)
    write_sums(acc, sums_ref)


def first_step(phi, tilt, devices):
    images = phi.shape[0]
    parts, rows, lanes = tilt.shape
    return pl.pallas_call(
        first_kernel,
        out_shape=[
            jax.ShapeDtypeStruct((images, parts, rows, lanes), jnp.float32),
            jax.ShapeDtypeStruct((images, rows, lanes), jnp.float32),
            jax.ShapeDtypeStruct((devices, 1, LANES), jnp.float32),
        ],
        in_specs=[vmem] * 2,
        out_specs=[vmem] * 3,
        scratch_shapes=[
            pltpu.VMEM((SLOTS, parts, rows, lanes), jnp.float32),
            pltpu.VMEM((2, images, TILE, lanes), jnp.float32),
            pltpu.VMEM((3 * LANES, 2 * LANES), jnp.bfloat16),
            pltpu.VMEM((SLOTS, (parts - 1) * rows, 2 * LANES), jnp.float32),
            pltpu.VMEM((SLOTS, rows, lanes), jnp.float32),
        ],
        compiler_params=pltpu.CompilerParams(vmem_limit_bytes=20 * MIB),
        name="first_step",
    )(phi, tilt)


def second_kernel(
    given_ref, phi_ref, strip_ref, moved_ref, tilt_ref, one_ref, two_ref, coef_ref, sums_ref, mu, acc, coefs, ones, twos
):
    images, parts, rows, lanes = moved_ref.shape
    planes = parts - 1
    core = rows - TILE
    slots = ones.shape[0]
    coef_row = tangent_share(read_sums(given_ref), images)
    coef_ref[...] = coef_row
    coefs[...] = spread(coef_row, images)
    ones[...] = jnp.zeros_like(ones)
    twos[...] = jnp.zeros_like(twos)

    def update(i, slot):
        after = jnp.minimum(i + 1, images - 1)
        before = jnp.maximum(i - 1, 0)
        scale = DT * coefs[pl.ds(i, 1)]
        for p in range(planes):
            at = slice(rows * p, rows * (p + 1))
            one = moved_ref[i, p] - scale * (phi_ref[after, at] - phi_ref[before, at])
            ones[slot, p] = one
            one_ref[i, p] = one[:core]
        ones[slot, planes] = moved_ref[i, planes] - scale * (strip_ref[after] - strip_ref[before])

    update(0, 0)

    def step(i, slot):
        update(jnp.minimum(i + 1, images - 1), (slot + 1) % slots)
        after, before, earlier = (ones.at[(slot + k) % slots] for k in (1, -1, -2))
        potential(lambda p: ones[slot, p], None, tilt_ref, mu.at[slot])
        coef = coefs[pl.ds(i, 1)]
        sums = [jnp.zeros((TILE, lanes), jnp.float32)] * 6
        for p in range(planes):
            force = force_plane(mu.at[slot], p)
            parts_of = [None] * 6
            for start in range(0, core, TILE):
                at = slice(start, start + TILE)
                x = ones[slot, p, at]
                diff = after[p, at] - before[p, at]
                diff_before = x - earlier[p, at]
                two = x + DT * (force[at] - coef * diff)
                twos[slot, p, at] = two
                two_ref[i, p, at] = two
                gap = two - twos[(slot - 1) % slots, p, at]
                terms = (force[at] * diff, diff * diff, gap * gap, gap * diff, gap * diff_before, diff * diff_before)
                parts_of = [term if part is None else part + term for part, term in zip(parts_of, terms, strict=True)]
            sums = [total + part for total, part in zip(sums, parts_of, strict=True)]
        for q in range(6):
            acc[q, i] = sums[q]

    def body(t, carry):
        for slot in range(slots):
            step(slots * t + slot, slot)
        return carry

    lax.fori_loop(0, images // slots, body, 0)
    write_sums(acc, sums_ref)


def second_step(given, phi, strips, moved, tilt):
    images, parts, rows, lanes = moved.shape
    core = (images, parts - 1, rows - TILE, lanes)
    return pl.pallas_call(
        second_kernel,
        out_shape=[
            jax.ShapeDtypeStruct(core, jnp.float32),
            jax.ShapeDtypeStruct(core, jnp.float32),
            jax.ShapeDtypeStruct((1, LANES), jnp.float32),
            jax.ShapeDtypeStruct(given.shape, jnp.float32),
        ],
        in_specs=[vmem] * 5,
        out_specs=[vmem] * 4,
        scratch_shapes=[
            pltpu.VMEM((SLOTS, parts, rows, lanes), jnp.float32),
            pltpu.VMEM((6, images, TILE, lanes), jnp.float32),
            pltpu.VMEM((images, lanes), jnp.float32),
            pltpu.VMEM((SLOTS, parts, rows, lanes), jnp.float32),
            pltpu.VMEM((SLOTS, parts - 1, rows - TILE, lanes), jnp.float32),
        ],
        compiler_params=pltpu.CompilerParams(vmem_limit_bytes=30 * MIB),
        name="second_step",
    )(given, phi, strips, moved, tilt)


def spacing(row, coef, images):
    def quantity(q):
        return pltpu.roll(row, (LANES - images * q) % LANES, 1)

    lane = lane_of(row.shape)
    change = jnp.where((lane > 0) & (lane < images - 1), tangent_share(row, images) - coef, 0.0)
    squares, gaps, gap_diff, gap_before, diff_before = (quantity(q) for q in range(1, 6))
    change_before = pltpu.roll(change, 1, 1)
    squares_before = pltpu.roll(squares, 1, 1)
    cross = change * gap_diff - change_before * gap_before
    tangent = change * change * squares + change_before * change_before * squares_before
    tangent = tangent - 2.0 * change * change_before * diff_before
    length = jnp.maximum(gaps - 2.0 * DT * cross + DT * DT * tangent, 0.0)
    dist = jnp.where((lane > 0) & (lane < images), jnp.sqrt(length + EPS), 0.0)

    shape = (images, LANES)
    slot = lane_of(shape)
    image = row_of(shape)
    arc = jnp.sum(jnp.where(image <= slot, spread(dist, images), 0.0), axis=0, keepdims=True)
    total = jnp.sum(dist, axis=1, keepdims=True)
    target = image.astype(jnp.float32) * (total / (images - 1))
    inside = (slot >= 1) & (slot <= images - 2) & (arc <= target)
    lower = jnp.sum(jnp.where(inside, 1.0, 0.0), axis=1, keepdims=True)
    where = slot.astype(jnp.float32)
    start = jnp.sum(jnp.where(where == lower, arc, 0.0), axis=1, keepdims=True)
    step = jnp.sum(jnp.where(where == lower + 1.0, dist, 0.0), axis=1, keepdims=True)
    return change, lower, (target - start) / step


def mix_kernel(given_ref, coef_ref, one_ref, two_ref, out_ref, final, changes, shares):
    images, planes, core, lanes = two_ref.shape
    change, lower, share = spacing(read_sums(given_ref), coef_ref[...], images)
    changes[...] = spread(change, images)
    shares[...] = share
    image = row_of(lower.shape)
    lowers = [jnp.sum(jnp.where(image == j, lower, 0.0)).astype(jnp.int32) for j in range(images)]

    def finish(i, carry):
        after = jnp.minimum(i + 1, images - 1)
        before = jnp.maximum(i - 1, 0)
        scale = DT * changes[pl.ds(i, 1)]
        for p in range(planes):
            final[i, p] = two_ref[i, p] - scale * (one_ref[after, p, :core] - one_ref[before, p, :core])
        return carry

    lax.fori_loop(0, images, finish, 0)
    for j in range(images):
        portion = shares[j : j + 1]
        for p in range(planes):
            out_ref[j, p] = (1.0 - portion) * final[lowers[j], p] + portion * final[lowers[j] + 1, p]


def mix(given, coef, one, two):
    images, planes, core, lanes = two.shape
    return pl.pallas_call(
        mix_kernel,
        out_shape=jax.ShapeDtypeStruct(two.shape, jnp.float32),
        in_specs=[vmem] * 4,
        out_specs=vmem,
        scratch_shapes=[
            pltpu.VMEM(two.shape, jnp.float32),
            pltpu.VMEM((images, lanes), jnp.float32),
            pltpu.VMEM((images, lanes), jnp.float32),
        ],
        compiler_params=pltpu.CompilerParams(vmem_limit_bytes=20 * MIB),
        name="mix",
    )(given, coef, one, two)


def place_kernel(blocks_ref, out_ref, held, sem):
    count, planes, half, lanes = blocks_ref.shape
    copies = []
    for p in range(planes):
        for k in range(count):
            r, c = divmod(k, count // 2)
            held[p, r * half : (r + 1) * half, c * lanes : (c + 1) * lanes] = blocks_ref[k, p]
        copies.append(pltpu.make_async_copy(held.at[p], out_ref.at[0, p], sem.at[p]))
        copies[p].start()
    for copy in copies:
        copy.wait()


def put_in_place(blocks):
    count, planes, half, lanes = blocks.shape
    plane = (2 * half, count // 2 * lanes)
    return pl.pallas_call(
        place_kernel,
        out_shape=jax.ShapeDtypeStruct((1, planes, *plane), jnp.float32),
        in_specs=[vmem],
        out_specs=anywhere,
        scratch_shapes=[pltpu.VMEM((planes, *plane), jnp.float32), pltpu.SemaphoreType.DMA((planes,))],
        compiler_params=pltpu.CompilerParams(vmem_limit_bytes=12 * MIB),
        name="put_in_place",
    )(blocks)


def exchange(block, axes):
    return lax.all_to_all(block, axes, split_axis=0, concat_axis=0, tiled=True)


def per_device(axes, path, tilt):
    devices = lax.axis_size(axes)
    place = lax.axis_index("img").astype(jnp.int32)[None]
    own = pltpu.with_memory_space_constraint(path[0], pltpu.HBM)
    tilt = pltpu.with_memory_space_constraint(tilt, pltpu.HBM)
    first, last, side = rim_rows(place, own, tilt)
    images = lax.axis_size("img")
    count = lax.axis_size("space")
    ahead = [(i, (i + 1) % count) for i in range(count)]
    back = [(target, source) for source, target in ahead]
    above = lax.ppermute(last, "space", ahead)
    below = lax.ppermute(first, "space", back)
    sideways = [(b * count + i, b * count + j) for b in range(images) for i, j in (ahead if 2 * b < images else back)]
    side = lax.ppermute(side, ("img", "space"), sideways)
    packed, tilt_block, tilt_rim = pack(place, own, tilt)
    packed, tilt_block = rims(place, above, below, side, tilt_rim, tilt_block, packed)
    packed, tilt_block = lax.optimization_barrier((packed, tilt_block))
    phi = exchange(packed, "img")
    moved, strips, sums = first_step(phi, tilt_block, devices)
    one, two, coef, sums = second_step(exchange(sums, axes), phi, strips, moved, tilt_block)
    mixed = mix(exchange(sums, axes), coef, one, two)
    return put_in_place(exchange(mixed, "img"))


def solution(mesh):
    return jax.shard_map(
        functools.partial(per_device, tuple(mesh.axis_names)),
        mesh=mesh,
        in_specs=(P("img", None, "space", None), P(None, "space", None)),
        out_specs=P("img", None, "space", None),
        check_vma=False,
    )
```

```python
import functools

import jax
import jax.numpy as jnp
from jax import lax
from jax.experimental import pallas as pl
from jax.experimental.pallas import tpu as pltpu
from jax.sharding import PartitionSpec as P

DT = 0.006
EPS = 1e-06
RIM = 4
TILE = 8
LANES = 128
GROUP = 16
MIB = 1024 * 1024
SLOTS = 4

vmem = pl.BlockSpec(memory_space=pltpu.VMEM)
smem = pl.BlockSpec(memory_space=pltpu.SMEM)
anywhere = pl.BlockSpec(memory_space=pl.ANY)


def lane_of(shape):
    return lax.broadcasted_iota(jnp.int32, shape, len(shape) - 1)


def row_of(shape):
    return lax.broadcasted_iota(jnp.int32, shape, len(shape) - 2)


def edges(tile, p, total):
    place = lane_of(tile.shape) - GROUP * p
    moved = pltpu.roll(tile, GROUP * p + RIM, 1)
    return jnp.where((place >= 0) & (place < 2 * RIM), moved, total)


def strip_of(before, own, after):
    lane = lane_of(own.shape)
    k = lane % GROUP
    left = jnp.where(k < RIM, before, own)
    right = jnp.where(k < RIM, own, after)
    both = jnp.where(k < 2 * RIM, left, pltpu.roll(right, 2 * RIM, 1))
    group = lane - k
    odd = jnp.where(k < 13, group + 8 + (k + 3) // 2, (group + GROUP) % LANES + 8 + (k - 13) // 2)
    source = jnp.where(k % 2 == 0, group + k // 2, odd)
    return jnp.take_along_axis(both, source, axis=1, mode="promise_in_bounds")


def own_plane(shape):
    lane = lane_of(shape)
    k = lane % GROUP
    group = lane // GROUP
    even = (k % 2 == 0) & (k >= 2 * RIM)
    here = even | (k == 1) | (k == 3)
    there = (k == 13) | (k == 15)
    return jnp.where(here, group, jnp.where(there, (group + 1) % (LANES // GROUP), -1))


def outer(before, after):
    lane = lane_of(before.shape)
    k = lane % GROUP
    both = jnp.where(k < RIM, before, after)
    source = lane - k + jnp.where(k % 2 == 0, k // 2, (k + 3) // 2) % (2 * RIM)
    return jnp.take_along_axis(both, source, axis=1, mode="promise_in_bounds")


def beside(first, second):
    return jnp.where(own_plane(first.shape) < 0, first, pltpu.roll(second, 2 * RIM, 1))


def pack_kernel(place_ref, path_ref, tilt_ref, out_ref, tilt_out, rim_out, held, near_tilt, edge, load_sem, tilt_sem):
    planes, rows, cols = path_ref.shape
    half = rows // 2
    ring = half + TILE
    near = (ring // TILE + 1) // 2 * TILE
    blocks = cols // LANES
    place = place_ref[0]
    loads = [pltpu.make_async_copy(path_ref.at[p], held.at[p], load_sem.at[p]) for p in range(planes)]
    rest = []
    start = pl.multiple_of((place // blocks) * half, half)
    next_to = pl.multiple_of(half - TILE * (place // blocks), TILE)
    for at, shift in enumerate((blocks - 1, 0, 1)):
        cut = pl.ds(pl.multiple_of(((place + shift) % blocks) * LANES, LANES), LANES)
        core = near_tilt.at[at, :, pl.ds(0, half)]
        rim = near_tilt.at[at, :, pl.ds(half, TILE)]
        rest.append(pltpu.make_async_copy(tilt_ref.at[:, pl.ds(start, half), cut], core, tilt_sem.at[2 * at]))
        rest.append(pltpu.make_async_copy(tilt_ref.at[:, pl.ds(next_to, TILE), cut], rim, tilt_sem.at[2 * at + 1]))
    for copy in loads + rest:
        copy.start()
    for p in range(planes):
        loads[p].wait()
        for c in range(blocks):
            cut = slice(c * LANES, (c + 1) * LANES)
            tile = held[p, :, cut]
            edge[c] = edges(tile, p, jnp.zeros_like(tile) if p == 0 else edge[c])
            for r in range(2):
                out_ref[r * blocks + c, ring * p : ring * p + half] = tile[r * half : (r + 1) * half]
                own = half - TILE * r
                out_ref[r * blocks + c, ring * p + half : ring * (p + 1)] = tile[own : own + TILE]
    for c in range(blocks):
        columns = outer(edge[(c - 1) % blocks], edge[(c + 1) % blocks])
        for r in range(2):
            part = columns[r * half : (r + 1) * half]
            at = ring * planes
            far = half - near
            out_ref[r * blocks + c, at : at + far] = beside(part[:far], part[near:])
            out_ref[r * blocks + c, at + far : at + near] = part[far:near]
    for copy in rest:
        copy.wait()
    sums = []
    for at in range(3):
        rim_out[at] = near_tilt[at, :, half:]
        total = jnp.zeros((half, LANES), jnp.float32)
        for p in range(planes):
            total = edges(near_tilt[at, p, :half], p, total)
        sums.append(total)
    tilt_out[:planes] = near_tilt[1]
    tilt_out[planes, :half] = strip_of(*sums)


def pack(place, path, tilt):
    planes, rows, cols = path.shape
    count, half = 2 * cols // LANES, rows // 2
    ring = half + TILE
    near = (ring // TILE + 1) // 2 * TILE
    return pl.pallas_call(
        pack_kernel,
        out_shape=[
            pltpu.VMEM((count, ring * planes + near, LANES), jnp.float32),
            pltpu.VMEM((planes + 1, ring, LANES), jnp.float32),
            pltpu.VMEM((3, planes, TILE, LANES), jnp.float32),
        ],
        in_specs=[smem] + [anywhere] * 2,
        out_specs=[vmem] * 3,
        scratch_shapes=[
            pltpu.VMEM((planes, rows, cols), jnp.float32),
            pltpu.VMEM((3, planes, ring, LANES), jnp.float32),
            pltpu.VMEM((count // 2, rows, LANES), jnp.float32),
            pltpu.SemaphoreType.DMA((planes,)),
            pltpu.SemaphoreType.DMA((6,)),
        ],
        compiler_params=pltpu.CompilerParams(vmem_limit_bytes=14 * MIB),
        cost_estimate=pl.CostEstimate(flops=10_000_000, bytes_accessed=16 * MIB, transcendentals=0),
        name="pack",
    )(place, path, tilt)


def rim_kernel(place_ref, path_ref, tilt_ref, first_ref, last_ref, side_ref, held, near, sem, near_sem):
    planes, rows, cols = path_ref.shape
    blocks = cols // LANES
    place = place_ref[0]
    upper = place < blocks
    start = pl.multiple_of((1 - place // blocks) * (rows - TILE), TILE)
    copies = []
    for at, row in enumerate((0, rows - TILE)):
        copies.append(pltpu.make_async_copy(path_ref.at[:, pl.ds(row, TILE)], held.at[at], sem.at[at]))
    for at, shift in enumerate((blocks - 1, 0, 1)):
        cut = pl.ds(pl.multiple_of(((place + shift) % blocks) * LANES, LANES), LANES)
        copies.append(pltpu.make_async_copy(tilt_ref.at[:, pl.ds(start, TILE), cut], near.at[at], near_sem.at[at]))
    for copy in copies:
        copy.start()
    for copy in copies:
        copy.wait()
    under = row_of((TILE, cols // 2)) < RIM
    for p in range(planes):
        left, right = slice(0, cols // 2), slice(cols // 2, cols)
        first_ref[p] = jnp.where(under, held[0, p, :, left], pltpu.roll(held[0, p, :, right], RIM, 0))
        last_ref[p] = jnp.where(under, pltpu.roll(held[1, p, :, left], RIM, 0), held[1, p, :, right])
        tiles = [jnp.where(upper, pltpu.roll(near[at, p], RIM, 0), near[at, p]) for at in range(3)]
        side_ref[p, :, :LANES] = jnp.where(under[:, :LANES], tiles[0], pltpu.roll(tiles[1], RIM, 0))
        side_ref[p, :, LANES:] = tiles[2]


def rim_rows(place, path, tilt):
    planes, rows, cols = path.shape
    half = jax.ShapeDtypeStruct((planes, TILE, cols // 2), jnp.float32)
    return pl.pallas_call(
        rim_kernel,
        out_shape=[half, half, jax.ShapeDtypeStruct((planes, TILE, 2 * LANES), jnp.float32)],
        in_specs=[smem] + [anywhere] * 2,
        out_specs=[vmem] * 3,
        scratch_shapes=[
            pltpu.VMEM((2, planes, TILE, cols), jnp.float32),
            pltpu.VMEM((3, planes, TILE, LANES), jnp.float32),
            pltpu.SemaphoreType.DMA((2,)),
            pltpu.SemaphoreType.DMA((3,)),
        ],
        compiler_params=pltpu.CompilerParams(vmem_limit_bytes=4 * MIB),
        name="rim_rows",
    )(place, path, tilt)


def rims_kernel(
    place_ref, above_ref, below_ref, side_ref, tilt_rim, tilt_ref, packed_ref, out_ref, tilt_out, edge
):
    planes, _, width = above_ref.shape
    count = out_ref.shape[0]
    ring = tilt_out.shape[1]
    half = ring - TILE
    near = out_ref.shape[1] - ring * planes
    blocks = count // 2
    upper = place_ref[0] < blocks
    under = row_of((TILE, LANES)) < RIM
    for r in range(2):
        for c in range(blocks):
            k = r * blocks + c
            turned = c * LANES // width
            cut = slice(c * LANES - turned * width, (c + 1) * LANES - turned * width)
            total = jnp.zeros((TILE, LANES), jnp.float32)
            for p in range(planes):
                at = slice(ring * p + half, ring * (p + 1))
                own = packed_ref[k, at]
                other = above_ref[p, :, cut] if r == 0 else below_ref[p, :, cut]
                if turned != 1 - r:
                    other = pltpu.roll(other, RIM, 0)
                tile = jnp.where(under, own, other) if r == 0 else jnp.where(under, other, own)
                out_ref[k, at] = tile
                total = edges(tile, p, total)
            edge[c] = total
        for c in range(blocks):
            columns = outer(edge[(c - 1) % blocks], edge[(c + 1) % blocks])
            at = ring * planes + half - near
            place_at = slice(at, at + TILE)
            out_ref[r * blocks + c, place_at] = beside(packed_ref[r * blocks + c, place_at], columns)
    sums = []
    for at in range(3):
        total = jnp.zeros((TILE, LANES), jnp.float32)
        for p in range(planes):
            own = tilt_rim[at, p]
            other = side_ref[p, :, LANES:] if at == 2 else side_ref[p, :, :LANES]
            turned = pltpu.roll(other, RIM, 0)
            if at == 1:
                other, turned = turned, other
            rim = jnp.where(upper, jnp.where(under, own, turned), jnp.where(under, other, own))
            if at == 1:
                tilt_out[p, half:] = rim
            total = edges(rim, p, total)
        sums.append(total)
    tilt_out[planes, half:] = strip_of(*sums)


def rims(place, above, below, side, tilt_rim, tilt, packed):
    return pl.pallas_call(
        rims_kernel,
        out_shape=[pltpu.VMEM(packed.shape, jnp.float32), pltpu.VMEM(tilt.shape, jnp.float32)],
        in_specs=[smem] + [vmem] * 6,
        out_specs=[vmem] * 2,
        input_output_aliases={6: 0, 5: 1},
        scratch_shapes=[pltpu.VMEM((packed.shape[0] // 2, TILE, LANES), jnp.float32)],
        compiler_params=pltpu.CompilerParams(vmem_limit_bytes=12 * MIB),
        cost_estimate=pl.CostEstimate(flops=1_000_000, bytes_accessed=4 * MIB, transcendentals=0),
        name="rims",
    )(place, above, below, side, tilt_rim, tilt, packed)


def rows_sum(x):
    return pltpu.roll(x, 1, 0) + pltpu.roll(x, x.shape[0] - 1, 0)


def neighbours_strip(s):
    total = pltpu.roll(s, GROUP, 1) + pltpu.roll(s, LANES - GROUP, 1)
    total = total + pltpu.roll(s, 2, 1) + pltpu.roll(s, LANES - 2, 1)
    return total + rows_sum(s)


def split(x):
    high = x.astype(jnp.bfloat16)
    rest = x - high.astype(jnp.float32)
    middle = rest.astype(jnp.bfloat16)
    low = (rest - middle.astype(jnp.float32)).astype(jnp.bfloat16)
    return jnp.concatenate([high, middle, low], axis=1)


def write_band(band):
    shape = (band.shape[0], LANES)
    row = row_of(shape) % LANES
    lane = lane_of(shape)
    apart = row - lane
    band[:, :LANES] = jnp.where((apart == 1) | (apart == -1), 1.0, 0.0).astype(jnp.bfloat16)
    k = lane % GROUP
    right = jnp.where(k > 2 * RIM, k - 13, k + 3) // 2 + LANES - RIM
    column = jnp.where(k % 2 == 0, k // 2 - RIM, right)
    band[:, LANES:] = jnp.where((row == column) & (own_plane(shape) >= 0), 1.0, 0.0).astype(jnp.bfloat16)


def neighbours_given(x, below, above, strip, p, within):
    lane = lane_of(x.shape)
    rim = pltpu.roll(strip, (LANES - GROUP * p - 6) % LANES, 1)
    rim = jnp.where((lane == 0) | (lane == LANES - 1), rim, 0.0)
    return (below + above) + rows_sum(x) + (within + rim)


def neighbours_plane(x, below, above, strip, p):
    lane = lane_of(x.shape)
    beside = pltpu.roll(strip, (LANES - GROUP * p - 6) % LANES, 1)
    left = jnp.where(lane == 0, beside, pltpu.roll(x, 1, 1))
    right = jnp.where(lane == LANES - 1, beside, pltpu.roll(x, LANES - 1, 1))
    return (below + above) + rows_sum(x) + (left + right)


def potential(field, sides, tilt_ref, mu):
    planes = mu.shape[0] - 1
    strip = field(planes)
    mu[planes] = strip * (strip * strip + 5.0) - (neighbours_strip(strip) + tilt_ref[planes])
    for p in range(planes):
        x = field(p)
        below, above = field((p - 1) % planes), field((p + 1) % planes)
        if sides is None:
            around = neighbours_plane(x, below, above, strip, p)
        else:
            around = neighbours_given(x, below, above, strip, p, sides(p))
        mu[p] = x * (x * x + 5.0) - (around + tilt_ref[p])


def force_plane(mu, p):
    planes = mu.shape[0] - 1
    return neighbours_plane(mu[p], mu[(p - 1) % planes], mu[(p + 1) % planes], mu[planes], p) - 6.0 * mu[p]


def fold(x):
    total = x[:TILE]
    for at in range(TILE, x.shape[0], TILE):
        total = total + x[at : at + TILE]
    return total


def write_sums(acc, out_ref):
    kinds, images = acc.shape[:2]
    row = jnp.zeros((1, LANES), jnp.float32)
    lane = lane_of((images, LANES))
    image = row_of((images, LANES))
    for q in range(kinds):
        part = jnp.sum(acc[q], axis=1)
        part = jnp.sum(part, axis=1, keepdims=True)
        row = row + jnp.sum(jnp.where(lane == images * q + image, part, 0.0), axis=0, keepdims=True)
    out_ref[...] = jnp.broadcast_to(row[None], out_ref.shape)


def read_sums(sums_ref):
    parts = [sums_ref[k] for k in range(TILE)]
    for k in range(TILE, sums_ref.shape[0]):
        parts[k % TILE] = parts[k % TILE] + sums_ref[k]
    while len(parts) > 1:
        parts = [a + b for a, b in zip(parts[::2], parts[1::2], strict=True)]
    return parts[0]


def spread(row, images):
    shape = (images, LANES)
    picked = jnp.where(lane_of(shape) == row_of(shape), row, 0.0)
    return jnp.broadcast_to(jnp.sum(picked, axis=1, keepdims=True), shape)


def tangent_share(row, images):
    lane = lane_of(row.shape)
    coef = row / (pltpu.roll(row, LANES - images, 1) + EPS)
    return jnp.where((lane > 0) & (lane < images - 1), coef, 0.0)


def first_kernel(phi_ref, tilt_ref, moved_ref, strip_ref, sums_ref, mu, acc, band, sides, strips):
    images, parts, rows, lanes = moved_ref.shape
    planes = parts - 1
    core = rows - TILE
    near = phi_ref.shape[1] - rows * planes
    write_band(band)
    owner = own_plane((rows, lanes))

    def plane(i, p):
        return phi_ref[i, rows * p : rows * (p + 1)]

    def prepare(i, slot):
        sides[slot] = jnp.dot(split(phi_ref[i, : rows * planes]), band[...], preferred_element_type=jnp.float32)
        columns = phi_ref[i, rows * planes :]
        far = pltpu.roll(columns[: rows - near], lanes - 2 * RIM, 1)
        strip = jnp.concatenate([columns, far], axis=0)
        for p in range(planes):
            strip = jnp.where(owner == p, sides[slot, rows * p : rows * (p + 1), lanes:], strip)
        strips[slot] = strip
        strip_ref[i] = strip

    def step(i, slot):
        after = jnp.minimum(i + 1, images - 1)
        before = jnp.maximum(i - 1, 0)

        def field(p):
            return strips[slot] if p == planes else plane(i, p)

        potential(field, lambda p: sides[slot, rows * p : rows * (p + 1), :lanes], tilt_ref, mu.at[slot])
        moved_ref[i, planes] = field(planes) + DT * (neighbours_strip(mu[slot, planes]) - 6.0 * mu[slot, planes])
        product = jnp.zeros((TILE, lanes), jnp.float32)
        square = jnp.zeros((TILE, lanes), jnp.float32)
        for p in range(planes):
            force = force_plane(mu.at[slot], p)
            moved_ref[i, p] = field(p) + DT * force
            at = slice(rows * p, rows * p + core)
            diff = phi_ref[after, at] - phi_ref[before, at]
            product = product + fold(force[:core] * diff)
            square = square + fold(diff * diff)
        acc[0, i] = product
        acc[1, i] = square

    slots = mu.shape[0]

    def body(t, carry):
        for slot in range(slots):
            prepare(jnp.minimum(slots * t + slot + 1, images - 1), (slot + 1) % slots)
            step(slots * t + slot, slot)
        return carry

    prepare(0, 0)
    lax.fori_loop(0, images // slots, body, 0)
    write_sums(acc, sums_ref)


def first_step(phi, tilt, devices):
    images = phi.shape[0]
    parts, rows, lanes = tilt.shape
    return pl.pallas_call(
        first_kernel,
        out_shape=[
            jax.ShapeDtypeStruct((images, parts, rows, lanes), jnp.float32),
            jax.ShapeDtypeStruct((images, rows, lanes), jnp.float32),
            jax.ShapeDtypeStruct((devices, 1, LANES), jnp.float32),
        ],
        in_specs=[vmem] * 2,
        out_specs=[vmem] * 3,
        scratch_shapes=[
            pltpu.VMEM((SLOTS, parts, rows, lanes), jnp.float32),
            pltpu.VMEM((2, images, TILE, lanes), jnp.float32),
            pltpu.VMEM((3 * LANES, 2 * LANES), jnp.bfloat16),
            pltpu.VMEM((SLOTS, (parts - 1) * rows, 2 * LANES), jnp.float32),
            pltpu.VMEM((SLOTS, rows, lanes), jnp.float32),
        ],
        compiler_params=pltpu.CompilerParams(vmem_limit_bytes=20 * MIB),
        name="first_step",
    )(phi, tilt)


def second_kernel(
    given_ref, phi_ref, strip_ref, moved_ref, tilt_ref, one_ref, two_ref, coef_ref, sums_ref, mu, acc, coefs, ones, twos
):
    images, parts, rows, lanes = moved_ref.shape
    planes = parts - 1
    core = rows - TILE
    slots = ones.shape[0]
    coef_row = tangent_share(read_sums(given_ref), images)
    coef_ref[...] = coef_row
    coefs[...] = spread(coef_row, images)
    ones[...] = jnp.zeros_like(ones)
    twos[...] = jnp.zeros_like(twos)

    def update(i, slot):
        after = jnp.minimum(i + 1, images - 1)
        before = jnp.maximum(i - 1, 0)
        scale = DT * coefs[pl.ds(i, 1)]
        for p in range(planes):
            at = slice(rows * p, rows * (p + 1))
            one = moved_ref[i, p] - scale * (phi_ref[after, at] - phi_ref[before, at])
            ones[slot, p] = one
            one_ref[i, p] = one[:core]
        ones[slot, planes] = moved_ref[i, planes] - scale * (strip_ref[after] - strip_ref[before])

    update(0, 0)

    def step(i, slot):
        update(jnp.minimum(i + 1, images - 1), (slot + 1) % slots)
        after, before, earlier = (ones.at[(slot + k) % slots] for k in (1, -1, -2))
        potential(lambda p: ones[slot, p], None, tilt_ref, mu.at[slot])
        coef = coefs[pl.ds(i, 1)]
        sums = [jnp.zeros((TILE, lanes), jnp.float32)] * 6
        for p in range(planes):
            force = force_plane(mu.at[slot], p)
            parts_of = [None] * 6
            for start in range(0, core, TILE):
                at = slice(start, start + TILE)
                x = ones[slot, p, at]
                diff = after[p, at] - before[p, at]
                diff_before = x - earlier[p, at]
                two = x + DT * (force[at] - coef * diff)
                twos[slot, p, at] = two
                two_ref[i, p, at] = two
                gap = two - twos[(slot - 1) % slots, p, at]
                terms = (force[at] * diff, diff * diff, gap * gap, gap * diff, gap * diff_before, diff * diff_before)
                parts_of = [term if part is None else part + term for part, term in zip(parts_of, terms, strict=True)]
            sums = [total + part for total, part in zip(sums, parts_of, strict=True)]
        for q in range(6):
            acc[q, i] = sums[q]

    def body(t, carry):
        for slot in range(slots):
            step(slots * t + slot, slot)
        return carry

    lax.fori_loop(0, images // slots, body, 0)
    write_sums(acc, sums_ref)


def second_step(given, phi, strips, moved, tilt):
    images, parts, rows, lanes = moved.shape
    core = (images, parts - 1, rows - TILE, lanes)
    return pl.pallas_call(
        second_kernel,
        out_shape=[
            jax.ShapeDtypeStruct(core, jnp.float32),
            jax.ShapeDtypeStruct(core, jnp.float32),
            jax.ShapeDtypeStruct((1, LANES), jnp.float32),
            jax.ShapeDtypeStruct(given.shape, jnp.float32),
        ],
        in_specs=[vmem] * 5,
        out_specs=[vmem] * 4,
        scratch_shapes=[
            pltpu.VMEM((SLOTS, parts, rows, lanes), jnp.float32),
            pltpu.VMEM((6, images, TILE, lanes), jnp.float32),
            pltpu.VMEM((images, lanes), jnp.float32),
            pltpu.VMEM((SLOTS, parts, rows, lanes), jnp.float32),
            pltpu.VMEM((SLOTS, parts - 1, rows - TILE, lanes), jnp.float32),
        ],
        compiler_params=pltpu.CompilerParams(vmem_limit_bytes=30 * MIB),
        name="second_step",
    )(given, phi, strips, moved, tilt)


def spacing(row, coef, images):
    def quantity(q):
        return pltpu.roll(row, (LANES - images * q) % LANES, 1)

    lane = lane_of(row.shape)
    change = jnp.where((lane > 0) & (lane < images - 1), tangent_share(row, images) - coef, 0.0)
    squares, gaps, gap_diff, gap_before, diff_before = (quantity(q) for q in range(1, 6))
    change_before = pltpu.roll(change, 1, 1)
    squares_before = pltpu.roll(squares, 1, 1)
    cross = change * gap_diff - change_before * gap_before
    tangent = change * change * squares + change_before * change_before * squares_before
    tangent = tangent - 2.0 * change * change_before * diff_before
    length = jnp.maximum(gaps - 2.0 * DT * cross + DT * DT * tangent, 0.0)
    dist = jnp.where((lane > 0) & (lane < images), jnp.sqrt(length + EPS), 0.0)

    shape = (images, LANES)
    slot = lane_of(shape)
    image = row_of(shape)
    arc = jnp.sum(jnp.where(image <= slot, spread(dist, images), 0.0), axis=0, keepdims=True)
    total = jnp.sum(dist, axis=1, keepdims=True)
    target = image.astype(jnp.float32) * (total / (images - 1))
    inside = (slot >= 1) & (slot <= images - 2) & (arc <= target)
    lower = jnp.sum(jnp.where(inside, 1.0, 0.0), axis=1, keepdims=True)
    where = slot.astype(jnp.float32)
    start = jnp.sum(jnp.where(where == lower, arc, 0.0), axis=1, keepdims=True)
    step = jnp.sum(jnp.where(where == lower + 1.0, dist, 0.0), axis=1, keepdims=True)
    return change, lower, (target - start) / step


def mix_kernel(given_ref, coef_ref, one_ref, two_ref, out_ref, final, changes, shares):
    images, planes, core, lanes = two_ref.shape
    change, lower, share = spacing(read_sums(given_ref), coef_ref[...], images)
    changes[...] = spread(change, images)
    shares[...] = share
    image = row_of(lower.shape)
    lowers = [jnp.sum(jnp.where(image == j, lower, 0.0)).astype(jnp.int32) for j in range(images)]

    def finish(i, carry):
        after = jnp.minimum(i + 1, images - 1)
        before = jnp.maximum(i - 1, 0)
        scale = DT * changes[pl.ds(i, 1)]
        for p in range(planes):
            final[i, p] = two_ref[i, p] - scale * (one_ref[after, p, :core] - one_ref[before, p, :core])
        return carry

    lax.fori_loop(0, images, finish, 0, unroll=4)
    for j in range(images):
        portion = shares[j : j + 1]
        for p in range(planes):
            out_ref[j, p] = (1.0 - portion) * final[lowers[j], p] + portion * final[lowers[j] + 1, p]


def mix(given, coef, one, two):
    images, planes, core, lanes = two.shape
    return pl.pallas_call(
        mix_kernel,
        out_shape=jax.ShapeDtypeStruct(two.shape, jnp.float32),
        in_specs=[vmem] * 4,
        out_specs=vmem,
        scratch_shapes=[
            pltpu.VMEM(two.shape, jnp.float32),
            pltpu.VMEM((images, lanes), jnp.float32),
            pltpu.VMEM((images, lanes), jnp.float32),
        ],
        compiler_params=pltpu.CompilerParams(vmem_limit_bytes=20 * MIB),
        name="mix",
    )(given, coef, one, two)


def place_kernel(blocks_ref, out_ref, held, sem):
    count, planes, half, lanes = blocks_ref.shape
    copies = []
    for p in range(planes):
        for k in range(count):
            r, c = divmod(k, count // 2)
            held[p, r * half : (r + 1) * half, c * lanes : (c + 1) * lanes] = blocks_ref[k, p]
        copies.append(pltpu.make_async_copy(held.at[p], out_ref.at[0, p], sem.at[p]))
        copies[p].start()
    for copy in copies:
        copy.wait()


def put_in_place(blocks):
    count, planes, half, lanes = blocks.shape
    plane = (2 * half, count // 2 * lanes)
    return pl.pallas_call(
        place_kernel,
        out_shape=jax.ShapeDtypeStruct((1, planes, *plane), jnp.float32),
        in_specs=[vmem],
        out_specs=anywhere,
        scratch_shapes=[pltpu.VMEM((planes, *plane), jnp.float32), pltpu.SemaphoreType.DMA((planes,))],
        compiler_params=pltpu.CompilerParams(vmem_limit_bytes=12 * MIB),
        name="put_in_place",
    )(blocks)


def exchange(block, axes):
    return lax.all_to_all(block, axes, split_axis=0, concat_axis=0, tiled=True)


def per_device(axes, path, tilt):
    devices = lax.axis_size(axes)
    place = lax.axis_index("img").astype(jnp.int32)[None]
    own = pltpu.with_memory_space_constraint(path[0], pltpu.HBM)
    tilt = pltpu.with_memory_space_constraint(tilt, pltpu.HBM)
    first, last, side = rim_rows(place, own, tilt)
    images = lax.axis_size("img")
    count = lax.axis_size("space")
    ahead = [(i, (i + 1) % count) for i in range(count)]
    back = [(target, source) for source, target in ahead]
    above = lax.ppermute(last, "space", ahead)
    below = lax.ppermute(first, "space", back)
    sideways = [(b * count + i, b * count + j) for b in range(images) for i, j in (ahead if 2 * b < images else back)]
    side = lax.ppermute(side, ("img", "space"), sideways)
    packed, tilt_block, tilt_rim = pack(place, own, tilt)
    packed, tilt_block = rims(place, above, below, side, tilt_rim, tilt_block, packed)
    packed, tilt_block = lax.optimization_barrier((packed, tilt_block))
    phi = exchange(packed, "img")
    moved, strips, sums = first_step(phi, tilt_block, devices)
    one, two, coef, sums = second_step(exchange(sums, axes), phi, strips, moved, tilt_block)
    mixed = mix(exchange(sums, axes), coef, one, two)
    return put_in_place(exchange(mixed, "img"))


def solution(mesh):
    return jax.shard_map(
        functools.partial(per_device, tuple(mesh.axis_names)),
        mesh=mesh,
        in_specs=(P("img", None, "space", None), P(None, "space", None)),
        out_specs=P("img", None, "space", None),
        check_vma=False,
    )
```
